32 devices in a mesh: row: 4 (over y, x), col: 4 (over z), layer: 2 (over core).
Axes of the slice: x: 2, y: 2, z: 4, core: 2. Of those that a mesh axis runs over, the one named last changes fastest.
Arguments:
- tasks: bfloat16 [2048, 4096], P(('row', 'col')), may hold values from -0.25 to 0.25
- task_owner: int32 [2048, 1], P(('row', 'col')), may hold values from 0 to 15; in each aligned block of 128 rows (0 to 127, 128 to 255, ...) at most 16 rows name the same one
- task_slot: int32 [2048], P(('row', 'col')), may hold values from 0 to 63
- p_pattern: int32 [32, 32], P('row', 'col'), may hold values from 0 to 1, as said below
- c_pattern: int32 [32, 32], P('row', 'col'), may hold values from 0 to 1, as said below
- occupations: float32 [2048], P('row'), may hold values from 0.1 to 0.9
Outputs:
- purified: float32 [2048, 2048], P(('row', 'layer'), 'col')
The draws below stay inside these ranges and needn't reach their ends.
Inputs may be any that keep to these rules, and one draw needn't show every extreme that they name: `task_owner`: the 128 tasks of one index of row and col name each owner at most 16 times. `task_slot`: a block of the owner's 8 x 8 blocks, row-major. `p_pattern`: 0 or 1; every diagonal block is 1. `c_pattern`: 0 or 1; every diagonal block is 1.
All inputs are finite; a program needn't handle non-finite values.
Results may differ from the reference program's by a relative error of at most 0.025.
Values may be sent and summed in bfloat16 or wider, within the bound.
No kernel may reach another device: no remote copies, remote signals or barrier semaphores. Data moves between devices by JAX's collectives and lax.ppermute only.
A program may use at most 64 MiB of HBM per device.

```python
import math
import jax
import jax.numpy as jnp
import numpy as np
from jax import lax

BLK = 64
RB_DEV = 8
TASK_DEV = 128
NB = 32
ORDER = 2048
CB_DEV = 8
CAP = 16
TASKS = 2048
N_ROW = 4
N_COL = 4


def banded(key, near, far):
    index = jnp.arange(NB, dtype=jnp.int32)
    spread = jnp.abs(index[:, None] - index[None, :])
    spread = jnp.minimum(spread, NB - spread)
    chance = near - (near - far) * 2 * spread // max(NB, 1)
    roll = jax.random.randint(key, (NB, NB), 0, 1000, dtype=jnp.int32)
    return jnp.where((roll < chance) | (spread == 0), 1, 0).astype(jnp.int32)


def draw_p_pattern(key, part):
    return banded(jax.random.fold_in(key, 11), 900, 150)


def draw_c_pattern(key, part):
    return banded(jax.random.fold_in(key, 23), 950, 300)


def place_ends(entries, own_key, smallest, largest):
    place = [jax.random.randint(jax.random.fold_in(own_key, axis), (), 0, length) for axis, length in enumerate(entries.shape)]
    main_axis = entries.shape.index(max(entries.shape))
    next_to = place[:main_axis] + [(place[main_axis] + 1) % entries.shape[main_axis]] + place[main_axis + 1:]
    return entries.at[tuple(place)].set(smallest).at[tuple(next_to)].set(largest)


def block_levels(rng, dims, split, low, top_value):
    gain, own = 1.0, jax.random.fold_in(rng, 6)
    for position, parts in split:
        steps = jnp.exp(jax.random.uniform(jax.random.fold_in(own, position), (parts,), jnp.float32, low / len(split), top_value / len(split)))
        gain = gain * jnp.repeat(steps, dims[position] // parts).reshape([-1 if axis == position else 1 for axis in range(len(dims))])
    return gain


def assign_block(rng, own, number, rows, amount, top, reach, lean):
    sequence = jax.random.permutation(rng, amount)
    heavy_load, ordinary = shares(amount, rows * top, reach, lean, True), shares(amount, rows * top, reach, lean, False)
    places = jnp.arange(amount)

    def named(tallies, rotation):
        used = int((tallies > 0).sum())
        fixed = max(1, used // 4)
        shifted = fixed + (places - fixed + rotation * (used - fixed)) % max(1, amount - fixed)
        return jnp.zeros((amount,), jnp.int32).at[sequence[jnp.where(places < fixed, places, shifted)]].set(jnp.asarray(tallies, jnp.int32))

    tallies = jnp.where(number % 4 == 0, named(heavy_load, number // 4), named(ordinary, number - number // 4 - 1))
    mixed = jax.random.permutation(jax.random.fold_in(own, 3), amount)
    donor, receiver = mixed[0:amount // 2 * 2:2], mixed[1:amount // 2 * 2:2]
    margin = jnp.minimum(tallies[donor] - 1, reach - tallies[receiver]) // 2
    margin = jnp.where((donor == sequence[0]) | (receiver == sequence[0]) | (tallies[receiver] == 0), 0, jnp.maximum(margin, 0))
    shifted = jax.random.randint(jax.random.fold_in(own, 4), (amount // 2,), 0, 1 << 20) % (margin + 1)
    tallies = tallies.at[donor].add(-shifted).at[receiver].add(shifted)
    labels = jnp.searchsorted(jnp.cumsum(tallies), jnp.arange(rows * top), side="right").astype(jnp.int32)
    listing = labels.reshape(top, rows).T
    listing = listing[jax.random.permutation(jax.random.fold_in(own, 1), rows)]
    rotation = jax.random.randint(jax.random.fold_in(own, 2), (rows, 1), 0, top)
    return jnp.take_along_axis(listing, (jnp.arange(top)[None, :] + rotation) % top, axis=1)


def shares(count, total, bound, skew, full):
    portions = [(1 << 20) // math.isqrt(grade ** skew) + 1 for grade in range(1, count + 1)]
    largest = bound if full else min(bound, max(-(-total // count), total * portions[0] // sum(portions)))
    least = 1 if total - largest >= count - 1 else 0
    given, surplus = [largest] + [least] * (count - 1), total - largest - least * (count - 1)
    while surplus > 0:
        movable = [i for i in range(1, count) if given[i] < largest] or [i for i in range(1, count) if given[i] < bound]
        pool, remaining = sum([portions[i] for i in movable]), surplus
        for i in movable:
            more = min(bound - given[i], max(1, remaining * portions[i] // pool), surplus)
            given[i] = given[i] + more
            surplus = surplus - more
    return np.array(given)


def centred(key, extent, scale, bound, pieces=(), held_as=jnp.bfloat16):
    loudness = block_levels(key, extent, pieces, -0.22, 0.18) if pieces else 1.0
    array = jax.random.normal(key, extent, jnp.float32) * scale * loudness
    return jnp.minimum(jnp.maximum(array, -bound), bound).astype(held_as)


def setup_inputs(seed: int = 0) -> dict:
    key_list = jax.random.split(jax.random.key(seed), 7)
    tasks = centred(key_list[0], (TASKS, BLK * BLK), (0.8 * (NB / (32 * TASKS)) ** 0.5), 0.25, ((0, 16),))
    task_owner_keys = jax.random.split(jax.random.fold_in(key_list[1], 1), TASKS // TASK_DEV)
    task_owner_turns = jax.random.permutation(jax.random.fold_in(key_list[1], 3), TASKS // TASK_DEV)
    task_owner = jax.vmap(lambda own, number: assign_block(jax.random.fold_in(key_list[1], 2), own, number, TASK_DEV, N_ROW * N_COL, 1, CAP, 2))(task_owner_keys, task_owner_turns).reshape((TASKS, 1))
    task_slot = place_ends(jax.random.randint(key_list[2], (TASKS,), 0, RB_DEV * CB_DEV), jax.random.fold_in(key_list[2], 1), 0, (RB_DEV * CB_DEV) - 1).astype(jnp.int32)
    p_pattern = draw_p_pattern(jax.random.fold_in(key_list[6], 71), 0)
    c_pattern = draw_c_pattern(jax.random.fold_in(key_list[6], 71), 0)
    occupations = jnp.clip(0.1 + 0.79999997 * jax.random.uniform(key_list[5], (ORDER,), jnp.float32) ** block_levels(key_list[5], (ORDER,), ((0, 4),), -0.2, 0.2), 0.1, 0.9)
    return {"tasks": tasks, "task_owner": task_owner, "task_slot": task_slot, "p_pattern": p_pattern, "c_pattern": c_pattern, "occupations": occupations}


def expand(pattern):
    return jnp.repeat(jnp.repeat(pattern.astype(jnp.float32), BLK, axis=0), BLK, axis=1)


def reference(tasks, task_owner, task_slot, p_pattern, c_pattern, occupations):
    owner = task_owner[:, 0]
    grid_cols = NB // CB_DEV
    block_row = (owner // grid_cols) * RB_DEV + task_slot // CB_DEV
    block_col = (owner % grid_cols) * CB_DEV + task_slot % CB_DEV
    target = (block_row * NB + block_col).astype(jnp.int32)
    blocks = jnp.zeros((NB * NB, BLK * BLK), jnp.float32).at[target].add(tasks.astype(jnp.float32))
    assembled = blocks.reshape(NB, NB, BLK, BLK).transpose(0, 2, 1, 3).reshape(ORDER, ORDER)
    density = (expand(p_pattern) * assembled + jnp.diag(occupations)).astype(jnp.bfloat16)
    wide = density.astype(jnp.float32)
    square = jnp.dot(wide, wide, precision=lax.Precision.HIGHEST)
    square_low = lax.optimization_barrier(square.astype(jnp.bfloat16)).astype(jnp.float32)
    cube = jnp.dot(wide, square_low, precision=lax.Precision.HIGHEST)
    return expand(c_pattern) * (3.0 * square - 2.0 * cube)
```

```python
import functools

import jax
import jax.numpy as jnp
from jax import lax
from jax.experimental import pallas as pl
from jax.experimental.pallas import tpu as pltpu
from jax.sharding import PartitionSpec as P

BLK = 64
LANES = 128
VMEM_BYTES = 56 * 1024 * 1024


def params():
    return pltpu.CompilerParams(vmem_limit_bytes=VMEM_BYTES)


def whole_ref():
    return pl.BlockSpec(memory_space=pltpu.VMEM)


def any_ref():
    return pl.BlockSpec(memory_space=pl.ANY)


def cost(flops, bytes_accessed):
    return pl.CostEstimate(flops=flops, bytes_accessed=bytes_accessed, transcendentals=0)


def pack_kernel(owners, capacity, block_shape, tasks_ref, owner_ref, slot_ref, out_ref, held, sem):
    count, part = held.shape
    layer = lax.axis_index("layer")
    start = pl.multiple_of(layer * part, part)
    copy = pltpu.make_async_copy(tasks_ref.at[:, pl.ds(start, part)], held, sem)
    copy.start()
    block_rows, block_cols = block_shape
    slot_row = slot_ref[...]
    slot_row = lax.rem(slot_row, block_cols) * block_rows + lax.div(slot_row, block_cols)
    across = lax.broadcasted_iota(jnp.int32, (count, count), 1)
    down = lax.broadcasted_iota(jnp.int32, (count, count), 0)
    eye = across == down
    owner_row = jnp.sum(
        jnp.where(eye, owner_ref[...].astype(jnp.float32), 0.0), axis=0, keepdims=True
    ).astype(jnp.int32)
    slot_col = jnp.sum(
        jnp.where(eye, slot_row.astype(jnp.float32), 0.0), axis=1, keepdims=True
    )
    same = (lax.broadcasted_iota(jnp.int32, (owners, count), 0) == owner_row).astype(jnp.float32)
    before = (down < across).astype(jnp.bfloat16)
    ahead = jnp.dot(same.astype(jnp.bfloat16), before, preferred_element_type=jnp.float32)
    placed = jnp.sum(ahead * same, axis=0, keepdims=True).astype(jnp.int32)
    target = owner_row * capacity + placed
    places = owners * capacity
    move = (
        (lax.broadcasted_iota(jnp.int32, (places, count), 0) == target)
        .astype(jnp.float32)
        .astype(jnp.bfloat16)
    )
    slots = jnp.broadcast_to(slot_col, (count, LANES)).astype(jnp.bfloat16)
    out_ref[:, part:] = jnp.dot(move, slots, preferred_element_type=jnp.float32).astype(
        jnp.bfloat16
    )
    copy.wait()
    step = 512
    for at in range(0, part, step):
        out_ref[:, at : at + step] = jnp.dot(
            move, held[:, at : at + step], preferred_element_type=jnp.float32
        ).astype(jnp.bfloat16)


def build_kernel(block_shape, got_ref, pattern_ref, occ_ref, out_ref, tall):
    block_rows, block_cols = block_shape
    rows, cols = out_ref.shape
    part_rows = rows // block_rows
    layers = BLK // part_rows
    part = part_rows * BLK
    places = got_ref.shape[0]
    slots = got_ref[:, part : part + LANES].astype(jnp.float32)
    lane = lax.broadcasted_iota(jnp.int32, (places, LANES), 1).astype(jnp.float32)
    marks = jnp.where(slots == lane, pattern_ref[...], 0.0)
    marks = marks.T[: block_rows * block_cols].astype(jnp.bfloat16)
    low = lax.broadcasted_iota(jnp.int32, (block_rows, LANES), 1) < BLK
    step = 256
    for at in range(0, part, step):
        summed = jnp.dot(marks, got_ref[:, at : at + step], preferred_element_type=jnp.float32)
        for pair in range(step // LANES):
            lanes = slice(pair * LANES, (pair + 1) * LANES)
            row = (at // LANES + pair) * 2
            for twin in range(block_cols // 2):
                first = summed[twin * 2 * block_rows : (twin * 2 + 1) * block_rows, lanes]
                second = summed[(twin * 2 + 1) * block_rows : (twin * 2 + 2) * block_rows, lanes]
                tall[twin, pl.ds(row, block_rows, stride=part_rows), :] = jnp.where(
                    low, first, pltpu.roll(second, BLK, 1)
                )
                tall[twin, pl.ds(row + 1, block_rows, stride=part_rows), :] = jnp.where(
                    low, pltpu.roll(first, BLK, 1), second
                )
    row_start = lax.axis_index("row") * (block_rows * BLK) + lax.axis_index("layer") * part_rows
    col_start = lax.axis_index("col") * cols
    index = lax.broadcasted_iota(jnp.int32, (rows, LANES), 0)
    row_id = row_start + lax.div(index, part_rows) * BLK + lax.rem(index, part_rows)
    col_id = col_start + lax.broadcasted_iota(jnp.int32, (rows, LANES), 1)
    occ = occ_ref[...]
    for twin in range(block_cols // 2):
        diagonal = jnp.where(row_id == col_id + twin * LANES, occ, 0.0)
        out_ref[:, twin * LANES : (twin + 1) * LANES] = (tall[twin] + diagonal).astype(
            jnp.bfloat16
        )


def load_panel(panel, pieces, mates, sems, first):
    me = lax.axis_index("row")
    layer = lax.axis_index("layer")
    copies = []
    for shift, (piece, mate) in enumerate(zip(pieces, mates)):
        block = me ^ shift
        copies.append(
            pltpu.make_async_copy(piece, panel.at[block, :, layer], sems.at[first + 2 * shift])
        )
        copies.append(
            pltpu.make_async_copy(
                mate, panel.at[block, :, 1 - layer], sems.at[first + 2 * shift + 1]
            )
        )
    return copies


def product(left, panel):
    blocks = left.shape[0]
    per_block = panel.shape[0] // blocks
    cols = panel.shape[-1]

    def term(block):
        a = left[block].reshape(-1, left.shape[-1])
        b = panel[pl.ds(block * per_block, per_block)].reshape(-1, cols)
        return jnp.dot(a, b, preferred_element_type=jnp.float32)

    total = term(0)
    if blocks <= 4:
        for block in range(1, blocks):
            total = total + term(block)
        return total
    return lax.fori_loop(1, blocks, lambda block, sofar: sofar + term(block), total)


def square_kernel(n_left, n_right, *refs):
    lefts = refs[:n_left]
    pieces = refs[n_left : n_left + n_right]
    mates = refs[n_left + n_right : n_left + 2 * n_right]
    low_ref, keep_ref, give_ref, left, panel, sems = refs[n_left + 2 * n_right :]
    col = lax.axis_index("col")
    layer = lax.axis_index("layer")
    copies = [
        pltpu.make_async_copy(piece, left.at[col ^ shift], sems.at[shift])
        for shift, piece in enumerate(lefts)
    ]
    copies += load_panel(panel, pieces, mates, sems, n_left)
    for copy in copies:
        copy.start()
    for copy in copies:
        copy.wait()
    here = keep_ref.shape[1]
    out = [
        pltpu.make_async_copy(left.at[:, pl.ds(layer * here, here)], keep_ref, sems.at[0]),
        pltpu.make_async_copy(left.at[:, pl.ds((1 - layer) * here, here)], give_ref, sems.at[1]),
    ]
    for copy in out:
        copy.start()
    low_ref[...] = product(left, panel).reshape(low_ref.shape).astype(jnp.bfloat16)
    for copy in out:
        copy.wait()


def cube_kernel(n_right, *refs):
    keep_ref, got_ref, pattern_ref = refs[:3]
    pieces = refs[3 : 3 + n_right]
    mates = refs[3 + n_right : 3 + 2 * n_right]
    out_ref, left, panel, sems = refs[3 + 2 * n_right :]
    row = lax.axis_index("row")
    layer = lax.axis_index("layer")
    copies = [
        pltpu.make_async_copy(keep_ref, left.at[:, :, layer], sems.at[0]),
        pltpu.make_async_copy(got_ref, left.at[:, :, 1 - layer], sems.at[1]),
    ]
    copies += load_panel(panel, pieces, mates, sems, 2)
    for copy in copies:
        copy.start()
    rows, cols = out_ref.shape
    pattern = pattern_ref[...].astype(jnp.float32).astype(jnp.bfloat16)
    block_rows, block_cols = pattern.shape
    across = lax.broadcasted_iota(jnp.int32, (block_cols, cols), 1)
    which = lax.broadcasted_iota(jnp.int32, (block_cols, cols), 0)
    wide = (lax.div(across, BLK) == which).astype(jnp.float32).astype(jnp.bfloat16)
    down = lax.broadcasted_iota(jnp.int32, (rows, block_rows), 0) + layer * rows
    which = lax.broadcasted_iota(jnp.int32, (rows, block_rows), 1)
    tall = (lax.div(down, BLK) == which).astype(jnp.float32).astype(jnp.bfloat16)
    mask = jnp.dot(
        jnp.dot(tall, pattern, preferred_element_type=jnp.float32).astype(jnp.bfloat16),
        wide,
        preferred_element_type=jnp.float32,
    )
    for copy in copies:
        copy.wait()
    here = left.shape[1]
    square = panel[row, pl.ds(layer * here, here)].reshape(rows, cols).astype(jnp.float32)
    out_ref[...] = mask * (3.0 * square - 2.0 * product(left, panel))


def xor_pairs(axis, shift):
    return [(i, i ^ shift) for i in range(lax.axis_size(axis))]


def gather(piece, axis):
    return [piece] + [
        lax.ppermute(piece, axis, xor_pairs(axis, shift))
        for shift in range(1, lax.axis_size(axis))
    ]


def swap(piece):
    return lax.ppermute(piece, "layer", xor_pairs("layer", 1))


def on_device(tasks, task_owner, task_slot, p_pattern, c_pattern, occupations):
    n_row, n_col, layers = (lax.axis_size(axis) for axis in ("row", "col", "layer"))
    owners = n_row * n_col
    count = tasks.shape[0]
    capacity = max(2, 2 * count // owners)
    places = owners * capacity
    block_rows, block_cols = p_pattern.shape
    part_rows = BLK // layers
    part = part_rows * BLK
    rows, cols = block_rows * part_rows, block_cols * BLK
    width = part + LANES
    layer = lax.axis_index("layer")

    sent = pl.pallas_call(
        functools.partial(pack_kernel, owners, capacity, p_pattern.shape),
        out_shape=jax.ShapeDtypeStruct((places, width), jnp.bfloat16),
        in_specs=[any_ref(), whole_ref(), whole_ref()],
        out_specs=whole_ref(),
        scratch_shapes=[pltpu.VMEM((count, part), jnp.bfloat16), pltpu.SemaphoreType.DMA],
        compiler_params=params(),
        cost_estimate=cost(2 * places * count * width, 2 * (places + count) * width),
        name="pack",
    )(tasks, task_owner, task_slot.reshape(1, count))
    got = lax.all_to_all(
        sent.reshape(owners, capacity, width),
        ("row", "col"),
        split_axis=0,
        concat_axis=0,
        tiled=True,
    ).reshape(places, width)

    pattern_row = p_pattern.astype(jnp.float32).T.reshape(1, block_rows * block_cols)
    pattern_row = jnp.pad(pattern_row, ((0, 0), (0, LANES - block_rows * block_cols)))
    occ_part = lax.dynamic_index_in_dim(
        occupations.reshape(block_rows, layers, part_rows), layer, 1, keepdims=False
    ).reshape(rows, 1)
    density = pl.pallas_call(
        functools.partial(build_kernel, p_pattern.shape),
        out_shape=jax.ShapeDtypeStruct((rows, cols), jnp.bfloat16),
        in_specs=[whole_ref()] * 3,
        out_specs=whole_ref(),
        scratch_shapes=[pltpu.VMEM((cols // LANES, rows, LANES), jnp.float32)],
        compiler_params=params(),
        cost_estimate=cost(2 * places * block_rows * block_cols * part, 2 * places * width),
        name="build",
    )(got, pattern_row, occ_part)
    density = density.reshape(block_rows, part_rows, cols)

    pieces = gather(density, "row")
    mates = [swap(piece) for piece in pieces]
    lefts = gather(density, "col")
    flops = 2 * rows * cols * n_col * cols
    panel_shape = (n_row, block_rows, layers, part_rows, cols)
    here = block_rows // layers
    half = jax.ShapeDtypeStruct((n_col, here, part_rows, cols), jnp.bfloat16)
    square, keep, give = pl.pallas_call(
        functools.partial(square_kernel, n_col, n_row),
        out_shape=[jax.ShapeDtypeStruct(density.shape, jnp.bfloat16), half, half],
        in_specs=[any_ref()] * (n_col + 2 * n_row),
        out_specs=[whole_ref(), any_ref(), any_ref()],
        scratch_shapes=[
            pltpu.VMEM((n_col, block_rows, part_rows, cols), jnp.bfloat16),
            pltpu.VMEM(panel_shape, jnp.bfloat16),
            pltpu.SemaphoreType.DMA((n_col + 2 * n_row,)),
        ],
        compiler_params=params(),
        cost_estimate=cost(flops, 8 * 1024 * 1024),
        name="square",
    )(*lefts, *pieces, *mates)

    received = swap(give)
    pieces = gather(square, "row")
    mates = [swap(piece) for piece in pieces]
    return pl.pallas_call(
        functools.partial(cube_kernel, n_row),
        out_shape=jax.ShapeDtypeStruct((rows, cols), jnp.float32),
        in_specs=[any_ref()] * 2 + [whole_ref()] + [any_ref()] * (2 * n_row),
        out_specs=whole_ref(),
        scratch_shapes=[
            pltpu.VMEM((n_col, here, layers, part_rows, cols), jnp.bfloat16),
            pltpu.VMEM(panel_shape, jnp.bfloat16),
            pltpu.SemaphoreType.DMA((2 + 2 * n_row,)),
        ],
        compiler_params=params(),
        cost_estimate=cost(flops, 8 * 1024 * 1024),
        name="cube",
    )(keep, received, c_pattern, *pieces, *mates)


def solution(mesh):
    return jax.shard_map(
        on_device,
        mesh=mesh,
        in_specs=(
            P(("row", "col"), None),
            P(("row", "col"), None),
            P(("row", "col")),
            P("row", "col"),
            P("row", "col"),
            P("row"),
        ),
        out_specs=P(("row", "layer"), "col"),
        check_vma=False,
    )
```

```python
import functools

import jax
import jax.numpy as jnp
from jax import lax
from jax.experimental import pallas as pl
from jax.experimental.pallas import tpu as pltpu
from jax.sharding import PartitionSpec as P

BLK = 64
LANES = 128


def params(held):
    return pltpu.CompilerParams(vmem_limit_bytes=held + 6 * 1024 * 1024)


def whole_ref():
    return pl.BlockSpec(memory_space=pltpu.VMEM)


def any_ref():
    return pl.BlockSpec(memory_space=pl.ANY)


def cost(flops, bytes_accessed):
    return pl.CostEstimate(flops=flops, bytes_accessed=bytes_accessed, transcendentals=0)


def pack_kernel(owners, capacity, block_shape, paired, tasks_ref, owner_ref, slot_ref, *refs):
    out_refs, held, sem = refs[:-2], refs[-2], refs[-1]
    count, part = held.shape
    layer = lax.axis_index("layer")
    start = pl.multiple_of(layer * part, part)
    copy = pltpu.make_async_copy(tasks_ref.at[:, pl.ds(start, part)], held, sem)
    copy.start()
    block_rows, block_cols = block_shape
    slot_row = slot_ref[...]
    slot_row = lax.rem(slot_row, block_cols) * block_rows + lax.div(slot_row, block_cols)
    across = lax.broadcasted_iota(jnp.int32, (count, count), 1)
    down = lax.broadcasted_iota(jnp.int32, (count, count), 0)
    slot_col = jnp.sum(
        jnp.where(across == down, slot_row.astype(jnp.float32), 0.0), axis=1, keepdims=True
    )
    owner_row = owner_ref[...]
    if paired:
        owner_row = owner_row ^ (
            lax.axis_index("row") * lax.axis_size("col") + lax.axis_index("col")
        )
    same = (lax.broadcasted_iota(jnp.int32, (owners, count), 0) == owner_row).astype(jnp.float32)
    before = (down < across).astype(jnp.float32).astype(jnp.bfloat16)
    ahead = jnp.dot(same.astype(jnp.bfloat16), before, preferred_element_type=jnp.float32)
    placed = jnp.sum(ahead * same, axis=0, keepdims=True).astype(jnp.int32)
    target = owner_row * capacity + placed
    places = owners * capacity
    move = (
        (lax.broadcasted_iota(jnp.int32, (places, count), 0) == target)
        .astype(jnp.float32)
        .astype(jnp.bfloat16)
    )

    def put(at, end, blocks):
        moved = jnp.dot(move, blocks, preferred_element_type=jnp.float32).astype(jnp.bfloat16)
        each = places // len(out_refs)
        for index, out_ref in enumerate(out_refs):
            out_ref[:, at:end] = moved[index * each : (index + 1) * each]

    put(part, part + LANES, jnp.broadcast_to(slot_col, (count, LANES)).astype(jnp.bfloat16))
    copy.wait()
    step = 512
    for at in range(0, part, step):
        put(at, at + step, held[:, at : at + step])


def build_kernel(block_shape, pattern_ref, occ_ref, *refs):
    got_refs, out_ref, tall = refs[:-2], refs[-2], refs[-1]
    block_rows, block_cols = block_shape
    rows, cols = out_ref.shape
    part_rows = rows // block_rows
    part = part_rows * BLK

    def got(at, end):
        return jnp.concatenate([ref[:, at:end] for ref in got_refs], axis=0)

    slots = got(part, part + LANES).astype(jnp.float32)
    lane = lax.broadcasted_iota(jnp.int32, slots.shape, 1).astype(jnp.float32)
    marks = jnp.where(slots == lane, pattern_ref[...], 0.0)
    marks = marks.T[: block_rows * block_cols].astype(jnp.bfloat16)
    low = lax.broadcasted_iota(jnp.int32, (block_rows, LANES), 1) < BLK
    step = 256
    for at in range(0, part, step):
        summed = jnp.dot(marks, got(at, at + step), preferred_element_type=jnp.float32)
        for pair in range(step // LANES):
            lanes = slice(pair * LANES, (pair + 1) * LANES)
            row = (at // LANES + pair) * 2
            for twin in range(block_cols // 2):
                first = summed[twin * 2 * block_rows : (twin * 2 + 1) * block_rows, lanes]
                second = summed[(twin * 2 + 1) * block_rows : (twin * 2 + 2) * block_rows, lanes]
                tall[twin, pl.ds(row, block_rows, stride=part_rows), :] = jnp.where(
                    low, first, pltpu.roll(second, BLK, 1)
                )
                tall[twin, pl.ds(row + 1, block_rows, stride=part_rows), :] = jnp.where(
                    low, pltpu.roll(first, BLK, 1), second
                )
    row_start = lax.axis_index("row") * (block_rows * BLK) + lax.axis_index("layer") * part_rows
    col_start = lax.axis_index("col") * cols
    index = lax.broadcasted_iota(jnp.int32, (rows, LANES), 0)
    row_id = row_start + lax.div(index, part_rows) * BLK + lax.rem(index, part_rows)
    col_id = col_start + lax.broadcasted_iota(jnp.int32, (rows, LANES), 1)
    occ = occ_ref[...]
    for twin in range(block_cols // 2):
        diagonal = jnp.where(row_id == col_id + twin * LANES, occ, 0.0)
        out_ref[:, twin * LANES : (twin + 1) * LANES] = (tall[twin] + diagonal).astype(
            jnp.bfloat16
        )


def load_panel(panel, pieces, mates, sems, first):
    me = lax.axis_index("row")
    layer = lax.axis_index("layer")
    copies = []
    for shift, (piece, mate) in enumerate(zip(pieces, mates)):
        block = me ^ shift
        copies.append(
            pltpu.make_async_copy(piece, panel.at[block, :, layer], sems.at[first + 2 * shift])
        )
        copies.append(
            pltpu.make_async_copy(
                mate, panel.at[block, :, 1 - layer], sems.at[first + 2 * shift + 1]
            )
        )
    return copies


def product(left, panel, blocks):
    per_block = panel.shape[0] // blocks
    cols = panel.shape[-1]

    def term(block):
        a = left[block].reshape(-1, left.shape[-1])
        b = panel[pl.ds(block * per_block, per_block)].reshape(-1, cols)
        return jnp.dot(a, b, preferred_element_type=jnp.float32)

    total = term(0)
    if blocks <= 4:
        for block in range(1, blocks):
            total = total + term(block)
        return total
    return lax.fori_loop(1, blocks, lambda block, sofar: sofar + term(block), total)


def square_kernel(n_col, n_left, n_right, *refs):
    lefts = refs[:n_left]
    pieces = refs[n_left : n_left + n_right]
    mates = refs[n_left + n_right : n_left + 2 * n_right]
    low_ref, keep_ref, give_ref, left, panel, sems = refs[n_left + 2 * n_right :]
    layer = lax.axis_index("layer")
    copies = [
        pltpu.make_async_copy(piece, left.at[block], sems.at[index])
        for index, (piece, block) in enumerate(zip(lefts, line_blocks(n_col)))
    ]
    copies += load_panel(panel, pieces, mates, sems, n_left)
    for copy in copies:
        copy.start()
    for copy in copies:
        copy.wait()
    here = keep_ref.shape[1]
    out = [
        pltpu.make_async_copy(
            left.at[pl.ds(0, n_col), pl.ds(where * here, here)], ref, sems.at[index]
        )
        for index, (where, ref) in enumerate(((layer, keep_ref), (1 - layer, give_ref)))
    ]
    for copy in out:
        copy.start()
    low_ref[...] = product(left, panel, n_col).reshape(low_ref.shape).astype(jnp.bfloat16)
    for copy in out:
        copy.wait()


def cube_kernel(n_right, *refs):
    keep_ref, got_ref, pattern_ref = refs[:3]
    pieces = refs[3 : 3 + n_right]
    mates = refs[3 + n_right : 3 + 2 * n_right]
    out_ref, left, panel, sems = refs[3 + 2 * n_right :]
    row = lax.axis_index("row")
    layer = lax.axis_index("layer")
    copies = [
        pltpu.make_async_copy(keep_ref, left.at[:, :, layer], sems.at[0]),
        pltpu.make_async_copy(got_ref, left.at[:, :, 1 - layer], sems.at[1]),
    ]
    copies += load_panel(panel, pieces, mates, sems, 2)
    for copy in copies:
        copy.start()
    rows, cols = out_ref.shape
    pattern = pattern_ref[...].astype(jnp.float32).astype(jnp.bfloat16)
    block_rows, block_cols = pattern.shape
    across = lax.broadcasted_iota(jnp.int32, (block_cols, cols), 1)
    which = lax.broadcasted_iota(jnp.int32, (block_cols, cols), 0)
    wide = (lax.div(across, BLK) == which).astype(jnp.float32).astype(jnp.bfloat16)
    down = lax.broadcasted_iota(jnp.int32, (rows, block_rows), 0) + layer * rows
    which = lax.broadcasted_iota(jnp.int32, (rows, block_rows), 1)
    tall = (lax.div(down, BLK) == which).astype(jnp.float32).astype(jnp.bfloat16)
    mask = jnp.dot(
        jnp.dot(tall, pattern, preferred_element_type=jnp.float32).astype(jnp.bfloat16),
        wide,
        preferred_element_type=jnp.float32,
    )
    for copy in copies:
        copy.wait()
    here = left.shape[1]
    square = panel[row, pl.ds(layer * here, here)].reshape(rows, cols).astype(jnp.float32)
    out_ref[...] = mask * (3.0 * square - 2.0 * product(left, panel, left.shape[0]))


def xor_pairs(axis, shift):
    return [(i, i ^ shift) for i in range(lax.axis_size(axis))]


def gather(piece, axis):
    return [piece] + [
        lax.ppermute(piece, axis, xor_pairs(axis, shift))
        for shift in range(1, lax.axis_size(axis))
    ]


def gather_line(piece):
    count = lax.axis_size("col")
    if count != 4:
        return gather(piece, "col")
    up = lax.ppermute(piece, "col", [(0, 1), (1, 2), (2, 3)])
    down = lax.ppermute(piece, "col", [(3, 2), (2, 1), (1, 0)])
    over = lax.ppermute(piece, "col", [(0, 2), (3, 1)])
    inner = lax.axis_index("col") < 2
    near = lax.ppermute(jnp.where(inner, down, up), "col", [(2, 3), (1, 0)])
    far = lax.ppermute(over, "col", [(2, 3), (1, 0)])
    return [piece, up, down, over, near, far]


def line_blocks(count):
    me = lax.axis_index("col")
    if count != 4:
        return [me ^ shift for shift in range(count)]
    end = (me == 0) | (me == count - 1)
    return [
        me,
        jnp.where(me == 0, count, me - 1),
        me + 1,
        jnp.where(end, count + 1, me ^ 2),
        jnp.where(end, me ^ 2, count),
        jnp.where(end, me ^ 3, count + 1),
    ]


def swap(piece):
    return lax.ppermute(piece, "layer", xor_pairs("layer", 1))


def on_device(tasks, task_owner, task_slot, p_pattern, c_pattern, occupations):
    n_row, n_col, layers = (lax.axis_size(axis) for axis in ("row", "col", "layer"))
    owners = n_row * n_col
    count = tasks.shape[0]
    capacity = max(2, 2 * count // owners)
    places = owners * capacity
    block_rows, block_cols = p_pattern.shape
    part_rows = BLK // layers
    part = part_rows * BLK
    rows, cols = block_rows * part_rows, block_cols * BLK
    width = part + LANES
    layer = lax.axis_index("layer")

    paired = capacity % 16 == 0
    parcels = owners if paired else 1
    sent = pl.pallas_call(
        functools.partial(pack_kernel, owners, capacity, p_pattern.shape, paired),
        out_shape=[jax.ShapeDtypeStruct((places // parcels, width), jnp.bfloat16)] * parcels,
        in_specs=[any_ref(), whole_ref(), whole_ref()],
        out_specs=[whole_ref()] * parcels,
        scratch_shapes=[pltpu.VMEM((count, part), jnp.bfloat16), pltpu.SemaphoreType.DMA],
        compiler_params=params(2 * (places + count) * width),
        cost_estimate=cost(2 * places * count * width, 2 * (places + count) * width),
        name="pack",
    )(tasks, task_owner.reshape(1, count), task_slot.reshape(1, count))
    if paired:
        got = [sent[0]] + [
            lax.ppermute(sent[k], ("row", "col"), [(i, i ^ k) for i in range(owners)])
            for k in range(1, owners)
        ]
    else:
        got = [
            lax.all_to_all(
                sent[0].reshape(owners, capacity, width),
                ("row", "col"),
                split_axis=0,
                concat_axis=0,
                tiled=True,
            ).reshape(places, width)
        ]

    pattern_row = p_pattern.astype(jnp.float32).T.reshape(1, block_rows * block_cols)
    pattern_row = jnp.pad(pattern_row, ((0, 0), (0, LANES - block_rows * block_cols)))
    occ_part = lax.dynamic_index_in_dim(
        occupations.reshape(block_rows, layers, part_rows), layer, 1, keepdims=False
    ).reshape(rows, 1)
    density = pl.pallas_call(
        functools.partial(build_kernel, p_pattern.shape),
        out_shape=jax.ShapeDtypeStruct((rows, cols), jnp.bfloat16),
        in_specs=[whole_ref()] * (2 + len(got)),
        out_specs=whole_ref(),
        scratch_shapes=[pltpu.VMEM((cols // LANES, rows, LANES), jnp.float32)],
        compiler_params=params(2 * places * width + 6 * rows * cols),
        cost_estimate=cost(2 * places * block_rows * block_cols * part, 2 * places * width),
        name="build",
    )(pattern_row, occ_part, *got)
    density = density.reshape(block_rows, part_rows, cols)

    pieces = gather(density, "row")
    mates = [swap(piece) for piece in pieces]
    lefts = gather_line(density)
    n_left = len(lefts)
    spare = 0 if n_left == n_col else 2
    flops = 2 * rows * cols * n_col * cols
    panel_shape = (n_row, block_rows, layers, part_rows, cols)
    here = block_rows // layers
    held = 2 * ((n_col + 3) * rows * cols + 2 * n_row * rows * cols) + 8 * rows * cols
    half = jax.ShapeDtypeStruct((n_col, here, part_rows, cols), jnp.bfloat16)
    square, keep, give = pl.pallas_call(
        functools.partial(square_kernel, n_col, n_left, n_row),
        out_shape=[jax.ShapeDtypeStruct(density.shape, jnp.bfloat16), half, half],
        in_specs=[any_ref()] * (n_left + 2 * n_row),
        out_specs=[whole_ref(), any_ref(), any_ref()],
        scratch_shapes=[
            pltpu.VMEM((n_col + spare, block_rows, part_rows, cols), jnp.bfloat16),
            pltpu.VMEM(panel_shape, jnp.bfloat16),
            pltpu.SemaphoreType.DMA((n_left + 2 * n_row,)),
        ],
        compiler_params=params(held),
        cost_estimate=cost(flops, 8 * 1024 * 1024),
        name="square",
    )(*lefts, *pieces, *mates)

    received = swap(give)
    pieces = gather(square, "row")
    mates = [swap(piece) for piece in pieces]
    return pl.pallas_call(
        functools.partial(cube_kernel, n_row),
        out_shape=jax.ShapeDtypeStruct((rows, cols), jnp.float32),
        in_specs=[any_ref()] * 2 + [whole_ref()] + [any_ref()] * (2 * n_row),
        out_specs=whole_ref(),
        scratch_shapes=[
            pltpu.VMEM((n_col, here, layers, part_rows, cols), jnp.bfloat16),
            pltpu.VMEM(panel_shape, jnp.bfloat16),
            pltpu.SemaphoreType.DMA((2 + 2 * n_row,)),
        ],
        compiler_params=params(held),
        cost_estimate=cost(flops, 8 * 1024 * 1024),
        name="cube",
    )(keep, received, c_pattern, *pieces, *mates)


def solution(mesh):
    return jax.shard_map(
        on_device,
        mesh=mesh,
        in_specs=(
            P(("row", "col"), None),
            P(("row", "col"), None),
            P(("row", "col")),
            P("row", "col"),
            P("row", "col"),
            P("row"),
        ),
        out_specs=P(("row", "layer"), "col"),
        check_vma=False,
    )
```

```python
import functools

import jax
import jax.numpy as jnp
from jax import lax
from jax.experimental import pallas as pl
from jax.experimental.pallas import tpu as pltpu
from jax.sharding import PartitionSpec as P

BLK = 64
LANES = 128


def params(held):
    return pltpu.CompilerParams(vmem_limit_bytes=held + 6 * 1024 * 1024)


def whole_ref():
    return pl.BlockSpec(memory_space=pltpu.VMEM)


def any_ref():
    return pl.BlockSpec(memory_space=pl.ANY)


def cost(flops, bytes_accessed):
    return pl.CostEstimate(flops=flops, bytes_accessed=bytes_accessed, transcendentals=0)


def pack_kernel(owners, capacity, block_shape, paired, tasks_ref, owner_ref, slot_ref, *refs):
    out_refs, held, sem = refs[:-2], refs[-2], refs[-1]
    count, part = held.shape
    layer = lax.axis_index("layer")
    start = pl.multiple_of(layer * part, part)
    copy = pltpu.make_async_copy(tasks_ref.at[:, pl.ds(start, part)], held, sem)
    copy.start()
    block_rows, block_cols = block_shape
    slot_row = slot_ref[...]
    slot_row = lax.rem(slot_row, block_cols) * block_rows + lax.div(slot_row, block_cols)
    across = lax.broadcasted_iota(jnp.int32, (count, count), 1)
    down = lax.broadcasted_iota(jnp.int32, (count, count), 0)
    slot_col = jnp.sum(
        jnp.where(across == down, slot_row.astype(jnp.float32), 0.0), axis=1, keepdims=True
    )
    owner_row = owner_ref[...]
    if paired:
        owner_row = owner_row ^ (
            lax.axis_index("row") * lax.axis_size("col") + lax.axis_index("col")
        )
    same = (lax.broadcasted_iota(jnp.int32, (owners, count), 0) == owner_row).astype(jnp.float32)
    before = (down < across).astype(jnp.float32).astype(jnp.bfloat16)
    ahead = jnp.dot(same.astype(jnp.bfloat16), before, preferred_element_type=jnp.float32)
    placed = jnp.sum(ahead * same, axis=0, keepdims=True).astype(jnp.int32)
    target = owner_row * capacity + placed
    places = owners * capacity
    move = (
        (lax.broadcasted_iota(jnp.int32, (places, count), 0) == target)
        .astype(jnp.float32)
        .astype(jnp.bfloat16)
    )

    def put(at, end, blocks):
        moved = jnp.dot(move, blocks, preferred_element_type=jnp.float32).astype(jnp.bfloat16)
        if not paired:
            out_refs[0][:, at:end] = moved
            return
        n_row, n_col = lax.axis_size("row"), lax.axis_size("col")
        if at < part + LANES - part // 2:
            for over, out_ref in enumerate(out_refs[:n_col]):
                for down in range(n_row):
                    place = (down * n_col + over) * capacity
                    out_ref[down * capacity : (down + 1) * capacity, at:end] = moved[
                        place : place + capacity
                    ]
        else:
            at, end = at - (part // 2 + LANES), end - (part // 2 + LANES)
            each = n_col * capacity
            for down, out_ref in enumerate(out_refs[n_col:]):
                out_ref[:, at:end] = moved[down * each : (down + 1) * each]

    slots = jnp.broadcast_to(slot_col, (count, LANES)).astype(jnp.bfloat16)
    put(0, LANES, slots)
    copy.wait()
    step = 512
    for at in range(0, part, step):
        put(LANES + at, LANES + at + step, held[:, at : at + step])


def mix_kernel(arrivals, capacity, *refs):
    for shift, out_ref in enumerate(refs[arrivals:], 1):
        for index, ref in enumerate(refs[:arrivals]):
            out_ref[index * capacity : (index + 1) * capacity, :] = ref[
                shift * capacity : (shift + 1) * capacity, :
            ]


def build_kernel(block_shape, pattern_ref, occ_ref, *refs):
    got_refs, out_ref, tall = refs[:-2], refs[-2], refs[-1]
    block_rows, block_cols = block_shape
    rows, cols = out_ref.shape
    part_rows = rows // block_rows
    part = part_rows * BLK

    def got(at, end):
        if len(got_refs) == 1:
            return got_refs[0][:, at:end]
        n_row, n_col = lax.axis_size("row"), lax.axis_size("col")
        first, second = got_refs[: n_col + n_row - 1], got_refs[n_col + n_row - 1 :]
        capacity = got_refs[0].shape[0] // n_row
        if at < part // 2 + LANES:
            parts = [ref[:capacity, at:end] for ref in first[:n_col]]
            parts += [ref[:, at:end] for ref in first[n_col:]]
        else:
            at, end = at - (part // 2 + LANES), end - (part // 2 + LANES)
            parts = []
            for down in range(n_row):
                parts.append(second[down][:capacity, at:end])
                parts += [
                    ref[down * capacity : (down + 1) * capacity, at:end] for ref in second[n_row:]
                ]
        return jnp.concatenate(parts, axis=0)

    slots = got(0, LANES).astype(jnp.float32)
    lane = lax.broadcasted_iota(jnp.int32, slots.shape, 1).astype(jnp.float32)
    marks = jnp.where(slots == lane, pattern_ref[...], 0.0)
    marks = marks.T[: block_rows * block_cols].astype(jnp.bfloat16)
    low = lax.broadcasted_iota(jnp.int32, (block_rows, LANES), 1) < BLK
    step = 256
    for at in range(0, part, step):
        summed = jnp.dot(marks, got(LANES + at, LANES + at + step), preferred_element_type=jnp.float32)
        for pair in range(step // LANES):
            lanes = slice(pair * LANES, (pair + 1) * LANES)
            row = (at // LANES + pair) * 2
            for twin in range(block_cols // 2):
                first = summed[twin * 2 * block_rows : (twin * 2 + 1) * block_rows, lanes]
                second = summed[(twin * 2 + 1) * block_rows : (twin * 2 + 2) * block_rows, lanes]
                tall[twin, pl.ds(row, block_rows, stride=part_rows), :] = jnp.where(
                    low, first, pltpu.roll(second, BLK, 1)
                )
                tall[twin, pl.ds(row + 1, block_rows, stride=part_rows), :] = jnp.where(
                    low, pltpu.roll(first, BLK, 1), second
                )
    row_start = lax.axis_index("row") * (block_rows * BLK) + lax.axis_index("layer") * part_rows
    col_start = lax.axis_index("col") * cols
    index = lax.broadcasted_iota(jnp.int32, (rows, LANES), 0)
    row_id = row_start + lax.div(index, part_rows) * BLK + lax.rem(index, part_rows)
    col_id = col_start + lax.broadcasted_iota(jnp.int32, (rows, LANES), 1)
    occ = occ_ref[...]
    for twin in range(block_cols // 2):
        diagonal = jnp.where(row_id == col_id + twin * LANES, occ, 0.0)
        out_ref[:, twin * LANES : (twin + 1) * LANES] = (tall[twin] + diagonal).astype(
            jnp.bfloat16
        )


def load_panel(panel, pieces, mates, sems, first):
    me = lax.axis_index("row")
    layer = lax.axis_index("layer")
    copies = []
    for shift, (piece, mate) in enumerate(zip(pieces, mates)):
        block = me ^ shift
        copies.append(
            pltpu.make_async_copy(piece, panel.at[block, :, layer], sems.at[first + 2 * shift])
        )
        copies.append(
            pltpu.make_async_copy(
                mate, panel.at[block, :, 1 - layer], sems.at[first + 2 * shift + 1]
            )
        )
    return copies


def product(left, panel, blocks):
    per_block = panel.shape[0] // blocks
    cols = panel.shape[-1]

    def term(block):
        a = left[block].reshape(-1, left.shape[-1])
        b = panel[pl.ds(block * per_block, per_block)].reshape(-1, cols)
        return jnp.dot(a, b, preferred_element_type=jnp.float32)

    total = term(0)
    if blocks <= 4:
        for block in range(1, blocks):
            total = total + term(block)
        return total
    return lax.fori_loop(1, blocks, lambda block, sofar: sofar + term(block), total)


def square_kernel(n_col, n_left, n_right, *refs):
    lefts = refs[:n_left]
    pieces = refs[n_left : n_left + n_right]
    mates = refs[n_left + n_right : n_left + 2 * n_right]
    low_ref, keep_ref, give_ref, left, panel, sems = refs[n_left + 2 * n_right :]
    layer = lax.axis_index("layer")
    copies = [
        pltpu.make_async_copy(piece, left.at[block], sems.at[index])
        for index, (piece, block) in enumerate(zip(lefts, line_blocks(n_col)))
    ]
    copies += load_panel(panel, pieces, mates, sems, n_left)
    for copy in copies:
        copy.start()
    for copy in copies:
        copy.wait()
    here = keep_ref.shape[1]
    out = [
        pltpu.make_async_copy(
            left.at[pl.ds(0, n_col), pl.ds(where * here, here)], ref, sems.at[index]
        )
        for index, (where, ref) in enumerate(((layer, keep_ref), (1 - layer, give_ref)))
    ]
    for copy in out:
        copy.start()
    low_ref[...] = product(left, panel, n_col).reshape(low_ref.shape).astype(jnp.bfloat16)
    for copy in out:
        copy.wait()


def cube_kernel(n_right, *refs):
    keep_ref, got_ref, pattern_ref = refs[:3]
    pieces = refs[3 : 3 + n_right]
    mates = refs[3 + n_right : 3 + 2 * n_right]
    out_ref, left, panel, sems = refs[3 + 2 * n_right :]
    row = lax.axis_index("row")
    layer = lax.axis_index("layer")
    copies = [
        pltpu.make_async_copy(keep_ref, left.at[:, :, layer], sems.at[0]),
        pltpu.make_async_copy(got_ref, left.at[:, :, 1 - layer], sems.at[1]),
    ]
    copies += load_panel(panel, pieces, mates, sems, 2)
    for copy in copies:
        copy.start()
    rows, cols = out_ref.shape
    pattern = pattern_ref[...].astype(jnp.float32).astype(jnp.bfloat16)
    block_rows, block_cols = pattern.shape
    across = lax.broadcasted_iota(jnp.int32, (block_cols, cols), 1)
    which = lax.broadcasted_iota(jnp.int32, (block_cols, cols), 0)
    wide = (lax.div(across, BLK) == which).astype(jnp.float32).astype(jnp.bfloat16)
    down = lax.broadcasted_iota(jnp.int32, (rows, block_rows), 0) + layer * rows
    which = lax.broadcasted_iota(jnp.int32, (rows, block_rows), 1)
    tall = (lax.div(down, BLK) == which).astype(jnp.float32).astype(jnp.bfloat16)
    mask = jnp.dot(
        jnp.dot(tall, pattern, preferred_element_type=jnp.float32).astype(jnp.bfloat16),
        wide,
        preferred_element_type=jnp.float32,
    )
    for copy in copies:
        copy.wait()
    here = left.shape[1]
    square = panel[row, pl.ds(layer * here, here)].reshape(rows, cols).astype(jnp.float32)
    out_ref[...] = mask * (3.0 * square - 2.0 * product(left, panel, left.shape[0]))


def xor_pairs(axis, shift):
    return [(i, i ^ shift) for i in range(lax.axis_size(axis))]


def gather(piece, axis):
    return [piece] + [
        lax.ppermute(piece, axis, xor_pairs(axis, shift))
        for shift in range(1, lax.axis_size(axis))
    ]


def exchange(first, second, capacity):
    def relay(parcels, out_axis, in_axis):
        arrived = [parcels[0]] + [
            lax.ppermute(parcel, out_axis, xor_pairs(out_axis, shift))
            for shift, parcel in enumerate(parcels)
            if shift
        ]
        steps = lax.axis_size(in_axis)
        shape = (len(arrived) * capacity, parcels[0].shape[1])
        mixed = pl.pallas_call(
            functools.partial(mix_kernel, len(arrived), capacity),
            out_shape=[jax.ShapeDtypeStruct(shape, jnp.bfloat16)] * (steps - 1),
            in_specs=[whole_ref()] * len(arrived),
            out_specs=[whole_ref()] * (steps - 1),
            compiler_params=params(4 * steps * shape[0] * shape[1]),
            cost_estimate=cost(0, 4 * steps * shape[0] * shape[1]),
            name="mix",
        )(*arrived)
        onward = [
            lax.ppermute(parcel, in_axis, xor_pairs(in_axis, shift + 1))
            for shift, parcel in enumerate(mixed)
        ]
        return arrived + onward

    return relay(first, "col", "row") + relay(second, "row", "col")


def gather_line(piece):
    count = lax.axis_size("col")
    if count != 4:
        return gather(piece, "col")
    up = lax.ppermute(piece, "col", [(0, 1), (1, 2), (2, 3)])
    down = lax.ppermute(piece, "col", [(3, 2), (2, 1), (1, 0)])
    over = lax.ppermute(piece, "col", [(0, 2), (3, 1)])
    inner = lax.axis_index("col") < 2
    near = lax.ppermute(jnp.where(inner, down, up), "col", [(2, 3), (1, 0)])
    far = lax.ppermute(over, "col", [(2, 3), (1, 0)])
    return [piece, up, down, over, near, far]


def line_blocks(count):
    me = lax.axis_index("col")
    if count != 4:
        return [me ^ shift for shift in range(count)]
    end = (me == 0) | (me == count - 1)
    return [
        me,
        jnp.where(me == 0, count, me - 1),
        me + 1,
        jnp.where(end, count + 1, me ^ 2),
        jnp.where(end, me ^ 2, count),
        jnp.where(end, me ^ 3, count + 1),
    ]


def swap(piece):
    return lax.ppermute(piece, "layer", xor_pairs("layer", 1))


def on_device(tasks, task_owner, task_slot, p_pattern, c_pattern, occupations):
    n_row, n_col, layers = (lax.axis_size(axis) for axis in ("row", "col", "layer"))
    owners = n_row * n_col
    count = tasks.shape[0]
    capacity = max(2, 2 * count // owners)
    places = owners * capacity
    block_rows, block_cols = p_pattern.shape
    part_rows = BLK // layers
    part = part_rows * BLK
    rows, cols = block_rows * part_rows, block_cols * BLK
    width = part + LANES
    layer = lax.axis_index("layer")

    paired = capacity % 16 == 0
    if paired:
        parcels = [(n_row * capacity, part // 2 + LANES)] * n_col
        parcels += [(n_col * capacity, part - part // 2)] * n_row
    else:
        parcels = [(places, width)]
    sent = pl.pallas_call(
        functools.partial(pack_kernel, owners, capacity, p_pattern.shape, paired),
        out_shape=[jax.ShapeDtypeStruct(shape, jnp.bfloat16) for shape in parcels],
        in_specs=[any_ref(), whole_ref(), whole_ref()],
        out_specs=[whole_ref()] * len(parcels),
        scratch_shapes=[pltpu.VMEM((count, part), jnp.bfloat16), pltpu.SemaphoreType.DMA],
        compiler_params=params(2 * (places + count) * width),
        cost_estimate=cost(2 * places * count * width, 2 * (places + count) * width),
        name="pack",
    )(tasks, task_owner.reshape(1, count), task_slot.reshape(1, count))
    if paired:
        got = exchange(sent[:n_col], sent[n_col:], capacity)
    else:
        got = [
            lax.all_to_all(
                sent[0].reshape(owners, capacity, width),
                ("row", "col"),
                split_axis=0,
                concat_axis=0,
                tiled=True,
            ).reshape(places, width)
        ]

    pattern_row = p_pattern.astype(jnp.float32).T.reshape(1, block_rows * block_cols)
    pattern_row = jnp.pad(pattern_row, ((0, 0), (0, LANES - block_rows * block_cols)))
    occ_part = lax.dynamic_index_in_dim(
        occupations.reshape(block_rows, layers, part_rows), layer, 1, keepdims=False
    ).reshape(rows, 1)
    density = pl.pallas_call(
        functools.partial(build_kernel, p_pattern.shape),
        out_shape=jax.ShapeDtypeStruct((rows, cols), jnp.bfloat16),
        in_specs=[whole_ref()] * (2 + len(got)),
        out_specs=whole_ref(),
        scratch_shapes=[pltpu.VMEM((cols // LANES, rows, LANES), jnp.float32)],
        compiler_params=params(2 * places * width + 6 * rows * cols),
        cost_estimate=cost(2 * places * block_rows * block_cols * part, 2 * places * width),
        name="build",
    )(pattern_row, occ_part, *got)
    density = density.reshape(block_rows, part_rows, cols)

    lefts = gather_line(density)
    mate = swap(density)
    pieces = gather(lax.optimization_barrier((density, mate))[0], "row")
    pieces[0] = density
    mates = [mate] + [swap(piece) for piece in pieces[1:]]
    n_left = len(lefts)
    spare = 0 if n_left == n_col else 2
    flops = 2 * rows * cols * n_col * cols
    panel_shape = (n_row, block_rows, layers, part_rows, cols)
    here = block_rows // layers
    held = 2 * ((n_col + 3) * rows * cols + 2 * n_row * rows * cols) + 8 * rows * cols
    half = jax.ShapeDtypeStruct((n_col, here, part_rows, cols), jnp.bfloat16)
    square, keep, give = pl.pallas_call(
        functools.partial(square_kernel, n_col, n_left, n_row),
        out_shape=[jax.ShapeDtypeStruct(density.shape, jnp.bfloat16), half, half],
        in_specs=[any_ref()] * (n_left + 2 * n_row),
        out_specs=[whole_ref(), any_ref(), any_ref()],
        scratch_shapes=[
            pltpu.VMEM((n_col + spare, block_rows, part_rows, cols), jnp.bfloat16),
            pltpu.VMEM(panel_shape, jnp.bfloat16),
            pltpu.SemaphoreType.DMA((n_left + 2 * n_row,)),
        ],
        compiler_params=params(held),
        cost_estimate=cost(flops, 8 * 1024 * 1024),
        name="square",
    )(*lefts, *pieces, *mates)

    pieces = gather(square, "row")
    mates = [swap(piece) for piece in pieces]
    received = swap(lax.optimization_barrier((give, mates[0]))[0])
    return pl.pallas_call(
        functools.partial(cube_kernel, n_row),
        out_shape=jax.ShapeDtypeStruct((rows, cols), jnp.float32),
        in_specs=[any_ref()] * 2 + [whole_ref()] + [any_ref()] * (2 * n_row),
        out_specs=whole_ref(),
        scratch_shapes=[
            pltpu.VMEM((n_col, here, layers, part_rows, cols), jnp.bfloat16),
            pltpu.VMEM(panel_shape, jnp.bfloat16),
            pltpu.SemaphoreType.DMA((2 + 2 * n_row,)),
        ],
        compiler_params=params(held),
        cost_estimate=cost(flops, 8 * 1024 * 1024),
        name="cube",
    )(keep, received, c_pattern, *pieces, *mates)


def solution(mesh):
    return jax.shard_map(
        on_device,
        mesh=mesh,
        in_specs=(
            P(("row", "col"), None),
            P(("row", "col"), None),
            P(("row", "col")),
            P("row", "col"),
            P("row", "col"),
            P("row"),
        ),
        out_specs=P(("row", "layer"), "col"),
        check_vma=False,
    )
```

```python
import functools

import jax
import jax.numpy as jnp
from jax import lax
from jax.experimental import pallas as pl
from jax.experimental.pallas import tpu as pltpu
from jax.sharding import PartitionSpec as P

BLK = 64
LANES = 128


def params(held):
    return pltpu.CompilerParams(vmem_limit_bytes=held + 6 * 1024 * 1024)


def whole_ref():
    return pl.BlockSpec(memory_space=pltpu.VMEM)


def any_ref():
    return pl.BlockSpec(memory_space=pl.ANY)


def cost(flops, bytes_accessed):
    return pl.CostEstimate(flops=flops, bytes_accessed=bytes_accessed, transcendentals=0)


def pack_kernel(owners, capacity, block_shape, paired, tasks_ref, owner_ref, slot_ref, *refs):
    out_refs, held, sem = refs[:-2], refs[-2], refs[-1]
    count, part = held.shape
    layer = lax.axis_index("layer")
    start = pl.multiple_of(layer * part, part)
    copy = pltpu.make_async_copy(tasks_ref.at[:, pl.ds(start, part)], held, sem)
    copy.start()
    block_rows, block_cols = block_shape
    slot_row = slot_ref[...]
    slot_row = lax.rem(slot_row, block_cols) * block_rows + lax.div(slot_row, block_cols)
    across = lax.broadcasted_iota(jnp.int32, (count, count), 1)
    down = lax.broadcasted_iota(jnp.int32, (count, count), 0)
    slot_col = jnp.sum(
        jnp.where(across == down, slot_row.astype(jnp.float32), 0.0), axis=1, keepdims=True
    )
    owner_row = owner_ref[...]
    if paired:
        owner_row = owner_row ^ (
            lax.axis_index("row") * lax.axis_size("col") + lax.axis_index("col")
        )
    same = (lax.broadcasted_iota(jnp.int32, (owners, count), 0) == owner_row).astype(jnp.float32)
    before = (down < across).astype(jnp.float32).astype(jnp.bfloat16)
    ahead = jnp.dot(same.astype(jnp.bfloat16), before, preferred_element_type=jnp.float32)
    placed = jnp.sum(ahead * same, axis=0, keepdims=True).astype(jnp.int32)
    target = owner_row * capacity + placed
    places = owners * capacity
    move = (
        (lax.broadcasted_iota(jnp.int32, (places, count), 0) == target)
        .astype(jnp.float32)
        .astype(jnp.bfloat16)
    )

    def put(at, end, blocks):
        moved = jnp.dot(move, blocks, preferred_element_type=jnp.float32).astype(jnp.bfloat16)
        if not paired:
            out_refs[0][:, at:end] = moved
            return
        n_row, n_col = lax.axis_size("row"), lax.axis_size("col")
        if at < part // 2 + LANES:
            each = n_col * capacity
            for down, out_ref in enumerate(out_refs[:n_row]):
                out_ref[:, at:end] = moved[down * each : (down + 1) * each]
            return
        at, end = at - (part // 2 + LANES), end - (part // 2 + LANES)
        for over, out_ref in enumerate(out_refs[n_row:]):
            for down in range(n_row):
                place = (down * n_col + over) * capacity
                out_ref[down * capacity : (down + 1) * capacity, at:end] = moved[
                    place : place + capacity
                ]

    slots = jnp.broadcast_to(slot_col, (count, LANES)).astype(jnp.bfloat16)
    put(0, LANES, slots)
    copy.wait()
    step = 512
    for at in range(0, part, step):
        put(LANES + at, LANES + at + step, held[:, at : at + step])


def mix_kernel(n_first, n_second, capacity, *refs):
    second, first = refs[:n_second][::-1], refs[n_second : n_first + n_second]
    outs = refs[n_first + n_second :]
    for arrived, onward in ((first, outs[: n_second - 1]), (second, outs[n_second - 1 :])):
        for shift, out_ref in enumerate(onward, 1):
            for index, ref in enumerate(arrived):
                out_ref[index * capacity : (index + 1) * capacity, :] = ref[
                    shift * capacity : (shift + 1) * capacity, :
                ]


def build_kernel(block_shape, pattern_ref, occ_ref, *refs):
    got_refs, out_ref, tall = refs[:-2], refs[-2], refs[-1]
    block_rows, block_cols = block_shape
    rows, cols = out_ref.shape
    part_rows = rows // block_rows
    part = part_rows * BLK

    def got(at, end):
        if len(got_refs) == 1:
            return got_refs[0][:, at:end]
        n_row, n_col = lax.axis_size("row"), lax.axis_size("col")
        first, second = got_refs[: n_row + n_col - 1], got_refs[n_row + n_col - 1 :]
        capacity = got_refs[0].shape[0] // n_col
        if at < part // 2 + LANES:
            parts = []
            for down in range(n_row):
                parts.append(first[down][:capacity, at:end])
                parts += [
                    ref[down * capacity : (down + 1) * capacity, at:end] for ref in first[n_row:]
                ]
        else:
            at, end = at - (part // 2 + LANES), end - (part // 2 + LANES)
            parts = [ref[:capacity, at:end] for ref in second[:n_col]]
            parts += [ref[:, at:end] for ref in second[n_col:]]
        return jnp.concatenate(parts, axis=0)

    slots = got(0, LANES).astype(jnp.float32)
    lane = lax.broadcasted_iota(jnp.int32, slots.shape, 1).astype(jnp.float32)
    marks = jnp.where(slots == lane, pattern_ref[...], 0.0)
    marks = marks.T[: block_rows * block_cols].astype(jnp.bfloat16)
    low = lax.broadcasted_iota(jnp.int32, (block_rows, LANES), 1) < BLK
    step = 256
    for at in range(0, part, step):
        summed = jnp.dot(marks, got(LANES + at, LANES + at + step), preferred_element_type=jnp.float32)
        for pair in range(step // LANES):
            lanes = slice(pair * LANES, (pair + 1) * LANES)
            row = (at // LANES + pair) * 2
            for twin in range(block_cols // 2):
                first = summed[twin * 2 * block_rows : (twin * 2 + 1) * block_rows, lanes]
                second = summed[(twin * 2 + 1) * block_rows : (twin * 2 + 2) * block_rows, lanes]
                tall[twin, pl.ds(row, block_rows, stride=part_rows), :] = jnp.where(
                    low, first, pltpu.roll(second, BLK, 1)
                )
                tall[twin, pl.ds(row + 1, block_rows, stride=part_rows), :] = jnp.where(
                    low, pltpu.roll(first, BLK, 1), second
                )
    row_start = lax.axis_index("row") * (block_rows * BLK) + lax.axis_index("layer") * part_rows
    col_start = lax.axis_index("col") * cols
    index = lax.broadcasted_iota(jnp.int32, (rows, LANES), 0)
    row_id = row_start + lax.div(index, part_rows) * BLK + lax.rem(index, part_rows)
    col_id = col_start + lax.broadcasted_iota(jnp.int32, (rows, LANES), 1)
    occ = occ_ref[...]
    for twin in range(block_cols // 2):
        diagonal = jnp.where(row_id == col_id + twin * LANES, occ, 0.0)
        out_ref[:, twin * LANES : (twin + 1) * LANES] = (tall[twin] + diagonal).astype(
            jnp.bfloat16
        )


def load_panel(panel, pieces, mates, sems, first):
    me = lax.axis_index("row")
    layer = lax.axis_index("layer")
    copies = []
    for shift, (piece, mate) in enumerate(zip(pieces, mates)):
        block = me ^ shift
        copies.append(
            pltpu.make_async_copy(piece, panel.at[block, :, layer], sems.at[first + 2 * shift])
        )
        copies.append(
            pltpu.make_async_copy(
                mate, panel.at[block, :, 1 - layer], sems.at[first + 2 * shift + 1]
            )
        )
    return copies


def product(left, panel):
    blocks = left.shape[0]
    per_block = panel.shape[0] // blocks
    cols = panel.shape[-1]

    def term(block):
        a = left[block].reshape(-1, left.shape[-1])
        b = panel[pl.ds(block * per_block, per_block)].reshape(-1, cols)
        return jnp.dot(a, b, preferred_element_type=jnp.float32)

    total = term(0)
    if blocks <= 4:
        for block in range(1, blocks):
            total = total + term(block)
        return total
    return lax.fori_loop(1, blocks, lambda block, sofar: sofar + term(block), total)


def square_kernel(n_left, n_right, *refs):
    lefts = refs[:n_left]
    pieces = refs[n_left : n_left + n_right]
    mates = refs[n_left + n_right : n_left + 2 * n_right]
    low_ref, keep_ref, give_ref, left, panel, sems = refs[n_left + 2 * n_right :]
    col = lax.axis_index("col")
    layer = lax.axis_index("layer")
    copies = [
        pltpu.make_async_copy(piece, left.at[col ^ shift], sems.at[shift])
        for shift, piece in enumerate(lefts)
    ]
    copies += load_panel(panel, pieces, mates, sems, n_left)
    for copy in copies:
        copy.start()
    for copy in copies:
        copy.wait()
    here = keep_ref.shape[1]
    out = [
        pltpu.make_async_copy(
            left.at[:, pl.ds(where * here, here)], ref, sems.at[index]
        )
        for index, (where, ref) in enumerate(((layer, keep_ref), (1 - layer, give_ref)))
    ]
    for copy in out:
        copy.start()
    low_ref[...] = product(left, panel).reshape(low_ref.shape).astype(jnp.bfloat16)
    for copy in out:
        copy.wait()


def cube_kernel(n_right, *refs):
    keep_ref, got_ref, pattern_ref = refs[:3]
    pieces = refs[3 : 3 + n_right]
    mates = refs[3 + n_right : 3 + 2 * n_right]
    out_ref, left, panel, sems = refs[3 + 2 * n_right :]
    row = lax.axis_index("row")
    layer = lax.axis_index("layer")
    copies = [
        pltpu.make_async_copy(keep_ref, left.at[:, :, layer], sems.at[0]),
        pltpu.make_async_copy(got_ref, left.at[:, :, 1 - layer], sems.at[1]),
    ]
    copies += load_panel(panel, pieces, mates, sems, 2)
    for copy in copies:
        copy.start()
    rows, cols = out_ref.shape
    pattern = pattern_ref[...].astype(jnp.float32).astype(jnp.bfloat16)
    block_rows, block_cols = pattern.shape
    across = lax.broadcasted_iota(jnp.int32, (block_cols, cols), 1)
    which = lax.broadcasted_iota(jnp.int32, (block_cols, cols), 0)
    wide = (lax.div(across, BLK) == which).astype(jnp.float32).astype(jnp.bfloat16)
    down = lax.broadcasted_iota(jnp.int32, (rows, block_rows), 0) + layer * rows
    which = lax.broadcasted_iota(jnp.int32, (rows, block_rows), 1)
    tall = (lax.div(down, BLK) == which).astype(jnp.float32).astype(jnp.bfloat16)
    mask = jnp.dot(
        jnp.dot(tall, pattern, preferred_element_type=jnp.float32).astype(jnp.bfloat16),
        wide,
        preferred_element_type=jnp.float32,
    )
    for copy in copies:
        copy.wait()
    here = left.shape[1]
    square = panel[row, pl.ds(layer * here, here)].reshape(rows, cols).astype(jnp.float32)
    out_ref[...] = mask * (3.0 * square - 2.0 * product(left, panel))


def xor_pairs(axis, shift):
    return [(i, i ^ shift) for i in range(lax.axis_size(axis))]


def gather(piece, axis):
    return [piece] + [
        lax.ppermute(piece, axis, xor_pairs(axis, shift))
        for shift in range(1, lax.axis_size(axis))
    ]


def exchange(first, second, capacity):
    def send(parcels, axis):
        return [
            lax.ppermute(parcel, axis, xor_pairs(axis, shift))
            for shift, parcel in enumerate(parcels, 1)
        ]

    along_row = [first[0], *send(first[1:], "row")]
    along_col = [second[0], *send(second[1:], "col")]
    n_row, n_col = len(along_row), len(along_col)
    shapes = [(n_row * capacity, first[0].shape[1])] * (n_col - 1)
    shapes += [(n_col * capacity, second[0].shape[1])] * (n_row - 1)
    mixed = pl.pallas_call(
        functools.partial(mix_kernel, n_row, n_col, capacity),
        out_shape=[jax.ShapeDtypeStruct(shape, jnp.bfloat16) for shape in shapes],
        in_specs=[whole_ref()] * (n_row + n_col),
        out_specs=[whole_ref()] * len(shapes),
        compiler_params=params(8 * n_row * n_col * capacity * first[0].shape[1]),
        cost_estimate=cost(0, 8 * n_row * n_col * capacity * first[0].shape[1]),
        name="mix",
    )(*along_col[::-1], *along_row)
    first = along_row + send(mixed[: n_col - 1], "col")
    return first + along_col + send(mixed[n_col - 1 :], "row")


def gather_line(piece):
    count = lax.axis_size("col")
    pieces = {0: piece}
    step = count // 2
    while step:
        pieces |= {
            shift + step: lax.ppermute(held, "col", xor_pairs("col", step))
            for shift, held in pieces.items()
        }
        step //= 2
    return [pieces[shift] for shift in range(count)]


def swap(piece):
    return lax.ppermute(piece, "layer", xor_pairs("layer", 1))


def on_device(tasks, task_owner, task_slot, p_pattern, c_pattern, occupations):
    n_row, n_col, layers = (lax.axis_size(axis) for axis in ("row", "col", "layer"))
    owners = n_row * n_col
    count = tasks.shape[0]
    capacity = max(2, 2 * count // owners)
    places = owners * capacity
    block_rows, block_cols = p_pattern.shape
    part_rows = BLK // layers
    part = part_rows * BLK
    rows, cols = block_rows * part_rows, block_cols * BLK
    width = part + LANES
    layer = lax.axis_index("layer")

    paired = capacity % 16 == 0
    if paired:
        parcels = [(n_col * capacity, part // 2 + LANES)] * n_row
        parcels += [(n_row * capacity, part - part // 2)] * n_col
    else:
        parcels = [(places, width)]
    sent = pl.pallas_call(
        functools.partial(pack_kernel, owners, capacity, p_pattern.shape, paired),
        out_shape=[jax.ShapeDtypeStruct(shape, jnp.bfloat16) for shape in parcels],
        in_specs=[pl.BlockSpec(memory_space=pltpu.HBM), whole_ref(), whole_ref()],
        out_specs=[whole_ref()] * len(parcels),
        scratch_shapes=[pltpu.VMEM((count, part), jnp.bfloat16), pltpu.SemaphoreType.DMA],
        compiler_params=params(2 * (places + count) * width),
        cost_estimate=cost(2 * places * count * width, 2 * (places + count) * width),
        name="pack",
    )(tasks, task_owner.reshape(1, count), task_slot.reshape(1, count))
    if paired:
        got = exchange(sent[:n_row], sent[n_row:], capacity)
    else:
        got = [
            lax.all_to_all(
                sent[0].reshape(owners, capacity, width),
                ("row", "col"),
                split_axis=0,
                concat_axis=0,
                tiled=True,
            ).reshape(places, width)
        ]

    pattern_row = p_pattern.astype(jnp.float32).T.reshape(1, block_rows * block_cols)
    pattern_row = jnp.pad(pattern_row, ((0, 0), (0, LANES - block_rows * block_cols)))
    occ_part = lax.dynamic_index_in_dim(
        occupations.reshape(block_rows, layers, part_rows), layer, 1, keepdims=False
    ).reshape(rows, 1)
    density = pl.pallas_call(
        functools.partial(build_kernel, p_pattern.shape),
        out_shape=jax.ShapeDtypeStruct((rows, cols), jnp.bfloat16),
        in_specs=[whole_ref()] * (2 + len(got)),
        out_specs=whole_ref(),
        scratch_shapes=[pltpu.VMEM((cols // LANES, rows, LANES), jnp.float32)],
        compiler_params=params(2 * places * width + 6 * rows * cols),
        cost_estimate=cost(2 * places * block_rows * block_cols * part, 2 * places * width),
        name="build",
    )(pattern_row, occ_part, *got)
    density = density.reshape(block_rows, part_rows, cols)

    lefts = gather_line(density)
    mate = swap(density)
    pieces = gather(lax.optimization_barrier((density, mate))[0], "row")
    pieces[0] = density
    mates = [mate] + [swap(piece) for piece in pieces[1:]]
    flops = 2 * rows * cols * n_col * cols
    panel_shape = (n_row, block_rows, layers, part_rows, cols)
    here = block_rows // layers
    held = 2 * ((n_col + 3) * rows * cols + 2 * n_row * rows * cols) + 8 * rows * cols
    half = jax.ShapeDtypeStruct((n_col, here, part_rows, cols), jnp.bfloat16)
    square, keep, give = pl.pallas_call(
        functools.partial(square_kernel, n_col, n_row),
        out_shape=[jax.ShapeDtypeStruct(density.shape, jnp.bfloat16), half, half],
        in_specs=[any_ref()] * (n_col + 2 * n_row),
        out_specs=[whole_ref(), any_ref(), any_ref()],
        scratch_shapes=[
            pltpu.VMEM((n_col, block_rows, part_rows, cols), jnp.bfloat16),
            pltpu.VMEM(panel_shape, jnp.bfloat16),
            pltpu.SemaphoreType.DMA((n_col + 2 * n_row,)),
        ],
        compiler_params=params(held),
        cost_estimate=cost(flops, 8 * 1024 * 1024),
        name="square",
    )(*lefts, *pieces, *mates)

    pieces = gather(square, "row")
    mates = [swap(piece) for piece in pieces]
    received = swap(lax.optimization_barrier((give, mates[0]))[0])
    return pl.pallas_call(
        functools.partial(cube_kernel, n_row),
        out_shape=jax.ShapeDtypeStruct((rows, cols), jnp.float32),
        in_specs=[any_ref()] * 2 + [whole_ref()] + [any_ref()] * (2 * n_row),
        out_specs=whole_ref(),
        scratch_shapes=[
            pltpu.VMEM((n_col, here, layers, part_rows, cols), jnp.bfloat16),
            pltpu.VMEM(panel_shape, jnp.bfloat16),
            pltpu.SemaphoreType.DMA((2 + 2 * n_row,)),
        ],
        compiler_params=params(held),
        cost_estimate=cost(flops, 8 * 1024 * 1024),
        name="cube",
    )(keep, received, c_pattern, *pieces, *mates)


def solution(mesh):
    return jax.shard_map(
        on_device,
        mesh=mesh,
        in_specs=(
            P(("row", "col"), None),
            P(("row", "col"), None),
            P(("row", "col")),
            P("row", "col"),
            P("row", "col"),
            P("row"),
        ),
        out_specs=P(("row", "layer"), "col"),
        check_vma=False,
    )
```

```python
import functools

import jax
import jax.numpy as jnp
from jax import lax
from jax.experimental import pallas as pl
from jax.experimental.pallas import tpu as pltpu
from jax.sharding import PartitionSpec as P

BLK = 64
LANES = 128


def params(held):
    return pltpu.CompilerParams(vmem_limit_bytes=held + 6 * 1024 * 1024)


def whole_ref():
    return pl.BlockSpec(memory_space=pltpu.VMEM)


def any_ref():
    return pl.BlockSpec(memory_space=pl.ANY)


def cost(flops, bytes_accessed):
    return pl.CostEstimate(flops=flops, bytes_accessed=bytes_accessed, transcendentals=0)


def pack_kernel(owners, capacity, block_shape, paired, tasks_ref, owner_ref, slot_ref, *refs):
    out_refs, held, sem = refs[:-2], refs[-2], refs[-1]
    count, part = held.shape
    layer = lax.axis_index("layer")
    start = pl.multiple_of(layer * part, part)
    copy = pltpu.make_async_copy(tasks_ref.at[:, pl.ds(start, part)], held, sem)
    copy.start()
    block_rows, block_cols = block_shape
    slot_row = slot_ref[...]
    slot_row = lax.rem(slot_row, block_cols) * block_rows + lax.div(slot_row, block_cols)
    across = lax.broadcasted_iota(jnp.int32, (count, count), 1)
    down = lax.broadcasted_iota(jnp.int32, (count, count), 0)
    slot_col = jnp.sum(
        jnp.where(across == down, slot_row.astype(jnp.float32), 0.0), axis=1, keepdims=True
    )
    owner_row = owner_ref[...]
    if paired:
        owner_row = owner_row ^ (
            lax.axis_index("row") * lax.axis_size("col") + lax.axis_index("col")
        )
    same = (lax.broadcasted_iota(jnp.int32, (owners, count), 0) == owner_row).astype(jnp.float32)
    before = (down < across).astype(jnp.float32).astype(jnp.bfloat16)
    ahead = jnp.dot(same.astype(jnp.bfloat16), before, preferred_element_type=jnp.float32)
    placed = jnp.sum(ahead * same, axis=0, keepdims=True).astype(jnp.int32)
    target = owner_row * capacity + placed
    places = owners * capacity
    move = (
        (lax.broadcasted_iota(jnp.int32, (places, count), 0) == target)
        .astype(jnp.float32)
        .astype(jnp.bfloat16)
    )

    def put(at, end, blocks):
        moved = jnp.dot(move, blocks, preferred_element_type=jnp.float32).astype(jnp.bfloat16)
        if not paired:
            out_refs[0][:, at:end] = moved
            return
        n_row, n_col = lax.axis_size("row"), lax.axis_size("col")
        if at < part // 2 + LANES:
            for over, out_ref in enumerate(out_refs[:n_col]):
                for down in range(n_row):
                    place = (down * n_col + over) * capacity
                    out_ref[down * capacity : (down + 1) * capacity, at:end] = moved[
                        place : place + capacity
                    ]
            return
        at, end = at - (part // 2 + LANES), end - (part // 2 + LANES)
        each = n_col * capacity
        for down, out_ref in enumerate(out_refs[n_col:]):
            out_ref[:, at:end] = moved[down * each : (down + 1) * each]

    slots = jnp.broadcast_to(slot_col, (count, LANES)).astype(jnp.bfloat16)
    put(0, LANES, slots)
    copy.wait()
    step = 512
    for at in range(0, part, step):
        put(LANES + at, LANES + at + step, held[:, at : at + step])


def mix_kernel(arrivals, capacity, *refs):
    for shift, out_ref in enumerate(refs[arrivals:], 1):
        for index, ref in enumerate(refs[:arrivals]):
            out_ref[index * capacity : (index + 1) * capacity, :] = ref[
                shift * capacity : (shift + 1) * capacity, :
            ]


def merge_kernel(*refs):
    out_ref = refs[-1]
    for index, ref in enumerate(refs[:-1]):
        out_ref[index] = ref[...]


def build_kernel(half, paired, occ_ref, marks_ref, *refs):
    block_rows, part_rows, cols = refs[-2].shape
    block_cols = cols // BLK
    rows = block_rows * part_rows
    part = part_rows * BLK
    out_ref, tall = refs[-2:]
    got_refs = refs[:-2]
    front = 0
    if not half:
        got_refs, held_ref = refs[:-3], refs[-3]
        front = LANES

    def got(at, end):
        if not paired:
            skip = half * (LANES + part)
            return got_refs[0][:, skip + at : skip + end]
        n_row, n_col = lax.axis_size("row"), lax.axis_size("col")
        if not half:
            capacity = got_refs[0].shape[0] // n_row
            parts = [ref[:capacity, at:end] for ref in got_refs[:n_col]]
            parts += [ref[:, at:end] for ref in got_refs[n_col:]]
        else:
            capacity = got_refs[0].shape[0] // n_col
            parts = []
            for down in range(n_row):
                place = slice(down * capacity, (down + 1) * capacity)
                parts.append(got_refs[down][:capacity, at:end])
                parts += [ref[place, at:end] for ref in got_refs[n_row:]]
        return jnp.concatenate(parts, axis=0)

    if half:
        marks = marks_ref[...]
    else:
        slots = got(0, LANES).astype(jnp.float32)
        lane = lax.broadcasted_iota(jnp.int32, slots.shape, 1).astype(jnp.float32)
        marks = jnp.where(slots == lane, marks_ref[...], 0.0)
        marks = marks.T[: block_rows * block_cols].astype(jnp.bfloat16)
        held_ref[...] = marks
    low = lax.broadcasted_iota(jnp.int32, (block_rows, LANES), 1) < BLK
    step = 256
    for at in range(0, part, step):
        summed = jnp.dot(
            marks, got(front + at, front + at + step), preferred_element_type=jnp.float32
        )
        for pair in range(step // LANES):
            lanes = slice(pair * LANES, (pair + 1) * LANES)
            row = (at // LANES + pair) * 2
            for twin in range(block_cols // 2):
                left = summed[twin * 2 * block_rows : (twin * 2 + 1) * block_rows, lanes]
                right = summed[(twin * 2 + 1) * block_rows : (twin * 2 + 2) * block_rows, lanes]
                tall[twin, pl.ds(row, block_rows, stride=part_rows), :] = jnp.where(
                    low, left, pltpu.roll(right, BLK, 1)
                )
                tall[twin, pl.ds(row + 1, block_rows, stride=part_rows), :] = jnp.where(
                    low, pltpu.roll(left, BLK, 1), right
                )
    row_start = lax.axis_index("row") * (block_rows * BLK)
    row_start += (lax.axis_index("layer") * 2 + half) * part_rows
    col_start = lax.axis_index("col") * cols
    index = lax.broadcasted_iota(jnp.int32, (rows, LANES), 0)
    row_id = row_start + lax.div(index, part_rows) * BLK + lax.rem(index, part_rows)
    col_id = col_start + lax.broadcasted_iota(jnp.int32, (rows, LANES), 1)
    occ = occ_ref[...]
    for twin in range(block_cols // 2):
        diagonal = jnp.where(row_id == col_id + twin * LANES, occ, 0.0)
        out_ref[:, :, twin * LANES : (twin + 1) * LANES] = (
            (tall[twin] + diagonal)
            .astype(jnp.bfloat16)
            .reshape(block_rows, part_rows, LANES)
        )


def load_panel(panel, pieces, mates, sems, first):
    me = lax.axis_index("row")
    layer = lax.axis_index("layer")
    copies = []
    for shift, (piece, mate) in enumerate(zip(pieces, mates)):
        block = me ^ shift
        copies.append(
            pltpu.make_async_copy(piece, panel.at[block, :, layer], sems.at[first + 2 * shift])
        )
        copies.append(
            pltpu.make_async_copy(
                mate, panel.at[block, :, 1 - layer], sems.at[first + 2 * shift + 1]
            )
        )
    return copies


def product(left, panel):
    blocks = left.shape[0]
    per_block = panel.shape[0] // blocks
    cols = panel.shape[-1]

    def term(block):
        a = left[block].reshape(-1, left.shape[-1])
        b = panel[pl.ds(block * per_block, per_block)].reshape(-1, cols)
        return jnp.dot(a, b, preferred_element_type=jnp.float32)

    total = term(0)
    if blocks <= 4:
        for block in range(1, blocks):
            total = total + term(block)
        return total
    return lax.fori_loop(1, blocks, lambda block, sofar: sofar + term(block), total)


def square_kernel(n_col, n_row, *refs):
    lefts = refs[: 2 * n_col]
    panels = refs[2 * n_col : 2 * n_col + 4]
    low_ref, keep_ref, give_ref, left, panel, sems = refs[2 * n_col + 4 :]
    row = lax.axis_index("row")
    col = lax.axis_index("col")
    layer = lax.axis_index("layer")
    pairs = [
        (lefts[half * n_col + shift], left.at[col ^ shift, :, half])
        for half in range(2)
        for shift in range(n_col)
    ]
    for half in range(2):
        for other, ref in enumerate(panels[2 * half : 2 * half + 2]):
            where = 1 - layer if other else layer
            pairs += [
                (ref.at[shift], panel.at[row ^ shift, :, where, half]) for shift in range(n_row)
            ]
    copies = [
        pltpu.make_async_copy(source, target, sems.at[index])
        for index, (source, target) in enumerate(pairs)
    ]
    for copy in copies:
        copy.start()
    for copy in copies:
        copy.wait()
    here = keep_ref.shape[1]
    out = [
        pltpu.make_async_copy(left.at[:, pl.ds(where * here, here)], ref, sems.at[index])
        for index, (where, ref) in enumerate(((layer, keep_ref), (1 - layer, give_ref)))
    ]
    for copy in out:
        copy.start()
    low_ref[...] = product(left, panel).reshape(low_ref.shape).astype(jnp.bfloat16)
    for copy in out:
        copy.wait()


def cube_kernel(n_right, *refs):
    keep_ref, got_ref, pattern_ref = refs[:3]
    pieces = refs[3 : 3 + n_right]
    mates = refs[3 + n_right : 3 + 2 * n_right]
    out_ref, left, panel, sems = refs[3 + 2 * n_right :]
    row = lax.axis_index("row")
    layer = lax.axis_index("layer")
    copies = [
        pltpu.make_async_copy(keep_ref, left.at[:, :, layer], sems.at[0]),
        pltpu.make_async_copy(got_ref, left.at[:, :, 1 - layer], sems.at[1]),
    ]
    copies += load_panel(panel, pieces, mates, sems, 2)
    for copy in copies:
        copy.start()
    rows, cols = out_ref.shape
    pattern = pattern_ref[...].astype(jnp.float32).astype(jnp.bfloat16)
    block_rows, block_cols = pattern.shape
    across = lax.broadcasted_iota(jnp.int32, (block_cols, cols), 1)
    which = lax.broadcasted_iota(jnp.int32, (block_cols, cols), 0)
    wide = (lax.div(across, BLK) == which).astype(jnp.float32).astype(jnp.bfloat16)
    down = lax.broadcasted_iota(jnp.int32, (rows, block_rows), 0) + layer * rows
    which = lax.broadcasted_iota(jnp.int32, (rows, block_rows), 1)
    tall = (lax.div(down, BLK) == which).astype(jnp.float32).astype(jnp.bfloat16)
    mask = jnp.dot(
        jnp.dot(tall, pattern, preferred_element_type=jnp.float32).astype(jnp.bfloat16),
        wide,
        preferred_element_type=jnp.float32,
    )
    for copy in copies:
        copy.wait()
    here = left.shape[1]
    square = panel[row, pl.ds(layer * here, here)].reshape(rows, cols).astype(jnp.float32)
    out_ref[...] = mask * (3.0 * square - 2.0 * product(left, panel))


def xor_pairs(axis, shift):
    return [(i, i ^ shift) for i in range(lax.axis_size(axis))]


def gather(piece, axis):
    return [piece] + [
        lax.ppermute(piece, axis, xor_pairs(axis, shift))
        for shift in range(1, lax.axis_size(axis))
    ]


def exchange(first, second, capacity):
    def relay(parcels, out_axis, in_axis):
        arrived = [parcels[0]] + [
            lax.ppermute(parcel, out_axis, xor_pairs(out_axis, shift))
            for shift, parcel in enumerate(parcels)
            if shift
        ]
        steps = lax.axis_size(in_axis)
        shape = (len(arrived) * capacity, parcels[0].shape[1])
        mixed = pl.pallas_call(
            functools.partial(mix_kernel, len(arrived), capacity),
            out_shape=[jax.ShapeDtypeStruct(shape, jnp.bfloat16)] * (steps - 1),
            in_specs=[whole_ref()] * len(arrived),
            out_specs=[whole_ref()] * (steps - 1),
            compiler_params=params(4 * steps * shape[0] * shape[1]),
            cost_estimate=cost(0, 4 * steps * shape[0] * shape[1]),
            name="mix",
        )(*arrived)
        return arrived + [
            lax.ppermute(parcel, in_axis, xor_pairs(in_axis, shift))
            for shift, parcel in enumerate(mixed, 1)
        ]

    return relay(first, "col", "row"), relay(second, "row", "col")


def after(value, *earlier):
    return lax.optimization_barrier((value, earlier))[0]


def gather_rows(piece, *earlier):
    pieces = after(gather(piece, "row"), *earlier)
    merged = pl.pallas_call(
        merge_kernel,
        out_shape=jax.ShapeDtypeStruct((len(pieces), *piece.shape), piece.dtype),
        in_specs=[whole_ref()] * len(pieces),
        out_specs=whole_ref(),
        compiler_params=params(4 * len(pieces) * piece.size),
        cost_estimate=cost(0, 4 * len(pieces) * piece.size),
        name="merge",
    )(*pieces)
    return [merged, swap(merged)]


def gather_line(piece):
    count = lax.axis_size("col")
    pieces = {0: piece}
    step = count // 2
    while step:
        pieces |= {
            shift + step: lax.ppermute(held, "col", xor_pairs("col", step))
            for shift, held in pieces.items()
        }
        step //= 2
    return [pieces[shift] for shift in range(count)]


def swap(piece):
    return lax.ppermute(piece, "layer", xor_pairs("layer", 1))


def on_device(tasks, task_owner, task_slot, p_pattern, c_pattern, occupations):
    n_row, n_col, layers = (lax.axis_size(axis) for axis in ("row", "col", "layer"))
    owners = n_row * n_col
    count = tasks.shape[0]
    capacity = max(2, 2 * count // owners)
    places = owners * capacity
    block_rows, block_cols = p_pattern.shape
    part_rows = BLK // layers
    part = part_rows * BLK
    rows, cols = block_rows * part_rows, block_cols * BLK
    width = part + LANES
    layer = lax.axis_index("layer")

    paired = capacity % 16 == 0
    if paired:
        parcels = [(n_row * capacity, part // 2 + LANES)] * n_col
        parcels += [(n_col * capacity, part - part // 2)] * n_row
    else:
        parcels = [(places, width)]
    sent = pl.pallas_call(
        functools.partial(pack_kernel, owners, capacity, p_pattern.shape, paired),
        out_shape=[jax.ShapeDtypeStruct(shape, jnp.bfloat16) for shape in parcels],
        in_specs=[pl.BlockSpec(memory_space=pltpu.HBM), whole_ref(), whole_ref()],
        out_specs=[whole_ref()] * len(parcels),
        scratch_shapes=[pltpu.VMEM((count, part), jnp.bfloat16), pltpu.SemaphoreType.DMA],
        compiler_params=params(2 * (places + count) * width),
        cost_estimate=cost(2 * places * count * width, 2 * (places + count) * width),
        name="pack",
    )(tasks, task_owner.reshape(1, count), task_slot.reshape(1, count))
    if paired:
        got = list(exchange(sent[:n_col], sent[n_col:], capacity))
    else:
        got = [
            [
                lax.all_to_all(
                    sent[0].reshape(owners, capacity, width),
                    ("row", "col"),
                    split_axis=0,
                    concat_axis=0,
                    tiled=True,
                ).reshape(places, width)
            ]
        ] * 2

    slots_here = block_rows * block_cols
    pattern_row = p_pattern.astype(jnp.float32).T.reshape(1, slots_here)
    marks = jnp.pad(pattern_row, ((0, 0), (0, LANES - slots_here)))
    half_rows = part_rows // 2
    occ_here = lax.dynamic_index_in_dim(
        occupations.reshape(block_rows, layers, 2, half_rows), layer, 1, keepdims=False
    )
    half_shape = jax.ShapeDtypeStruct((block_rows, half_rows, cols), jnp.bfloat16)
    marks_shape = jax.ShapeDtypeStruct((slots_here, places), jnp.bfloat16)
    lefts, panels = [], []
    for half in range(2):
        built = pl.pallas_call(
            functools.partial(build_kernel, half, paired),
            out_shape=[half_shape] if half else [marks_shape, half_shape],
            in_specs=[whole_ref()] * (2 + len(got[half])),
            out_specs=[whole_ref()] * (1 if half else 2),
            scratch_shapes=[pltpu.VMEM((cols // LANES, rows // 2, LANES), jnp.float32)],
            compiler_params=params(2 * places * width + 6 * rows * cols),
            cost_estimate=cost(places * slots_here * part, places * width),
            name="build",
        )(occ_here[:, half].reshape(rows // 2, 1), marks, *got[half])
        density = built[-1]
        marks = built[0]
        line = gather_line(density)
        lefts += line
        if half:
            panels += gather_rows(density, lefts[:-1])
        else:
            panels += gather_rows(density, line[1])
            got[1] = after(got[1], line[n_col // 2])

    flops = 2 * rows * cols * n_col * cols
    panel_shape = (n_row, block_rows, layers, part_rows, cols)
    here = block_rows // layers
    held = 2 * ((n_col + 3) * rows * cols + 2 * n_row * rows * cols) + 8 * rows * cols
    share = jax.ShapeDtypeStruct((n_col, here, 2, half_rows, cols), jnp.bfloat16)
    square, keep, give = pl.pallas_call(
        functools.partial(square_kernel, n_col, n_row),
        out_shape=[
            jax.ShapeDtypeStruct((block_rows, part_rows, cols), jnp.bfloat16),
            share,
            share,
        ],
        in_specs=[any_ref()] * (2 * n_col + 4),
        out_specs=[whole_ref(), any_ref(), any_ref()],
        scratch_shapes=[
            pltpu.VMEM((n_col, block_rows, 2, half_rows, cols), jnp.bfloat16),
            pltpu.VMEM((n_row, block_rows, layers, 2, half_rows, cols), jnp.bfloat16),
            pltpu.SemaphoreType.DMA((2 * n_col + 4 * n_row,)),
        ],
        compiler_params=params(held),
        cost_estimate=cost(flops, 8 * 1024 * 1024),
        name="square",
    )(*lefts, *panels)

    pieces = gather(square, "row")
    mates = [swap(piece) for piece in pieces]
    received = swap(lax.optimization_barrier((give, mates[0]))[0])
    return pl.pallas_call(
        functools.partial(cube_kernel, n_row),
        out_shape=jax.ShapeDtypeStruct((rows, cols), jnp.float32),
        in_specs=[any_ref()] * 2 + [whole_ref()] + [any_ref()] * (2 * n_row),
        out_specs=whole_ref(),
        scratch_shapes=[
            pltpu.VMEM((n_col, here, layers, 2, half_rows, cols), jnp.bfloat16),
            pltpu.VMEM(panel_shape, jnp.bfloat16),
            pltpu.SemaphoreType.DMA((2 + 2 * n_row,)),
        ],
        compiler_params=params(held),
        cost_estimate=cost(flops, 8 * 1024 * 1024),
        name="cube",
    )(keep, received, c_pattern, *pieces, *mates)


def solution(mesh):
    return jax.shard_map(
        on_device,
        mesh=mesh,
        in_specs=(
            P(("row", "col"), None),
            P(("row", "col"), None),
            P(("row", "col")),
            P("row", "col"),
            P("row", "col"),
            P("row"),
        ),
        out_specs=P(("row", "layer"), "col"),
        check_vma=False,
    )
```

```python
import functools

import jax
import jax.numpy as jnp
from jax import lax
from jax.experimental import pallas as pl
from jax.experimental.pallas import tpu as pltpu
from jax.sharding import PartitionSpec as P

BLK = 64
LANES = 128


def params(held):
    return pltpu.CompilerParams(vmem_limit_bytes=held + 6 * 1024 * 1024)


def whole_ref():
    return pl.BlockSpec(memory_space=pltpu.VMEM)


def any_ref():
    return pl.BlockSpec(memory_space=pl.ANY)


def cost(flops, bytes_accessed):
    return pl.CostEstimate(flops=flops, bytes_accessed=bytes_accessed, transcendentals=0)


def pack_kernel(owners, capacity, block_shape, paired, tasks_ref, owner_ref, slot_ref, *refs):
    out_refs, held, sem = refs[:-2], refs[-2], refs[-1]
    count, part = held.shape
    layer = lax.axis_index("layer")
    start = pl.multiple_of(layer * part, part)
    copy = pltpu.make_async_copy(tasks_ref.at[:, pl.ds(start, part)], held, sem)
    copy.start()
    block_rows, block_cols = block_shape
    slot_row = slot_ref[...]
    slot_row = lax.rem(slot_row, block_cols) * block_rows + lax.div(slot_row, block_cols)
    across = lax.broadcasted_iota(jnp.int32, (count, count), 1)
    down = lax.broadcasted_iota(jnp.int32, (count, count), 0)
    slot_col = jnp.sum(
        jnp.where(across == down, slot_row.astype(jnp.float32), 0.0), axis=1, keepdims=True
    )
    owner_row = owner_ref[...]
    if paired:
        owner_row = owner_row ^ (
            lax.axis_index("row") * lax.axis_size("col") + lax.axis_index("col")
        )
    same = (lax.broadcasted_iota(jnp.int32, (owners, count), 0) == owner_row).astype(jnp.float32)
    before = (down < across).astype(jnp.float32).astype(jnp.bfloat16)
    ahead = jnp.dot(same.astype(jnp.bfloat16), before, preferred_element_type=jnp.float32)
    placed = jnp.sum(ahead * same, axis=0, keepdims=True).astype(jnp.int32)
    target = owner_row * capacity + placed
    places = owners * capacity
    move = (
        (lax.broadcasted_iota(jnp.int32, (places, count), 0) == target)
        .astype(jnp.float32)
        .astype(jnp.bfloat16)
    )

    def put(at, end, blocks):
        moved = jnp.dot(move, blocks, preferred_element_type=jnp.float32).astype(jnp.bfloat16)
        if not paired:
            out_refs[0][:, at:end] = moved
            return
        n_row, n_col = lax.axis_size("row"), lax.axis_size("col")
        if at < part // 2 + LANES:
            for over, out_ref in enumerate(out_refs[:n_col]):
                for down in range(n_row):
                    place = (down * n_col + over) * capacity
                    out_ref[down * capacity : (down + 1) * capacity, at:end] = moved[
                        place : place + capacity
                    ]
            return
        at, end = at - (part // 2 + LANES), end - (part // 2 + LANES)
        each = n_col * capacity
        for down, out_ref in enumerate(out_refs[n_col:]):
            out_ref[:, at:end] = moved[down * each : (down + 1) * each]

    slots = jnp.broadcast_to(slot_col, (count, LANES)).astype(jnp.bfloat16)
    put(0, LANES, slots)
    copy.wait()
    step = 512
    for at in range(0, part, step):
        put(LANES + at, LANES + at + step, held[:, at : at + step])


def mix_kernel(arrivals, capacity, *refs):
    for shift, out_ref in enumerate(refs[arrivals:], 1):
        for index, ref in enumerate(refs[:arrivals]):
            out_ref[index * capacity : (index + 1) * capacity, :] = ref[
                shift * capacity : (shift + 1) * capacity, :
            ]


def build_kernel(half, paired, occ_ref, marks_ref, *refs):
    block_rows, cols = refs[-2].shape[0], refs[-2].shape[2]
    part_rows = BLK // lax.axis_size("layer") // 2
    block_cols = cols // BLK
    rows = block_rows * part_rows
    part = part_rows * BLK
    out_ref, tall = refs[-2:]
    got_refs = refs[:-2]
    front = 0
    if half:
        got_refs, first_ref = refs[:-3], refs[-3]
        out_ref[:, :part_rows] = first_ref[...]
    else:
        got_refs, held_ref = refs[:-3], refs[-3]
        front = LANES

    def got(at, end):
        if not paired:
            skip = half * (LANES + part)
            return got_refs[0][:, skip + at : skip + end]
        n_row, n_col = lax.axis_size("row"), lax.axis_size("col")
        if not half:
            capacity = got_refs[0].shape[0] // n_row
            parts = [ref[:capacity, at:end] for ref in got_refs[:n_col]]
            parts += [ref[:, at:end] for ref in got_refs[n_col:]]
        else:
            capacity = got_refs[0].shape[0] // n_col
            parts = []
            for down in range(n_row):
                place = slice(down * capacity, (down + 1) * capacity)
                parts.append(got_refs[down][:capacity, at:end])
                parts += [ref[place, at:end] for ref in got_refs[n_row:]]
        return jnp.concatenate(parts, axis=0)

    if half:
        marks = marks_ref[...]
    else:
        slots = got(0, LANES).astype(jnp.float32)
        lane = lax.broadcasted_iota(jnp.int32, slots.shape, 1).astype(jnp.float32)
        marks = jnp.where(slots == lane, marks_ref[...], 0.0)
        marks = marks.T[: block_rows * block_cols].astype(jnp.bfloat16)
        held_ref[...] = marks
    low = lax.broadcasted_iota(jnp.int32, (block_rows, LANES), 1) < BLK
    step = 256
    for at in range(0, part, step):
        summed = jnp.dot(
            marks, got(front + at, front + at + step), preferred_element_type=jnp.float32
        )
        for pair in range(step // LANES):
            lanes = slice(pair * LANES, (pair + 1) * LANES)
            row = (at // LANES + pair) * 2
            for twin in range(block_cols // 2):
                left = summed[twin * 2 * block_rows : (twin * 2 + 1) * block_rows, lanes]
                right = summed[(twin * 2 + 1) * block_rows : (twin * 2 + 2) * block_rows, lanes]
                tall[twin, pl.ds(row, block_rows, stride=part_rows), :] = jnp.where(
                    low, left, pltpu.roll(right, BLK, 1)
                )
                tall[twin, pl.ds(row + 1, block_rows, stride=part_rows), :] = jnp.where(
                    low, pltpu.roll(left, BLK, 1), right
                )
    row_start = lax.axis_index("row") * (block_rows * BLK)
    row_start += (lax.axis_index("layer") * 2 + half) * part_rows
    col_start = lax.axis_index("col") * cols
    index = lax.broadcasted_iota(jnp.int32, (rows, LANES), 0)
    row_id = row_start + lax.div(index, part_rows) * BLK + lax.rem(index, part_rows)
    col_id = col_start + lax.broadcasted_iota(jnp.int32, (rows, LANES), 1)
    occ = occ_ref[...]
    for twin in range(block_cols // 2):
        diagonal = jnp.where(row_id == col_id + twin * LANES, occ, 0.0)
        here = slice(half * part_rows, (half + 1) * part_rows)
        out_ref[:, here, twin * LANES : (twin + 1) * LANES] = (
            (tall[twin] + diagonal)
            .astype(jnp.bfloat16)
            .reshape(block_rows, part_rows, LANES)
        )


def load_panel(panel, pieces, mates, sems, first):
    me = lax.axis_index("row")
    layer = lax.axis_index("layer")
    copies = []
    for shift, (piece, mate) in enumerate(zip(pieces, mates)):
        block = me ^ shift
        copies.append(
            pltpu.make_async_copy(piece, panel.at[block, :, layer], sems.at[first + 2 * shift])
        )
        copies.append(
            pltpu.make_async_copy(
                mate, panel.at[block, :, 1 - layer], sems.at[first + 2 * shift + 1]
            )
        )
    return copies


def product(left, panel):
    blocks = left.shape[0]
    per_block = panel.shape[0] // blocks
    cols = panel.shape[-1]

    def term(block):
        a = left[block].reshape(-1, left.shape[-1])
        b = panel[pl.ds(block * per_block, per_block)].reshape(-1, cols)
        return jnp.dot(a, b, preferred_element_type=jnp.float32)

    total = term(0)
    if blocks <= 4:
        for block in range(1, blocks):
            total = total + term(block)
        return total
    return lax.fori_loop(1, blocks, lambda block, sofar: sofar + term(block), total)


def square_kernel(n_left, n_right, *refs):
    lefts = refs[:n_left]
    pieces = refs[n_left : n_left + n_right]
    mates = refs[n_left + n_right : n_left + 2 * n_right]
    low_ref, keep_ref, give_ref, left, panel, sems = refs[n_left + 2 * n_right :]
    col = lax.axis_index("col")
    layer = lax.axis_index("layer")
    copies = [
        pltpu.make_async_copy(piece, left.at[col ^ shift], sems.at[shift])
        for shift, piece in enumerate(lefts)
    ]
    copies += load_panel(panel, pieces, mates, sems, n_left)
    for copy in copies:
        copy.start()
    for copy in copies:
        copy.wait()
    here = keep_ref.shape[1]
    out = [
        pltpu.make_async_copy(
            left.at[:, pl.ds(where * here, here)], ref, sems.at[index]
        )
        for index, (where, ref) in enumerate(((layer, keep_ref), (1 - layer, give_ref)))
    ]
    for copy in out:
        copy.start()
    low_ref[...] = product(left, panel).reshape(low_ref.shape).astype(jnp.bfloat16)
    for copy in out:
        copy.wait()


def cube_kernel(n_right, *refs):
    keep_ref, got_ref, pattern_ref = refs[:3]
    pieces = refs[3 : 3 + n_right]
    mates = refs[3 + n_right : 3 + 2 * n_right]
    out_ref, left, panel, sems = refs[3 + 2 * n_right :]
    row = lax.axis_index("row")
    layer = lax.axis_index("layer")
    copies = [
        pltpu.make_async_copy(keep_ref, left.at[:, :, layer], sems.at[0]),
        pltpu.make_async_copy(got_ref, left.at[:, :, 1 - layer], sems.at[1]),
    ]
    copies += load_panel(panel, pieces, mates, sems, 2)
    for copy in copies:
        copy.start()
    rows, cols = out_ref.shape
    pattern = pattern_ref[...].astype(jnp.float32).astype(jnp.bfloat16)
    block_rows, block_cols = pattern.shape
    across = lax.broadcasted_iota(jnp.int32, (block_cols, cols), 1)
    which = lax.broadcasted_iota(jnp.int32, (block_cols, cols), 0)
    wide = (lax.div(across, BLK) == which).astype(jnp.float32).astype(jnp.bfloat16)
    down = lax.broadcasted_iota(jnp.int32, (rows, block_rows), 0) + layer * rows
    which = lax.broadcasted_iota(jnp.int32, (rows, block_rows), 1)
    tall = (lax.div(down, BLK) == which).astype(jnp.float32).astype(jnp.bfloat16)
    mask = jnp.dot(
        jnp.dot(tall, pattern, preferred_element_type=jnp.float32).astype(jnp.bfloat16),
        wide,
        preferred_element_type=jnp.float32,
    )
    for copy in copies:
        copy.wait()
    here = left.shape[1]
    square = panel[row, pl.ds(layer * here, here)].reshape(rows, cols).astype(jnp.float32)
    out_ref[...] = mask * (3.0 * square - 2.0 * product(left, panel))


def xor_pairs(axis, shift):
    return [(i, i ^ shift) for i in range(lax.axis_size(axis))]


def gather(piece, axis):
    return [piece] + [
        lax.ppermute(piece, axis, xor_pairs(axis, shift))
        for shift in range(1, lax.axis_size(axis))
    ]


def exchange(first, second, capacity):
    def relay(parcels, out_axis, in_axis):
        arrived = [parcels[0]] + [
            lax.ppermute(parcel, out_axis, xor_pairs(out_axis, shift))
            for shift, parcel in enumerate(parcels)
            if shift
        ]
        steps = lax.axis_size(in_axis)
        shape = (len(arrived) * capacity, parcels[0].shape[1])
        mixed = pl.pallas_call(
            functools.partial(mix_kernel, len(arrived), capacity),
            out_shape=[jax.ShapeDtypeStruct(shape, jnp.bfloat16)] * (steps - 1),
            in_specs=[whole_ref()] * len(arrived),
            out_specs=[whole_ref()] * (steps - 1),
            compiler_params=params(4 * steps * shape[0] * shape[1]),
            cost_estimate=cost(0, 4 * steps * shape[0] * shape[1]),
            name="mix",
        )(*arrived)
        return arrived + [
            lax.ppermute(parcel, in_axis, xor_pairs(in_axis, shift))
            for shift, parcel in enumerate(mixed, 1)
        ]

    return relay(first, "col", "row"), relay(second, "row", "col")


def after(value, *earlier):
    return lax.optimization_barrier((value, earlier))[0]


def gather_line(piece):
    count = lax.axis_size("col")
    pieces = {0: piece}
    step = count // 2
    while step:
        pieces |= {
            shift + step: lax.ppermute(held, "col", xor_pairs("col", step))
            for shift, held in pieces.items()
        }
        step //= 2
    return [pieces[shift] for shift in range(count)]


def swap(piece):
    return lax.ppermute(piece, "layer", xor_pairs("layer", 1))


def on_device(tasks, task_owner, task_slot, p_pattern, c_pattern, occupations):
    n_row, n_col, layers = (lax.axis_size(axis) for axis in ("row", "col", "layer"))
    owners = n_row * n_col
    count = tasks.shape[0]
    capacity = max(2, 2 * count // owners)
    places = owners * capacity
    block_rows, block_cols = p_pattern.shape
    part_rows = BLK // layers
    part = part_rows * BLK
    rows, cols = block_rows * part_rows, block_cols * BLK
    width = part + LANES
    layer = lax.axis_index("layer")

    paired = capacity % 16 == 0
    if paired:
        parcels = [(n_row * capacity, part // 2 + LANES)] * n_col
        parcels += [(n_col * capacity, part - part // 2)] * n_row
    else:
        parcels = [(places, width)]
    sent = pl.pallas_call(
        functools.partial(pack_kernel, owners, capacity, p_pattern.shape, paired),
        out_shape=[jax.ShapeDtypeStruct(shape, jnp.bfloat16) for shape in parcels],
        in_specs=[pl.BlockSpec(memory_space=pltpu.HBM), whole_ref(), whole_ref()],
        out_specs=[whole_ref()] * len(parcels),
        scratch_shapes=[pltpu.VMEM((count, part), jnp.bfloat16), pltpu.SemaphoreType.DMA],
        compiler_params=params(2 * (places + count) * width),
        cost_estimate=cost(2 * places * count * width, 2 * (places + count) * width),
        name="pack",
    )(tasks, task_owner.reshape(1, count), task_slot.reshape(1, count))
    if paired:
        got = list(exchange(sent[:n_col], sent[n_col:], capacity))
    else:
        got = [
            [
                lax.all_to_all(
                    sent[0].reshape(owners, capacity, width),
                    ("row", "col"),
                    split_axis=0,
                    concat_axis=0,
                    tiled=True,
                ).reshape(places, width)
            ]
        ] * 2

    slots_here = block_rows * block_cols
    pattern_row = p_pattern.astype(jnp.float32).T.reshape(1, slots_here)
    marks = jnp.pad(pattern_row, ((0, 0), (0, LANES - slots_here)))
    half_rows = part_rows // 2
    occ_here = lax.dynamic_index_in_dim(
        occupations.reshape(block_rows, layers, 2, half_rows), layer, 1, keepdims=False
    )
    half_shape = jax.ShapeDtypeStruct((block_rows, half_rows, cols), jnp.bfloat16)
    density_shape = jax.ShapeDtypeStruct((block_rows, part_rows, cols), jnp.bfloat16)
    marks_shape = jax.ShapeDtypeStruct((slots_here, places), jnp.bfloat16)

    def build(half, marks, *blocks):
        return pl.pallas_call(
            functools.partial(build_kernel, half, paired),
            out_shape=[density_shape] if half else [marks_shape, half_shape],
            in_specs=[whole_ref()] * (2 + len(blocks)),
            out_specs=[whole_ref()] * (1 if half else 2),
            scratch_shapes=[pltpu.VMEM((cols // LANES, rows // 2, LANES), jnp.float32)],
            compiler_params=params(2 * places * width + 6 * rows * cols),
            cost_estimate=cost(places * slots_here * part, places * width),
            name="build",
        )(occ_here[:, half].reshape(rows // 2, 1), marks, *blocks)

    marks, first_half = build(0, marks, *got[0])
    (density,) = build(1, marks, *got[1], first_half)

    lefts = gather_line(density)
    mate = swap(density)
    pieces = gather(after(density, mate), "row")
    pieces[0] = density
    mates = [mate] + [swap(piece) for piece in pieces[1:]]
    flops = 2 * rows * cols * n_col * cols
    panel_shape = (n_row, block_rows, layers, part_rows, cols)
    here = block_rows // layers
    held = 2 * ((n_col + 3) * rows * cols + 2 * n_row * rows * cols) + 8 * rows * cols
    half = jax.ShapeDtypeStruct((n_col, here, part_rows, cols), jnp.bfloat16)
    square, keep, give = pl.pallas_call(
        functools.partial(square_kernel, n_col, n_row),
        out_shape=[jax.ShapeDtypeStruct(density.shape, jnp.bfloat16), half, half],
        in_specs=[any_ref()] * (n_col + 2 * n_row),
        out_specs=[whole_ref(), any_ref(), any_ref()],
        scratch_shapes=[
            pltpu.VMEM((n_col, block_rows, part_rows, cols), jnp.bfloat16),
            pltpu.VMEM(panel_shape, jnp.bfloat16),
            pltpu.SemaphoreType.DMA((n_col + 2 * n_row,)),
        ],
        compiler_params=params(held),
        cost_estimate=cost(flops, 8 * 1024 * 1024),
        name="square",
    )(*lefts, *pieces, *mates)

    pieces = gather(square, "row")
    mates = [swap(piece) for piece in pieces]
    received = swap(after(give, mates[0]))
    return pl.pallas_call(
        functools.partial(cube_kernel, n_row),
        out_shape=jax.ShapeDtypeStruct((rows, cols), jnp.float32),
        in_specs=[any_ref()] * 2 + [whole_ref()] + [any_ref()] * (2 * n_row),
        out_specs=whole_ref(),
        scratch_shapes=[
            pltpu.VMEM((n_col, here, layers, part_rows, cols), jnp.bfloat16),
            pltpu.VMEM(panel_shape, jnp.bfloat16),
            pltpu.SemaphoreType.DMA((2 + 2 * n_row,)),
        ],
        compiler_params=params(held),
        cost_estimate=cost(flops, 8 * 1024 * 1024),
        name="cube",
    )(keep, received, c_pattern, *pieces, *mates)


def solution(mesh):
    return jax.shard_map(
        on_device,
        mesh=mesh,
        in_specs=(
            P(("row", "col"), None),
            P(("row", "col"), None),
            P(("row", "col")),
            P("row", "col"),
            P("row", "col"),
            P("row"),
        ),
        out_specs=P(("row", "layer"), "col"),
        check_vma=False,
    )
```

```python
import functools

import jax
import jax.numpy as jnp
from jax import lax
from jax.experimental import pallas as pl
from jax.experimental.pallas import tpu as pltpu
from jax.sharding import PartitionSpec as P

BLK = 64
LANES = 128


def params(held):
    return pltpu.CompilerParams(vmem_limit_bytes=held + 6 * 1024 * 1024)


def whole_ref():
    return pl.BlockSpec(memory_space=pltpu.VMEM)


def any_ref():
    return pl.BlockSpec(memory_space=pl.ANY)


def cost(flops, bytes_accessed):
    return pl.CostEstimate(flops=flops, bytes_accessed=bytes_accessed, transcendentals=0)


def pack_kernel(owners, capacity, block_shape, paired, tasks_ref, owner_ref, slot_ref, *refs):
    out_refs, held, sem = refs[:-2], refs[-2], refs[-1]
    count, part = held.shape
    layer = lax.axis_index("layer")
    start = pl.multiple_of(layer * part, part)
    copy = pltpu.make_async_copy(tasks_ref.at[:, pl.ds(start, part)], held, sem)
    copy.start()
    block_rows, block_cols = block_shape
    slot_row = slot_ref[...]
    slot_row = lax.rem(slot_row, block_cols) * block_rows + lax.div(slot_row, block_cols)
    across = lax.broadcasted_iota(jnp.int32, (count, count), 1)
    down = lax.broadcasted_iota(jnp.int32, (count, count), 0)
    slot_col = jnp.sum(
        jnp.where(across == down, slot_row.astype(jnp.float32), 0.0), axis=1, keepdims=True
    )
    owner_row = owner_ref[...]
    if paired:
        owner_row = owner_row ^ (
            lax.axis_index("row") * lax.axis_size("col") + lax.axis_index("col")
        )
    same = (lax.broadcasted_iota(jnp.int32, (owners, count), 0) == owner_row).astype(jnp.float32)
    before = (down < across).astype(jnp.float32).astype(jnp.bfloat16)
    ahead = jnp.dot(same.astype(jnp.bfloat16), before, preferred_element_type=jnp.float32)
    placed = jnp.sum(ahead * same, axis=0, keepdims=True).astype(jnp.int32)
    target = owner_row * capacity + placed
    places = owners * capacity
    move = (
        (lax.broadcasted_iota(jnp.int32, (places, count), 0) == target)
        .astype(jnp.float32)
        .astype(jnp.bfloat16)
    )

    def put(at, end, blocks):
        moved = jnp.dot(move, blocks, preferred_element_type=jnp.float32).astype(jnp.bfloat16)
        if not paired:
            out_refs[0][:, at:end] = moved
            return
        n_row, n_col = lax.axis_size("row"), lax.axis_size("col")
        if at < part // 2 + LANES:
            for over, out_ref in enumerate(out_refs[:n_col]):
                for down in range(n_row):
                    place = (down * n_col + over) * capacity
                    out_ref[down * capacity : (down + 1) * capacity, at:end] = moved[
                        place : place + capacity
                    ]
            return
        at, end = at - (part // 2 + LANES), end - (part // 2 + LANES)
        each = n_col * capacity
        for down, out_ref in enumerate(out_refs[n_col:]):
            out_ref[:, at:end] = moved[down * each : (down + 1) * each]

    slots = jnp.broadcast_to(slot_col, (count, LANES)).astype(jnp.bfloat16)
    put(0, LANES, slots)
    copy.wait()
    step = 512
    for at in range(0, part, step):
        put(LANES + at, LANES + at + step, held[:, at : at + step])


def mix_kernel(arrivals, capacity, *refs):
    for shift, out_ref in enumerate(refs[arrivals:], 1):
        for index, ref in enumerate(refs[:arrivals]):
            out_ref[index * capacity : (index + 1) * capacity, :] = ref[
                shift * capacity : (shift + 1) * capacity, :
            ]


def merge_kernel(*refs):
    out_ref = refs[-1]
    for index, ref in enumerate(refs[:-1]):
        out_ref[index] = ref[...]


def build_kernel(half, paired, occ_ref, marks_ref, *refs):
    block_rows, part_rows, cols = refs[-2].shape
    block_cols = cols // BLK
    rows = block_rows * part_rows
    part = part_rows * BLK
    out_ref, tall = refs[-2:]
    got_refs = refs[:-2]
    front = 0
    if half:
        got_refs, first_ref, all_ref = refs[:-4], refs[-4], refs[-3]
        all_ref[:, :part_rows] = first_ref[...]
    else:
        got_refs, held_ref = refs[:-3], refs[-3]
        front = LANES

    def got(at, end):
        if not paired:
            skip = half * (LANES + part)
            return got_refs[0][:, skip + at : skip + end]
        n_row, n_col = lax.axis_size("row"), lax.axis_size("col")
        if not half:
            capacity = got_refs[0].shape[0] // n_row
            parts = [ref[:capacity, at:end] for ref in got_refs[:n_col]]
            parts += [ref[:, at:end] for ref in got_refs[n_col:]]
        else:
            capacity = got_refs[0].shape[0] // n_col
            parts = []
            for down in range(n_row):
                place = slice(down * capacity, (down + 1) * capacity)
                parts.append(got_refs[down][:capacity, at:end])
                parts += [ref[place, at:end] for ref in got_refs[n_row:]]
        return jnp.concatenate(parts, axis=0)

    if half:
        marks = marks_ref[...]
    else:
        slots = got(0, LANES).astype(jnp.float32)
        lane = lax.broadcasted_iota(jnp.int32, slots.shape, 1).astype(jnp.float32)
        marks = jnp.where(slots == lane, marks_ref[...], 0.0)
        marks = marks.T[: block_rows * block_cols].astype(jnp.bfloat16)
        held_ref[...] = marks
    low = lax.broadcasted_iota(jnp.int32, (block_rows, LANES), 1) < BLK
    step = 256
    for at in range(0, part, step):
        summed = jnp.dot(
            marks, got(front + at, front + at + step), preferred_element_type=jnp.float32
        )
        for pair in range(step // LANES):
            lanes = slice(pair * LANES, (pair + 1) * LANES)
            row = (at // LANES + pair) * 2
            for twin in range(block_cols // 2):
                left = summed[twin * 2 * block_rows : (twin * 2 + 1) * block_rows, lanes]
                right = summed[(twin * 2 + 1) * block_rows : (twin * 2 + 2) * block_rows, lanes]
                tall[twin, pl.ds(row, block_rows, stride=part_rows), :] = jnp.where(
                    low, left, pltpu.roll(right, BLK, 1)
                )
                tall[twin, pl.ds(row + 1, block_rows, stride=part_rows), :] = jnp.where(
                    low, pltpu.roll(left, BLK, 1), right
                )
    row_start = lax.axis_index("row") * (block_rows * BLK)
    row_start += (lax.axis_index("layer") * 2 + half) * part_rows
    col_start = lax.axis_index("col") * cols
    index = lax.broadcasted_iota(jnp.int32, (rows, LANES), 0)
    row_id = row_start + lax.div(index, part_rows) * BLK + lax.rem(index, part_rows)
    col_id = col_start + lax.broadcasted_iota(jnp.int32, (rows, LANES), 1)
    occ = occ_ref[...]
    for twin in range(block_cols // 2):
        diagonal = jnp.where(row_id == col_id + twin * LANES, occ, 0.0)
        lanes = slice(twin * LANES, (twin + 1) * LANES)
        density = (tall[twin] + diagonal).astype(jnp.bfloat16)
        density = density.reshape(block_rows, part_rows, LANES)
        out_ref[:, :, lanes] = density
        if half:
            all_ref[:, part_rows:, lanes] = density


def load_panel(place, pieces, mates):
    me = lax.axis_index("row")
    layer = lax.axis_index("layer")
    pairs = []
    for shift, (piece, mate) in enumerate(zip(pieces, mates)):
        pairs += [(piece, place(me ^ shift, layer)), (mate, place(me ^ shift, 1 - layer))]
    return pairs


def start_copies(pairs, sems):
    copies = [
        pltpu.make_async_copy(source, target, sems.at[index])
        for index, (source, target) in enumerate(pairs)
    ]
    for copy in copies:
        copy.start()
    return copies


def product(left, panel):
    blocks = left.shape[0]
    per_block = panel.shape[0] // blocks
    cols = panel.shape[-1]

    def term(block):
        a = left[block].reshape(-1, left.shape[-1])
        b = panel[pl.ds(block * per_block, per_block)].reshape(-1, cols)
        return jnp.dot(a, b, preferred_element_type=jnp.float32)

    total = term(0)
    if blocks <= 4:
        for block in range(1, blocks):
            total = total + term(block)
        return total
    return lax.fori_loop(1, blocks, lambda block, sofar: sofar + term(block), total)


def square_kernel(half, n_col, n_row, *refs):
    pieces, mates = refs[:n_row], refs[n_row : 2 * n_row]
    lefts = refs[2 * n_row : n_col + 2 * n_row]
    low_ref, keep_ref, give_ref, left, panel, sems = refs[n_col + 2 * n_row :]
    col = lax.axis_index("col")
    layer = lax.axis_index("layer")
    part_rows = left.shape[2]
    lefts = list(lefts)
    lefts[1] = lefts[1].at[:, pl.ds(half * part_rows, part_rows)]
    pairs = [(piece, left.at[col ^ shift]) for shift, piece in enumerate(lefts)]
    pairs += load_panel(lambda block, which: panel.at[block, :, which], pieces, mates)
    for copy in start_copies(pairs, sems):
        copy.wait()
    here = keep_ref.shape[1]
    out = start_copies(
        [
            (left.at[:, pl.ds(layer * here, here)], keep_ref),
            (left.at[:, pl.ds((1 - layer) * here, here)], give_ref),
        ],
        sems,
    )
    low_ref[...] = product(left, panel).reshape(low_ref.shape).astype(jnp.bfloat16)
    for copy in out:
        copy.wait()


def cube_kernel(n_row, *refs):
    keeps, gots, pattern_ref, merged, mate = refs[:2], refs[2:4], refs[4], refs[5], refs[6]
    pieces, mates = refs[7 : 7 + n_row], refs[7 + n_row : 7 + 2 * n_row]
    out_ref, left, panel, sems = refs[7 + 2 * n_row :]
    row = lax.axis_index("row")
    layer = lax.axis_index("layer")
    pairs = []
    for half in range(2):
        pairs += [
            (keeps[half], left.at[:, :, layer, half]),
            (gots[half], left.at[:, :, 1 - layer, half]),
        ]
    pairs += load_panel(
        lambda block, which: panel.at[block, :, which, 0],
        [merged.at[shift] for shift in range(n_row)],
        [mate.at[shift] for shift in range(n_row)],
    )
    pairs += load_panel(lambda block, which: panel.at[block, :, which, 1], pieces, mates)
    copies = start_copies(pairs, sems)
    rows, cols = out_ref.shape
    pattern = pattern_ref[...].astype(jnp.float32).astype(jnp.bfloat16)
    block_rows, block_cols = pattern.shape
    across = lax.broadcasted_iota(jnp.int32, (block_cols, cols), 1)
    which = lax.broadcasted_iota(jnp.int32, (block_cols, cols), 0)
    wide = (lax.div(across, BLK) == which).astype(jnp.float32).astype(jnp.bfloat16)
    down = lax.broadcasted_iota(jnp.int32, (rows, block_rows), 0) + layer * rows
    which = lax.broadcasted_iota(jnp.int32, (rows, block_rows), 1)
    tall = (lax.div(down, BLK) == which).astype(jnp.float32).astype(jnp.bfloat16)
    mask = jnp.dot(
        jnp.dot(tall, pattern, preferred_element_type=jnp.float32).astype(jnp.bfloat16),
        wide,
        preferred_element_type=jnp.float32,
    )
    for copy in copies:
        copy.wait()
    here = left.shape[1]
    square = panel[row, pl.ds(layer * here, here)].reshape(rows, cols).astype(jnp.float32)
    out_ref[...] = mask * (3.0 * square - 2.0 * product(left, panel))


def xor_pairs(axis, shift):
    return [(i, i ^ shift) for i in range(lax.axis_size(axis))]


def gather(piece, axis):
    return [piece] + [
        lax.ppermute(piece, axis, xor_pairs(axis, shift))
        for shift in range(1, lax.axis_size(axis))
    ]


def exchange(first, second, capacity):
    def relay(parcels, out_axis, in_axis):
        arrived = [parcels[0]] + [
            lax.ppermute(parcel, out_axis, xor_pairs(out_axis, shift))
            for shift, parcel in enumerate(parcels)
            if shift
        ]
        steps = lax.axis_size(in_axis)
        shape = (len(arrived) * capacity, parcels[0].shape[1])
        mixed = pl.pallas_call(
            functools.partial(mix_kernel, len(arrived), capacity),
            out_shape=[jax.ShapeDtypeStruct(shape, jnp.bfloat16)] * (steps - 1),
            in_specs=[whole_ref()] * len(arrived),
            out_specs=[whole_ref()] * (steps - 1),
            compiler_params=params(4 * steps * shape[0] * shape[1]),
            cost_estimate=cost(0, 4 * steps * shape[0] * shape[1]),
            name="mix",
        )(*arrived)
        return arrived + [
            lax.ppermute(parcel, in_axis, xor_pairs(in_axis, shift))
            for shift, parcel in enumerate(mixed, 1)
        ]

    return relay(first, "col", "row"), relay(second, "row", "col")


def after(value, *earlier):
    return lax.optimization_barrier((value, earlier))[0]


def merge(pieces):
    shape = (len(pieces), *pieces[0].shape)
    return pl.pallas_call(
        merge_kernel,
        out_shape=jax.ShapeDtypeStruct(shape, pieces[0].dtype),
        in_specs=[whole_ref()] * len(pieces),
        out_specs=whole_ref(),
        compiler_params=params(4 * len(pieces) * pieces[0].size),
        cost_estimate=cost(0, 4 * len(pieces) * pieces[0].size),
        name="merge",
    )(*pieces)


def gather_line(piece, near):
    count = lax.axis_size("col")
    pieces = {0: piece}
    step = count // 2
    while step:
        pieces |= {
            shift + step: lax.ppermute(held, "col", xor_pairs("col", step))
            if shift + step > 1
            else near
            for shift, held in pieces.items()
        }
        step //= 2
    return [pieces[shift] for shift in range(count)]


def swap(piece):
    return lax.ppermute(piece, "layer", xor_pairs("layer", 1))


def on_device(tasks, task_owner, task_slot, p_pattern, c_pattern, occupations):
    n_row, n_col, layers = (lax.axis_size(axis) for axis in ("row", "col", "layer"))
    owners = n_row * n_col
    count = tasks.shape[0]
    capacity = max(2, 2 * count // owners)
    places = owners * capacity
    block_rows, block_cols = p_pattern.shape
    part_rows = BLK // layers
    part = part_rows * BLK
    rows, cols = block_rows * part_rows, block_cols * BLK
    width = part + LANES
    layer = lax.axis_index("layer")

    paired = capacity % 16 == 0
    if paired:
        parcels = [(n_row * capacity, part // 2 + LANES)] * n_col
        parcels += [(n_col * capacity, part - part // 2)] * n_row
    else:
        parcels = [(places, width)]
    sent = pl.pallas_call(
        functools.partial(pack_kernel, owners, capacity, p_pattern.shape, paired),
        out_shape=[jax.ShapeDtypeStruct(shape, jnp.bfloat16) for shape in parcels],
        in_specs=[pl.BlockSpec(memory_space=pltpu.HBM), whole_ref(), whole_ref()],
        out_specs=[whole_ref()] * len(parcels),
        scratch_shapes=[pltpu.VMEM((count, part), jnp.bfloat16), pltpu.SemaphoreType.DMA],
        compiler_params=params(2 * (places + count) * width),
        cost_estimate=cost(2 * places * count * width, 2 * (places + count) * width),
        name="pack",
    )(tasks, task_owner.reshape(1, count), task_slot.reshape(1, count))
    if paired:
        got = list(exchange(sent[:n_col], sent[n_col:], capacity))
    else:
        got = [
            [
                lax.all_to_all(
                    sent[0].reshape(owners, capacity, width),
                    ("row", "col"),
                    split_axis=0,
                    concat_axis=0,
                    tiled=True,
                ).reshape(places, width)
            ]
        ] * 2

    slots_here = block_rows * block_cols
    pattern_row = p_pattern.astype(jnp.float32).T.reshape(1, slots_here)
    marks = jnp.pad(pattern_row, ((0, 0), (0, LANES - slots_here)))
    half_rows = part_rows // 2
    occ_here = lax.dynamic_index_in_dim(
        occupations.reshape(block_rows, layers, 2, half_rows), layer, 1, keepdims=False
    )
    half_shape = jax.ShapeDtypeStruct((block_rows, half_rows, cols), jnp.bfloat16)
    density_shape = jax.ShapeDtypeStruct((block_rows, part_rows, cols), jnp.bfloat16)
    marks_shape = jax.ShapeDtypeStruct((slots_here, places), jnp.bfloat16)

    def build(half, marks, *blocks):
        return pl.pallas_call(
            functools.partial(build_kernel, half, paired),
            out_shape=[density_shape if half else marks_shape, half_shape],
            in_specs=[whole_ref()] * (2 + len(blocks)),
            out_specs=[whole_ref()] * 2,
            scratch_shapes=[pltpu.VMEM((cols // LANES, rows // 2, LANES), jnp.float32)],
            compiler_params=params(2 * places * width + 6 * rows * cols),
            cost_estimate=cost(places * slots_here * part, places * width),
            name="build",
        )(occ_here[:, half].reshape(rows // 2, 1), marks, *blocks)

    marks, first_half = build(0, marks, *got[0])
    density, second_half = build(1, marks, *got[1], first_half)

    near = lax.ppermute(density, "col", xor_pairs("col", 1))
    lines = [gather_line(first_half, near), gather_line(second_half, near)]
    far = n_col // 2
    mate = swap(density)
    pieces = gather(after(density, mate), "row")
    pieces[0] = density
    mates = {0: mate}
    mates |= {shift: swap(after(pieces[shift], near)) for shift in range(3, n_row)}
    mates[2] = swap(after(pieces[2], lines[1][far]))
    mates[1] = swap(after(pieces[1], lines[0][-1], mates[2], mates[n_row - 1]))
    mates = [mates[shift] for shift in range(n_row)]
    flops = 2 * rows * cols * n_col * cols
    here = block_rows // layers
    held = 2 * ((n_col + 3) * rows * cols + 2 * n_row * rows * cols) + 8 * rows * cols
    share = jax.ShapeDtypeStruct((n_col, here, half_rows, cols), jnp.bfloat16)

    def square(half):
        return pl.pallas_call(
            functools.partial(square_kernel, half, n_col, n_row),
            out_shape=[half_shape, share, share],
            in_specs=[any_ref()] * (n_col + 2 * n_row),
            out_specs=[whole_ref(), any_ref(), any_ref()],
            scratch_shapes=[
                pltpu.VMEM((n_col, block_rows, half_rows, cols), jnp.bfloat16),
                pltpu.VMEM((n_row, block_rows, layers, part_rows, cols), jnp.bfloat16),
                pltpu.SemaphoreType.DMA((n_col + 2 * n_row,)),
            ],
            compiler_params=params(held),
            cost_estimate=cost(flops // 2, 8 * 1024 * 1024),
            name="square",
        )(*pieces, *mates, *lines[half])

    low, keep, give = zip(square(0))
    earlier = gather(low[0], "row")
    lines[1] = after(lines[1], earlier[-1])
    low, keep, give = zip((low[0], keep[0], give[0]), square(1))
    merged = merge(after(earlier, low[1]))
    other = swap(merged)
    later = gather(low[1], "row")
    later_mates = [swap(piece) for piece in later]
    received = [swap(after(give[0], other)), swap(after(give[1], later_mates[0]))]
    return pl.pallas_call(
        functools.partial(cube_kernel, n_row),
        out_shape=jax.ShapeDtypeStruct((rows, cols), jnp.float32),
        in_specs=[any_ref()] * 4 + [whole_ref()] + [any_ref()] * (2 + 2 * n_row),
        out_specs=whole_ref(),
        scratch_shapes=[
            pltpu.VMEM((n_col, here, layers, 2, half_rows, cols), jnp.bfloat16),
            pltpu.VMEM((n_row, block_rows, layers, 2, half_rows, cols), jnp.bfloat16),
            pltpu.SemaphoreType.DMA((4 + 4 * n_row,)),
        ],
        compiler_params=params(held),
        cost_estimate=cost(flops, 8 * 1024 * 1024),
        name="cube",
    )(*keep, *received, c_pattern, merged, other, *later, *later_mates)


def solution(mesh):
    return jax.shard_map(
        on_device,
        mesh=mesh,
        in_specs=(
            P(("row", "col"), None),
            P(("row", "col"), None),
            P(("row", "col")),
            P("row", "col"),
            P("row", "col"),
            P("row"),
        ),
        out_specs=P(("row", "layer"), "col"),
        check_vma=False,
    )
```

```python
import functools

import jax
import jax.numpy as jnp
from jax import lax
from jax.experimental import pallas as pl
from jax.experimental.pallas import tpu as pltpu
from jax.sharding import PartitionSpec as P

BLK = 64
LANES = 128
WEIGHT = 10**9


def params(held):
    return pltpu.CompilerParams(vmem_limit_bytes=held + 6 * 1024 * 1024)


def whole_ref():
    return pl.BlockSpec(memory_space=pltpu.VMEM)


def any_ref():
    return pl.BlockSpec(memory_space=pl.ANY)


def cost(flops, bytes_accessed):
    return pl.CostEstimate(flops=flops, bytes_accessed=bytes_accessed, transcendentals=0)


def pack_kernel(owners, capacity, block_shape, paired, tasks_ref, owner_ref, slot_ref, *refs):
    out_refs, held, sem = refs[:-2], refs[-2], refs[-1]
    count, part = held.shape
    layer = lax.axis_index("layer")
    start = pl.multiple_of(layer * part, part)
    copy = pltpu.make_async_copy(tasks_ref.at[:, pl.ds(start, part)], held, sem)
    copy.start()
    block_rows, block_cols = block_shape
    slot_row = slot_ref[...]
    slot_row = lax.rem(slot_row, block_cols) * block_rows + lax.div(slot_row, block_cols)
    across = lax.broadcasted_iota(jnp.int32, (count, count), 1)
    down = lax.broadcasted_iota(jnp.int32, (count, count), 0)
    slot_col = jnp.sum(
        jnp.where(across == down, slot_row.astype(jnp.float32), 0.0), axis=1, keepdims=True
    )
    owner_row = owner_ref[...]
    if paired:
        owner_row = owner_row ^ (
            lax.axis_index("row") * lax.axis_size("col") + lax.axis_index("col")
        )
    same = (lax.broadcasted_iota(jnp.int32, (owners, count), 0) == owner_row).astype(jnp.float32)
    before = (down < across).astype(jnp.float32).astype(jnp.bfloat16)
    ahead = jnp.dot(same.astype(jnp.bfloat16), before, preferred_element_type=jnp.float32)
    placed = jnp.sum(ahead * same, axis=0, keepdims=True).astype(jnp.int32)
    target = owner_row * capacity + placed
    places = owners * capacity
    move = (
        (lax.broadcasted_iota(jnp.int32, (places, count), 0) == target)
        .astype(jnp.float32)
        .astype(jnp.bfloat16)
    )

    def put(at, end, blocks):
        moved = jnp.dot(move, blocks, preferred_element_type=jnp.float32).astype(jnp.bfloat16)
        if not paired:
            out_refs[0][:, at:end] = moved
            return
        n_row, n_col = lax.axis_size("row"), lax.axis_size("col")
        if at < part // 2 + LANES:
            for over, out_ref in enumerate(out_refs[:n_col]):
                for down in range(n_row):
                    place = (down * n_col + over) * capacity
                    out_ref[down * capacity : (down + 1) * capacity, at:end] = moved[
                        place : place + capacity
                    ]
            return
        at, end = at - (part // 2 + LANES), end - (part // 2 + LANES)
        each = n_col * capacity
        for down, out_ref in enumerate(out_refs[n_col:]):
            out_ref[:, at:end] = moved[down * each : (down + 1) * each]

    slots = jnp.broadcast_to(slot_col, (count, LANES)).astype(jnp.bfloat16)
    put(0, LANES, slots)
    copy.wait()
    step = 512
    for at in range(0, part, step):
        put(LANES + at, LANES + at + step, held[:, at : at + step])


def mix_kernel(arrivals, capacity, *refs):
    for shift, out_ref in enumerate(refs[arrivals:], 1):
        for index, ref in enumerate(refs[:arrivals]):
            out_ref[index * capacity : (index + 1) * capacity, :] = ref[
                shift * capacity : (shift + 1) * capacity, :
            ]


def build_kernel(half, paired, occ_ref, marks_ref, *refs):
    out_ref, sorted_ref, tall = refs[-3:]
    layers = lax.axis_size("layer")
    block_rows, cols = out_ref.shape[0], out_ref.shape[2]
    part_rows = BLK // layers // 2
    block_cols = cols // BLK
    rows = block_rows * part_rows
    part = part_rows * BLK
    front = 0
    if half:
        got_refs, before = refs[:-5], refs[-5:-3]
        for ref, old_ref in zip((out_ref, sorted_ref), before):
            ref[:, :part_rows] = old_ref[...]
    else:
        got_refs, held_ref = refs[:-4], refs[-4]
        front = LANES

    def got(at, end):
        if not paired:
            skip = half * (LANES + part)
            return got_refs[0][:, skip + at : skip + end]
        n_row, n_col = lax.axis_size("row"), lax.axis_size("col")
        if not half:
            capacity = got_refs[0].shape[0] // n_row
            parts = [ref[:capacity, at:end] for ref in got_refs[:n_col]]
            parts += [ref[:, at:end] for ref in got_refs[n_col:]]
        else:
            capacity = got_refs[0].shape[0] // n_col
            parts = []
            for down in range(n_row):
                place = slice(down * capacity, (down + 1) * capacity)
                parts.append(got_refs[down][:capacity, at:end])
                parts += [ref[place, at:end] for ref in got_refs[n_row:]]
        return jnp.concatenate(parts, axis=0)

    if half:
        marks = marks_ref[...]
    else:
        slots = got(0, LANES).astype(jnp.float32)
        lane = lax.broadcasted_iota(jnp.int32, slots.shape, 1).astype(jnp.float32)
        which = lax.broadcasted_iota(jnp.int32, (block_cols, LANES), 1)
        spread = lax.div(which, block_rows) == lax.broadcasted_iota(jnp.int32, which.shape, 0)
        which = lax.broadcasted_iota(jnp.int32, (block_rows, LANES), 1)
        here = lax.rem(which, block_rows) == lax.broadcasted_iota(jnp.int32, which.shape, 0)
        pattern = jnp.dot(
            marks_ref[...].astype(jnp.float32),
            spread.astype(jnp.float32),
            preferred_element_type=jnp.float32,
        )
        pattern = jnp.sum(jnp.where(here, pattern, 0.0), axis=0, keepdims=True)
        marks = jnp.where(slots == lane, pattern, 0.0)
        marks = marks.T[: block_rows * block_cols].astype(jnp.bfloat16)
        held_ref[...] = marks
    low = lax.broadcasted_iota(jnp.int32, (block_rows, LANES), 1) < BLK
    step = 256
    for at in range(0, part, step):
        summed = jnp.dot(
            marks, got(front + at, front + at + step), preferred_element_type=jnp.float32
        )
        for pair in range(step // LANES):
            lanes = slice(pair * LANES, (pair + 1) * LANES)
            row = (at // LANES + pair) * 2
            for twin in range(block_cols // 2):
                left = summed[twin * 2 * block_rows : (twin * 2 + 1) * block_rows, lanes]
                right = summed[(twin * 2 + 1) * block_rows : (twin * 2 + 2) * block_rows, lanes]
                tall[twin, pl.ds(row, block_rows, stride=part_rows), :] = jnp.where(
                    low, left, pltpu.roll(right, BLK, 1)
                )
                tall[twin, pl.ds(row + 1, block_rows, stride=part_rows), :] = jnp.where(
                    low, pltpu.roll(left, BLK, 1), right
                )
    tile_rows = block_rows * BLK
    row_here = (lax.axis_index("layer") * 2 + half) * part_rows
    row_start = lax.axis_index("row") * tile_rows + row_here
    col_start = lax.axis_index("col") * cols
    index = lax.broadcasted_iota(jnp.int32, (rows, LANES), 0)
    inside = lax.div(index, part_rows) * BLK + lax.rem(index, part_rows)
    row_id = row_start + inside
    lane = lax.broadcasted_iota(jnp.int32, (rows, LANES), 1)
    occ = jnp.zeros((rows, 1), jnp.float32)
    for at in range(0, tile_rows, LANES):
        mine = jnp.where(row_here + inside == at + lane, occ_ref[:, at : at + LANES], 0.0)
        occ = occ + jnp.sum(mine, axis=1, keepdims=True)
    values = []
    for twin in range(block_cols // 2):
        diagonal = jnp.where(row_id == col_start + twin * LANES + lane, occ, 0.0)
        values.append(tall[twin] + diagonal)
    here = slice(half * part_rows, (half + 1) * part_rows)

    def put(ref, at, value):
        ref[:, here, at : at + LANES] = value.astype(jnp.bfloat16).reshape(
            block_rows, part_rows, LANES
        )

    for twin, value in enumerate(values):
        put(out_ref, twin * LANES, value)
    quarter = LANES // 4
    spot = lax.div(lane, quarter)
    for twin in range(0, block_cols // 2, 2):
        first, second = values[twin], values[twin + 1]
        at = twin // (block_rows // 2) * tile_rows + twin % (block_rows // 2) // 2 * LANES
        back, ahead = pltpu.roll(first, 3 * quarter, 1), pltpu.roll(second, quarter, 1)
        far_back, far_ahead = pltpu.roll(first, 2 * quarter, 1), pltpu.roll(second, 2 * quarter, 1)
        put(
            sorted_ref,
            at,
            jnp.where(
                spot == 0, first, jnp.where(spot == 1, back, jnp.where(spot == 2, far_ahead, ahead))
            ),
        )
        put(
            sorted_ref,
            at + tile_rows // 2,
            jnp.where(
                spot == 0, back, jnp.where(spot == 1, far_back, jnp.where(spot == 2, ahead, second))
            ),
        )


def start_copies(pairs, sems):
    copies = [
        pltpu.make_async_copy(source, target, sems.at[index])
        for index, (source, target) in enumerate(pairs)
    ]
    for copy in copies:
        copy.start()
    return copies


def left_blocks(tile_rows, cols):
    width = tile_rows // 2
    return [
        (at // tile_rows, at % tile_rows // width, slice(at, at + width))
        for at in range(0, cols, width)
    ]


def flat(value):
    return value.reshape(-1, value.shape[-1])


def near_square_kernel(n_col, n_row, *refs):
    lefts, pieces = refs[: n_col - 1], refs[n_col - 1 : n_col - 1 + n_row]
    sum_ref, other_ref, met_ref, left, sems = refs[n_col - 1 + n_row :]
    row, col, layer = (lax.axis_index(axis) for axis in ("row", "col", "layer"))
    cols = sum_ref.shape[1]
    per_col = n_row // n_col
    copies = start_copies(
        [
            (piece.at[:, :, lanes], left.at[(col ^ shift) * per_col + block, which])
            for shift, piece in enumerate(lefts)
            for block, which, lanes in left_blocks(cols // per_col, cols)
        ],
        sems,
    )
    last = col ^ (n_col - 1)
    for block in range(per_col):
        left[last * per_col + block] = jnp.zeros(left.shape[1:], left.dtype)
    for shift in range(n_row):

        @pl.when(lax.div(row ^ shift, per_col) == last)
        def _(shift=shift):
            met_ref[lax.rem(row ^ shift, per_col)] = flat(pieces[shift][...])

    for copy in copies:
        copy.wait()
    total = jnp.zeros(sum_ref.shape, jnp.float32)
    for shift in range(n_row):
        total = total + jnp.dot(
            flat(left[row ^ shift, layer]),
            flat(pieces[shift][...]),
            preferred_element_type=jnp.float32,
        )
        other_ref[shift] = flat(left[row ^ shift, 1 - layer])
    sum_ref[...] = total


def far_square_kernel(n_col, n_row, *refs):
    sum_ref, other_ref, met_ref = refs[:3]
    mates, lefts = refs[3 : 3 + n_row], refs[3 + n_row : 3 + n_row + n_col]
    low_ref, give_ref, sems = refs[3 + n_row + n_col :]
    row, col, layer = (lax.axis_index(axis) for axis in ("row", "col", "layer"))
    here = give_ref.shape[1]
    copies = start_copies(
        [
            (piece.at[pl.ds((1 - layer) * here, here)], give_ref.at[col ^ shift])
            for shift, piece in enumerate(lefts)
        ],
        sems,
    )
    left_ref = lefts[-1]
    per_col = met_ref.shape[0]
    width = other_ref.shape[2]

    def columns(block, which):
        start = pl.multiple_of((block * 2 + which) * width, width)
        return flat(left_ref[:, :, pl.ds(start, width)])

    total = sum_ref[...]
    for block in range(per_col):
        total = total + jnp.dot(
            columns(block, layer), met_ref[block], preferred_element_type=jnp.float32
        )
    for shift, mate in enumerate(mates):
        met = row ^ shift
        left = jnp.where(
            lax.div(met, per_col) == col ^ (n_col - 1),
            columns(lax.rem(met, per_col), 1 - layer),
            other_ref[shift],
        )
        total = total + jnp.dot(left, flat(mate[...]), preferred_element_type=jnp.float32)
    low_ref[...] = total.astype(jnp.bfloat16).reshape(low_ref.shape)
    for copy in copies:
        copy.wait()


def near_cube_kernel(n_col, n_row, *refs):
    lefts, given, pattern_ref = refs[:n_col], refs[n_col], refs[n_col + 1]
    pieces, mate_ref = refs[n_col + 2 : n_col + 2 + n_row], refs[n_col + 2 + n_row]
    sum_ref, mask_ref, other_ref, left, own, sems = refs[n_col + 3 + n_row :]
    row, col, layer = (lax.axis_index(axis) for axis in ("row", "col", "layer"))
    rows, cols = sum_ref.shape
    per_col = n_row // n_col
    here = given.shape[1]
    mine = pl.ds(layer * here, here)
    pairs = []
    for block, which, lanes in left_blocks(cols // per_col, cols):
        for shift, piece in enumerate(lefts):
            at = (col ^ shift) * per_col + block
            pairs.append((piece.at[mine, :, lanes], left.at[at, which, :, layer]))
            pairs.append(
                (given.at[col ^ shift, :, :, lanes], left.at[at, which, :, 1 - layer])
            )
    copies = start_copies(pairs, sems)
    own[:, layer] = pieces[0][mine]
    own[:, 1 - layer] = mate_ref[mine]
    pattern = pattern_ref[...].astype(jnp.float32).astype(jnp.bfloat16)
    block_rows, block_cols = pattern.shape
    across = lax.broadcasted_iota(jnp.int32, (block_cols, cols), 1)
    which = lax.broadcasted_iota(jnp.int32, (block_cols, cols), 0)
    wide = (lax.div(across, BLK) == which).astype(jnp.float32).astype(jnp.bfloat16)
    down = lax.broadcasted_iota(jnp.int32, (rows, block_rows), 0) + layer * rows
    which = lax.broadcasted_iota(jnp.int32, (rows, block_rows), 1)
    tall = (lax.div(down, BLK) == which).astype(jnp.float32).astype(jnp.bfloat16)
    tall = jnp.dot(tall, pattern, preferred_element_type=jnp.float32).astype(jnp.bfloat16)
    mask = jnp.dot(tall, wide, preferred_element_type=jnp.float32)
    mask_ref[...] = mask.astype(jnp.bfloat16)
    total = 1.5 * flat(own[...]).astype(jnp.float32)
    for copy in copies:
        copy.wait()
    for shift in range(n_row):
        total = total - jnp.dot(
            flat(left[row ^ shift, layer]),
            flat(pieces[shift][...]),
            preferred_element_type=jnp.float32,
        )
        other_ref[shift] = flat(left[row ^ shift, 1 - layer])
    sum_ref[...] = total


def far_cube_kernel(sum_ref, mask_ref, left_ref, *refs):
    mates, out_ref = refs[:-1], refs[-1]
    total = sum_ref[...]
    for shift, mate in enumerate(mates):
        total = total - jnp.dot(
            left_ref[shift], flat(mate[...]), preferred_element_type=jnp.float32
        )
    out_ref[...] = mask_ref[...].astype(jnp.float32) * (2.0 * total)


def xor_pairs(axis, shift):
    return [(i, i ^ shift) for i in range(lax.axis_size(axis))]


def gather(piece, axis):
    return [piece] + [
        lax.ppermute(piece, axis, xor_pairs(axis, shift))
        for shift in range(1, lax.axis_size(axis))
    ]


def exchange(first, second, capacity):
    def relay(parcels, out_axis, in_axis, weight):
        arrived = [parcels[0]] + [
            lax.ppermute(parcel, out_axis, xor_pairs(out_axis, shift))
            for shift, parcel in enumerate(parcels)
            if shift
        ]
        steps = lax.axis_size(in_axis)
        shape = (len(arrived) * capacity, parcels[0].shape[1])
        mixed = pl.pallas_call(
            functools.partial(mix_kernel, len(arrived), capacity),
            out_shape=[jax.ShapeDtypeStruct(shape, jnp.bfloat16)] * (steps - 1),
            in_specs=[whole_ref()] * len(arrived),
            out_specs=[whole_ref()] * (steps - 1),
            compiler_params=params(4 * steps * shape[0] * shape[1]),
            cost_estimate=cost(weight, 4 * steps * shape[0] * shape[1]),
            name="mix",
        )(*arrived)
        return arrived + [
            lax.ppermute(parcel, in_axis, xor_pairs(in_axis, shift))
            for shift, parcel in enumerate(mixed, 1)
        ]

    return relay(first, "col", "row", 0), relay(second, "row", "col", WEIGHT)


def after(value, *earlier):
    return lax.optimization_barrier((value, earlier))[0]


def gather_line(piece):
    count = lax.axis_size("col")
    pieces = {0: piece}
    step = count // 2
    while step:
        pieces |= {
            shift + step: lax.ppermute(held, "col", xor_pairs("col", step))
            for shift, held in pieces.items()
        }
        step //= 2
    return [pieces[shift] for shift in range(count)]


def swap(piece):
    return lax.ppermute(piece, "layer", xor_pairs("layer", 1))


def on_device(tasks, task_owner, task_slot, p_pattern, c_pattern, occupations):
    n_row, n_col, layers = (lax.axis_size(axis) for axis in ("row", "col", "layer"))
    owners = n_row * n_col
    count = tasks.shape[0]
    capacity = max(2, 2 * count // owners)
    places = owners * capacity
    block_rows, block_cols = p_pattern.shape
    part_rows = BLK // layers
    part = part_rows * BLK
    rows, cols = block_rows * part_rows, block_cols * BLK
    width = part + LANES
    layer = lax.axis_index("layer")

    paired = capacity % 16 == 0
    if paired:
        parcels = [(n_row * capacity, part // 2 + LANES)] * n_col
        parcels += [(n_col * capacity, part - part // 2)] * n_row
    else:
        parcels = [(places, width)]
    sent = pl.pallas_call(
        functools.partial(pack_kernel, owners, capacity, p_pattern.shape, paired),
        out_shape=[jax.ShapeDtypeStruct(shape, jnp.bfloat16) for shape in parcels],
        in_specs=[pl.BlockSpec(memory_space=pltpu.HBM), whole_ref(), whole_ref()],
        out_specs=[whole_ref()] * len(parcels),
        scratch_shapes=[pltpu.VMEM((count, part), jnp.bfloat16), pltpu.SemaphoreType.DMA],
        compiler_params=params(2 * (places + count) * width),
        cost_estimate=cost(2 * places * count * width, 2 * (places + count) * width),
        name="pack",
    )(tasks, task_owner.reshape(1, count), task_slot.reshape(1, count))
    if paired:
        got = list(exchange(sent[:n_col], sent[n_col:], capacity))
    else:
        got = [
            [
                lax.all_to_all(
                    sent[0].reshape(owners, capacity, width),
                    ("row", "col"),
                    split_axis=0,
                    concat_axis=0,
                    tiled=True,
                ).reshape(places, width)
            ]
        ] * 2

    slots_here = block_rows * block_cols
    half_shape = jax.ShapeDtypeStruct((block_rows, part_rows // 2, cols), jnp.bfloat16)
    piece_shape = jax.ShapeDtypeStruct((block_rows, part_rows, cols), jnp.bfloat16)
    marks_shape = jax.ShapeDtypeStruct((slots_here, places), jnp.bfloat16)

    def build(half, marks, *blocks):
        return pl.pallas_call(
            functools.partial(build_kernel, half, paired),
            out_shape=[piece_shape] * 2 if half else [marks_shape, half_shape, half_shape],
            in_specs=[whole_ref()] * (2 + len(blocks)),
            out_specs=[whole_ref()] * (2 if half else 3),
            scratch_shapes=[pltpu.VMEM((cols // LANES, rows // 2, LANES), jnp.float32)],
            compiler_params=params(2 * places * width + 8 * rows * cols),
            cost_estimate=cost(places * slots_here * part, places * width),
            name="build",
        )(occupations.reshape(1, block_rows * BLK), marks, *blocks)

    marks, *first_half = build(0, p_pattern, *got[0])
    density, ordered = build(1, marks, *got[1], *first_half)

    lefts = gather_line(ordered)
    mate = swap(density)
    pieces = gather(after(density, mate), "row")
    pieces[0] = density
    ahead = (lefts[1], lefts[n_col // 2])
    mates = [mate] + [swap(after(piece, *ahead)) for piece in pieces[1:]]
    flops = 2 * rows * cols * n_col * cols
    half_width = block_rows * BLK // layers
    panel_bytes = 2 * n_row * layers * rows * half_width
    sum_shape = jax.ShapeDtypeStruct((rows, cols), jnp.float32)
    other_shape = jax.ShapeDtypeStruct((n_row, rows, half_width), jnp.bfloat16)
    met_shape = jax.ShapeDtypeStruct((n_row // n_col, rows, cols), jnp.bfloat16)
    partial, other, met = pl.pallas_call(
        functools.partial(near_square_kernel, n_col, n_row),
        out_shape=[sum_shape, other_shape, met_shape],
        in_specs=[any_ref()] * (n_col - 1) + [whole_ref()] * n_row,
        out_specs=[whole_ref()] * 3,
        scratch_shapes=[
            pltpu.VMEM((n_row, layers, block_rows, part_rows, half_width), jnp.bfloat16),
            pltpu.SemaphoreType.DMA((n_row * layers,)),
        ],
        compiler_params=params(2 * panel_bytes + 16 * rows * cols),
        cost_estimate=cost(0, 0),
        name="near_square",
    )(*lefts[:-1], *pieces)
    here = block_rows // layers
    square, give = pl.pallas_call(
        functools.partial(far_square_kernel, n_col, n_row),
        out_shape=[
            piece_shape,
            jax.ShapeDtypeStruct((n_col, here, part_rows, cols), jnp.bfloat16),
        ],
        in_specs=[whole_ref()] * (3 + n_row + n_col),
        out_specs=[whole_ref(), any_ref()],
        scratch_shapes=[pltpu.SemaphoreType.DMA((n_col,))],
        compiler_params=params(panel_bytes + 16 * rows * cols),
        cost_estimate=cost(0, 0),
        name="far_square",
    )(partial, other, met, *mates, *lefts)

    pieces = gather(square, "row")
    mates = [swap(piece) for piece in [square] + pieces[1:]]
    received = swap(give)
    partial, mask, other = pl.pallas_call(
        functools.partial(near_cube_kernel, n_col, n_row),
        out_shape=[
            sum_shape,
            jax.ShapeDtypeStruct((rows, cols), jnp.bfloat16),
            other_shape,
        ],
        in_specs=[any_ref()] * (n_col + 1) + [whole_ref()] * (2 + n_row),
        out_specs=[whole_ref()] * 3,
        scratch_shapes=[
            pltpu.VMEM((n_row, layers, here, layers, part_rows, half_width), jnp.bfloat16),
            pltpu.VMEM((here, layers, part_rows, cols), jnp.bfloat16),
            pltpu.SemaphoreType.DMA((2 * n_row * layers,)),
        ],
        compiler_params=params(2 * panel_bytes + 16 * rows * cols),
        cost_estimate=cost(0, 0),
        name="near_cube",
    )(*lefts, received, c_pattern, *pieces, mates[0])
    return pl.pallas_call(
        far_cube_kernel,
        out_shape=sum_shape,
        in_specs=[whole_ref()] * (3 + n_row),
        out_specs=whole_ref(),
        compiler_params=params(16 * rows * cols),
        cost_estimate=cost(flops // 2, 4 * 1024 * 1024),
        name="far_cube",
    )(partial, mask, other, *mates)


def solution(mesh):
    return jax.shard_map(
        on_device,
        mesh=mesh,
        in_specs=(
            P(("row", "col"), None),
            P(("row", "col"), None),
            P(("row", "col")),
            P("row", "col"),
            P("row", "col"),
            P("row"),
        ),
        out_specs=P(("row", "layer"), "col"),
        check_vma=False,
    )
```

```python
import functools

import jax
import jax.numpy as jnp
from jax import lax
from jax.experimental import pallas as pl
from jax.experimental.pallas import tpu as pltpu
from jax.sharding import PartitionSpec as P

BLK = 64
LANES = 128
HEAVY = 4 * 10**9
LIGHT = 2 * 10**9
AHEAD = 10 * 10**9
BEHIND = 10 * 10**9


def params(held):
    return pltpu.CompilerParams(vmem_limit_bytes=held + 6 * 1024 * 1024)


def whole_ref():
    return pl.BlockSpec(memory_space=pltpu.VMEM)


def any_ref():
    return pl.BlockSpec(memory_space=pl.ANY)


def cost(flops, bytes_accessed):
    return pl.CostEstimate(flops=flops, bytes_accessed=bytes_accessed, transcendentals=0)


def pack_kernel(owners, capacity, block_shape, paired, tasks_ref, owner_ref, slot_ref, *refs):
    out_refs, held, sem = refs[:-2], refs[-2], refs[-1]
    count, part = held.shape
    layer = lax.axis_index("layer")
    start = pl.multiple_of(layer * part, part)
    copy = pltpu.make_async_copy(tasks_ref.at[:, pl.ds(start, part)], held, sem)
    copy.start()
    block_rows, block_cols = block_shape
    slot_row = slot_ref[...]
    slot_row = lax.rem(slot_row, block_cols) * block_rows + lax.div(slot_row, block_cols)
    across = lax.broadcasted_iota(jnp.int32, (count, count), 1)
    down = lax.broadcasted_iota(jnp.int32, (count, count), 0)
    slot_col = jnp.sum(
        jnp.where(across == down, slot_row.astype(jnp.float32), 0.0), axis=1, keepdims=True
    )
    owner_row = owner_ref[...]
    if paired:
        owner_row = owner_row ^ (
            lax.axis_index("row") * lax.axis_size("col") + lax.axis_index("col")
        )
    same = (lax.broadcasted_iota(jnp.int32, (owners, count), 0) == owner_row).astype(jnp.float32)
    before = (down < across).astype(jnp.float32).astype(jnp.bfloat16)
    ahead = jnp.dot(same.astype(jnp.bfloat16), before, preferred_element_type=jnp.float32)
    placed = jnp.sum(ahead * same, axis=0, keepdims=True).astype(jnp.int32)
    target = owner_row * capacity + placed
    places = owners * capacity
    move = (
        (lax.broadcasted_iota(jnp.int32, (places, count), 0) == target)
        .astype(jnp.float32)
        .astype(jnp.bfloat16)
    )

    def put(at, end, blocks):
        moved = jnp.dot(move, blocks, preferred_element_type=jnp.float32).astype(jnp.bfloat16)
        if not paired:
            out_refs[0][:, at:end] = moved
            return
        n_row, n_col = lax.axis_size("row"), lax.axis_size("col")
        if at < part // 2 + LANES:
            for over, out_ref in enumerate(out_refs[:n_col]):
                for down in range(n_row):
                    place = (down * n_col + over) * capacity
                    out_ref[down * capacity : (down + 1) * capacity, at:end] = moved[
                        place : place + capacity
                    ]
            return
        at, end = at - (part // 2 + LANES), end - (part // 2 + LANES)
        each = n_col * capacity
        for down, out_ref in enumerate(out_refs[n_col:]):
            out_ref[:, at:end] = moved[down * each : (down + 1) * each]

    slots = jnp.broadcast_to(slot_col, (count, LANES)).astype(jnp.bfloat16)
    put(0, LANES, slots)
    copy.wait()
    step = 512
    for at in range(0, part, step):
        put(LANES + at, LANES + at + step, held[:, at : at + step])


def mix_kernel(arrivals, capacity, *refs):
    for shift, out_ref in enumerate(refs[arrivals:], 1):
        for index, ref in enumerate(refs[:arrivals]):
            out_ref[index * capacity : (index + 1) * capacity, :] = ref[
                shift * capacity : (shift + 1) * capacity, :
            ]


def token_kernel(*refs):
    refs[-1][...] = jnp.zeros_like(refs[-1])


def build_kernel(half, paired, occ_ref, marks_ref, *refs):
    out_ref, sorted_ref, alone_ref, tall = refs[-4:] if half else (*refs[-3:-1], None, refs[-1])
    layers = lax.axis_size("layer")
    block_rows, cols = out_ref.shape[0], out_ref.shape[2]
    part_rows = BLK // layers // 2
    block_cols = cols // BLK
    rows = block_rows * part_rows
    part = part_rows * BLK
    front = 0
    if half:
        got_refs, before = refs[: -7 if paired else -6], refs[-6:-4]
        for ref, old_ref in zip((out_ref, sorted_ref), before):
            ref[:, :part_rows] = old_ref[...]
    else:
        got_refs, held_ref = refs[:-4], refs[-4]
        front = LANES

    def got(at, end):
        if not paired:
            skip = half * (LANES + part)
            return got_refs[0][:, skip + at : skip + end]
        n_row, n_col = lax.axis_size("row"), lax.axis_size("col")
        if not half:
            capacity = got_refs[0].shape[0] // n_row
            parts = [ref[:capacity, at:end] for ref in got_refs[:n_col]]
            parts += [ref[:, at:end] for ref in got_refs[n_col:]]
        else:
            capacity = got_refs[0].shape[0] // n_col
            parts = []
            for down in range(n_row):
                place = slice(down * capacity, (down + 1) * capacity)
                parts.append(got_refs[down][:capacity, at:end])
                parts += [ref[place, at:end] for ref in got_refs[n_row:]]
        return jnp.concatenate(parts, axis=0)

    if half:
        marks = marks_ref[...]
    else:
        slots = got(0, LANES).astype(jnp.float32)
        lane = lax.broadcasted_iota(jnp.int32, slots.shape, 1).astype(jnp.float32)
        which = lax.broadcasted_iota(jnp.int32, (block_cols, LANES), 1)
        spread = lax.div(which, block_rows) == lax.broadcasted_iota(jnp.int32, which.shape, 0)
        which = lax.broadcasted_iota(jnp.int32, (block_rows, LANES), 1)
        here = lax.rem(which, block_rows) == lax.broadcasted_iota(jnp.int32, which.shape, 0)
        pattern = jnp.dot(
            marks_ref[...].astype(jnp.float32),
            spread.astype(jnp.float32),
            preferred_element_type=jnp.float32,
        )
        pattern = jnp.sum(jnp.where(here, pattern, 0.0), axis=0, keepdims=True)
        marks = jnp.where(slots == lane, pattern, 0.0)
        marks = marks.T[: block_rows * block_cols].astype(jnp.bfloat16)
        held_ref[...] = marks
    low = lax.broadcasted_iota(jnp.int32, (block_rows, LANES), 1) < BLK
    step = 256
    for at in range(0, part, step):
        summed = jnp.dot(
            marks, got(front + at, front + at + step), preferred_element_type=jnp.float32
        )
        for pair in range(step // LANES):
            lanes = slice(pair * LANES, (pair + 1) * LANES)
            row = (at // LANES + pair) * 2
            for twin in range(block_cols // 2):
                left = summed[twin * 2 * block_rows : (twin * 2 + 1) * block_rows, lanes]
                right = summed[(twin * 2 + 1) * block_rows : (twin * 2 + 2) * block_rows, lanes]
                tall[twin, pl.ds(row, block_rows, stride=part_rows), :] = jnp.where(
                    low, left, pltpu.roll(right, BLK, 1)
                )
                tall[twin, pl.ds(row + 1, block_rows, stride=part_rows), :] = jnp.where(
                    low, pltpu.roll(left, BLK, 1), right
                )
    tile_rows = block_rows * BLK
    row_here = (lax.axis_index("layer") * 2 + half) * part_rows
    row_start = lax.axis_index("row") * tile_rows + row_here
    col_start = lax.axis_index("col") * cols
    index = lax.broadcasted_iota(jnp.int32, (rows, LANES), 0)
    inside = lax.div(index, part_rows) * BLK + lax.rem(index, part_rows)
    row_id = row_start + inside
    lane = lax.broadcasted_iota(jnp.int32, (rows, LANES), 1)
    occ = jnp.zeros((rows, 1), jnp.float32)
    for at in range(0, tile_rows, LANES):
        mine = jnp.where(row_here + inside == at + lane, occ_ref[:, at : at + LANES], 0.0)
        occ = occ + jnp.sum(mine, axis=1, keepdims=True)
    values = []
    for twin in range(block_cols // 2):
        diagonal = jnp.where(row_id == col_start + twin * LANES + lane, occ, 0.0)
        values.append(tall[twin] + diagonal)
    here = slice(half * part_rows, (half + 1) * part_rows)

    def put(ref, at, value):
        value = value.astype(jnp.bfloat16).reshape(block_rows, part_rows, LANES)
        ref[:, here, at : at + LANES] = value
        if half and ref is sorted_ref:
            alone_ref[:, :, at : at + LANES] = value

    for twin, value in enumerate(values):
        put(out_ref, twin * LANES, value)
    quarter = LANES // 4
    spot = lax.div(lane, quarter)
    for twin in range(0, block_cols // 2, 2):
        first, second = values[twin], values[twin + 1]
        at = twin // (block_rows // 2) * tile_rows + twin % (block_rows // 2) // 2 * LANES
        back, ahead = pltpu.roll(first, 3 * quarter, 1), pltpu.roll(second, quarter, 1)
        far_back, far_ahead = pltpu.roll(first, 2 * quarter, 1), pltpu.roll(second, 2 * quarter, 1)
        put(
            sorted_ref,
            at,
            jnp.where(
                spot == 0, first, jnp.where(spot == 1, back, jnp.where(spot == 2, far_ahead, ahead))
            ),
        )
        put(
            sorted_ref,
            at + tile_rows // 2,
            jnp.where(
                spot == 0, back, jnp.where(spot == 1, far_back, jnp.where(spot == 2, ahead, second))
            ),
        )


def start_copies(pairs, sems):
    copies = [
        pltpu.make_async_copy(source, target, sems.at[index])
        for index, (source, target) in enumerate(pairs)
    ]
    for copy in copies:
        copy.start()
    return copies


def left_blocks(tile_rows, cols):
    width = tile_rows // 2
    return [
        (at // tile_rows, at % tile_rows // width, slice(at, at + width))
        for at in range(0, cols, width)
    ]


def flat(value):
    return value.reshape(-1, value.shape[-1])


def half_rows(half, part_rows):
    if half is None:
        return pl.ds(0, part_rows)
    return pl.ds(half * (part_rows // 2), part_rows // 2)


def near_square_kernel(places, n_col, n_row, *refs):
    count = len(places) - 2
    lefts, pieces = refs[:count], refs[count : count + n_row]
    sum_ref, other_ref, met_ref, give_ref, left, sems = refs[count + n_row + 1 :]
    row, col, layer = (lax.axis_index(axis) for axis in ("row", "col", "layer"))
    cols = sum_ref.shape[1]
    per_col = n_row // n_col
    here, part_rows = give_ref.shape[1:3]
    pairs = []
    for (shift, half), piece in zip(places, lefts):
        rows = half_rows(half, part_rows)
        for block, which, lanes in left_blocks(cols // per_col, cols):
            at = (col ^ shift) * per_col + block
            pairs.append((piece.at[:, :, lanes], left.at[at, which, :, rows]))
    inner = len(pairs)
    for (shift, half), piece in zip(places, lefts):
        rows = half_rows(half, part_rows)
        pairs.append(
            (piece.at[pl.ds((1 - layer) * here, here)], give_ref.at[col ^ shift, :, rows])
        )
    copies = start_copies(pairs, sems)
    last = col ^ (n_col - 1)
    for block in range(per_col):
        left[last * per_col + block] = jnp.zeros(left.shape[1:], left.dtype)
    for shift in range(n_row):

        @pl.when(lax.div(row ^ shift, per_col) == last)
        def _(shift=shift):
            met_ref[lax.rem(row ^ shift, per_col)] = flat(pieces[shift][...])

    for copy in copies[:inner]:
        copy.wait()
    total = jnp.zeros(sum_ref.shape, jnp.float32)
    for shift in range(n_row):
        total = total + jnp.dot(
            flat(left[row ^ shift, layer]),
            flat(pieces[shift][...]),
            preferred_element_type=jnp.float32,
        )
        other_ref[shift] = flat(left[row ^ shift, 1 - layer])
    sum_ref[...] = total
    for copy in copies[inner:]:
        copy.wait()


def far_square_kernel(n_col, n_row, *refs):
    sum_ref, other_ref, met_ref = refs[:3]
    mates, lefts = refs[3 : 3 + n_row], refs[3 + n_row : 5 + n_row]
    low_ref, give_ref, sems = refs[7 + n_row :]
    row, col, layer = (lax.axis_index(axis) for axis in ("row", "col", "layer"))
    last = col ^ (n_col - 1)
    here, part_rows = give_ref.shape[1:3]
    copies = start_copies(
        [
            (
                piece.at[pl.ds((1 - layer) * here, here)],
                give_ref.at[last, :, half_rows(half, part_rows)],
            )
            for half, piece in enumerate(lefts)
        ],
        sems,
    )
    per_col = met_ref.shape[0]
    width = other_ref.shape[2]

    def columns(block, which):
        lanes = pl.ds(pl.multiple_of((block * 2 + which) * width, width), width)
        return flat(jnp.concatenate([ref[:, :, lanes] for ref in lefts], axis=1))

    total = sum_ref[...]
    for block in range(per_col):
        total = total + jnp.dot(
            columns(block, layer), met_ref[block], preferred_element_type=jnp.float32
        )
    for shift, mate in enumerate(mates):
        met = row ^ shift
        left = jnp.where(
            lax.div(met, per_col) == last,
            columns(lax.rem(met, per_col), 1 - layer),
            other_ref[shift],
        )
        total = total + jnp.dot(left, flat(mate[...]), preferred_element_type=jnp.float32)
    low_ref[...] = total.astype(jnp.bfloat16).reshape(low_ref.shape)
    for copy in copies:
        copy.wait()


def near_cube_kernel(places, n_col, n_row, *refs):
    count = len(places)
    lefts, given, pattern_ref = refs[:count], refs[count], refs[count + 1]
    pieces, mate_ref = refs[count + 2 : count + 2 + n_row], refs[count + 2 + n_row]
    sum_ref, mask_ref, other_ref, left, own, sems = refs[count + 3 + n_row :]
    row, col, layer = (lax.axis_index(axis) for axis in ("row", "col", "layer"))
    rows, cols = sum_ref.shape
    per_col = n_row // n_col
    here = given.shape[1]
    mine = pl.ds(layer * here, here)
    pairs = []
    for block, which, lanes in left_blocks(cols // per_col, cols):
        for (shift, half), piece in zip(places, lefts):
            at = (col ^ shift) * per_col + block
            part = half_rows(half, left.shape[4])
            pairs.append((piece.at[mine, :, lanes], left.at[at, which, :, layer, part]))
        for shift in range(n_col):
            at = (col ^ shift) * per_col + block
            pairs.append(
                (given.at[col ^ shift, :, :, lanes], left.at[at, which, :, 1 - layer])
            )
    copies = start_copies(pairs, sems)
    own[:, layer] = pieces[0][mine]
    own[:, 1 - layer] = mate_ref[mine]
    pattern = pattern_ref[...].astype(jnp.float32).astype(jnp.bfloat16)
    block_rows, block_cols = pattern.shape
    across = lax.broadcasted_iota(jnp.int32, (block_cols, cols), 1)
    which = lax.broadcasted_iota(jnp.int32, (block_cols, cols), 0)
    wide = (lax.div(across, BLK) == which).astype(jnp.float32).astype(jnp.bfloat16)
    down = lax.broadcasted_iota(jnp.int32, (rows, block_rows), 0) + layer * rows
    which = lax.broadcasted_iota(jnp.int32, (rows, block_rows), 1)
    tall = (lax.div(down, BLK) == which).astype(jnp.float32).astype(jnp.bfloat16)
    tall = jnp.dot(tall, pattern, preferred_element_type=jnp.float32).astype(jnp.bfloat16)
    mask = jnp.dot(tall, wide, preferred_element_type=jnp.float32)
    mask_ref[...] = mask.astype(jnp.bfloat16)
    total = 1.5 * flat(own[...]).astype(jnp.float32)
    for copy in copies:
        copy.wait()
    for shift in range(n_row):
        total = total - jnp.dot(
            flat(left[row ^ shift, layer]),
            flat(pieces[shift][...]),
            preferred_element_type=jnp.float32,
        )
        other_ref[shift] = flat(left[row ^ shift, 1 - layer])
    sum_ref[...] = total


def far_cube_kernel(sum_ref, mask_ref, left_ref, *refs):
    mates, out_ref = refs[:-1], refs[-1]
    total = sum_ref[...]
    for shift, mate in enumerate(mates):
        total = total - jnp.dot(
            left_ref[shift], flat(mate[...]), preferred_element_type=jnp.float32
        )
    out_ref[...] = mask_ref[...].astype(jnp.float32) * (2.0 * total)


def xor_pairs(axis, shift):
    return [(i, i ^ shift) for i in range(lax.axis_size(axis))]


def gather(piece, axis):
    return [piece] + [
        lax.ppermute(piece, axis, xor_pairs(axis, shift))
        for shift in range(1, lax.axis_size(axis))
    ]


def exchange(first, second, capacity):
    def relay(parcels, out_axis, in_axis, weight):
        arrived = [parcels[0]] + [
            lax.ppermute(parcel, out_axis, xor_pairs(out_axis, shift))
            for shift, parcel in enumerate(parcels)
            if shift
        ]
        steps = lax.axis_size(in_axis)
        shape = (len(arrived) * capacity, parcels[0].shape[1])
        mixed = pl.pallas_call(
            functools.partial(mix_kernel, len(arrived), capacity),
            out_shape=[jax.ShapeDtypeStruct(shape, jnp.bfloat16)] * (steps - 1),
            in_specs=[whole_ref()] * len(arrived),
            out_specs=[whole_ref()] * (steps - 1),
            compiler_params=params(4 * steps * shape[0] * shape[1]),
            cost_estimate=cost(weight, 4 * steps * shape[0] * shape[1]),
            name="mix",
        )(*arrived)
        return arrived + [
            lax.ppermute(parcel, in_axis, xor_pairs(in_axis, shift))
            for shift, parcel in enumerate(mixed, 1)
        ]

    first = relay(first, "col", "row", HEAVY)
    second = relay(second, "row", "col", 0)
    return first, [*second, token(second, LIGHT)]


def after(value, *earlier):
    return lax.optimization_barrier((value, earlier))[0]


def token(values, weight):
    return pl.pallas_call(
        token_kernel,
        out_shape=jax.ShapeDtypeStruct((8, LANES), jnp.float32),
        in_specs=[any_ref()] * len(values),
        out_specs=whole_ref(),
        compiler_params=params(0),
        cost_estimate=cost(weight, 0),
        name="token",
    )(*values)


def gather_line(piece, halves):
    count = lax.axis_size("col")
    near = lax.ppermute(piece, "col", xor_pairs("col", 1))
    found = {}
    for half, own in enumerate(halves):
        found[0, half] = own
        step = count // 2
        while step > 1:
            for shift in range(0, count, 2 * step):
                sent = found[shift, half]
                if half:
                    sent = after(sent, found[shift + step, 0])
                found[shift + step, half] = lax.ppermute(sent, "col", xor_pairs("col", step))
            step //= 2
        for shift in range(2, count, 2):
            sent = found[shift, half]
            if half:
                sent = after(sent, found[shift + 1, 0])
            found[shift + 1, half] = lax.ppermute(sent, "col", xor_pairs("col", 1))
    places = [(0, None), (1, None)]
    places += [(shift, half) for shift in range(2, count) for half in range(2)]
    return [piece, near] + [found[place] for place in places[2:]], places


def swap(piece):
    return lax.ppermute(piece, "layer", xor_pairs("layer", 1))


def on_device(tasks, task_owner, task_slot, p_pattern, c_pattern, occupations):
    n_row, n_col, layers = (lax.axis_size(axis) for axis in ("row", "col", "layer"))
    owners = n_row * n_col
    count = tasks.shape[0]
    capacity = max(2, 2 * count // owners)
    spots = owners * capacity
    block_rows, block_cols = p_pattern.shape
    part_rows = BLK // layers
    part = part_rows * BLK
    rows, cols = block_rows * part_rows, block_cols * BLK
    width = part + LANES
    layer = lax.axis_index("layer")

    paired = capacity % 16 == 0
    if paired:
        parcels = [(n_row * capacity, part // 2 + LANES)] * n_col
        parcels += [(n_col * capacity, part - part // 2)] * n_row
    else:
        parcels = [(spots, width)]
    sent = pl.pallas_call(
        functools.partial(pack_kernel, owners, capacity, p_pattern.shape, paired),
        out_shape=[jax.ShapeDtypeStruct(shape, jnp.bfloat16) for shape in parcels],
        in_specs=[pl.BlockSpec(memory_space=pltpu.HBM), whole_ref(), whole_ref()],
        out_specs=[whole_ref()] * len(parcels),
        scratch_shapes=[pltpu.VMEM((count, part), jnp.bfloat16), pltpu.SemaphoreType.DMA],
        compiler_params=params(2 * (spots + count) * width),
        cost_estimate=cost(2 * spots * count * width, 2 * (spots + count) * width),
        name="pack",
    )(tasks, task_owner.reshape(1, count), task_slot.reshape(1, count))
    if paired:
        got = list(exchange(sent[:n_col], sent[n_col:], capacity))
    else:
        got = [
            [
                lax.all_to_all(
                    sent[0].reshape(owners, capacity, width),
                    ("row", "col"),
                    split_axis=0,
                    concat_axis=0,
                    tiled=True,
                ).reshape(spots, width)
            ]
        ] * 2

    slots_here = block_rows * block_cols
    half_shape = jax.ShapeDtypeStruct((block_rows, part_rows // 2, cols), jnp.bfloat16)
    piece_shape = jax.ShapeDtypeStruct((block_rows, part_rows, cols), jnp.bfloat16)
    marks_shape = jax.ShapeDtypeStruct((slots_here, spots), jnp.bfloat16)

    def build(half, marks, *blocks):
        return pl.pallas_call(
            functools.partial(build_kernel, half, paired),
            out_shape=[piece_shape if half else marks_shape, piece_shape if half else half_shape]
            + [half_shape],
            in_specs=[whole_ref()] * (2 + len(blocks)),
            out_specs=[whole_ref()] * 3,
            scratch_shapes=[pltpu.VMEM((cols // LANES, rows // 2, LANES), jnp.float32)],
            compiler_params=params(2 * spots * width + 8 * rows * cols),
            cost_estimate=cost(spots * slots_here * part, spots * width),
            name="build",
        )(occupations.reshape(1, block_rows * BLK), marks, *blocks)

    marks, *first_half = build(0, p_pattern, *got[0])
    density, ordered, second_half = build(1, marks, *got[1], *first_half)

    lefts, places = gather_line(ordered, (first_half[1], second_half))
    mate = swap(density)
    pieces = gather(after(density, mate), "row")
    pieces[0] = density
    mates = [mate, None] + [swap(after(piece, lefts[1])) for piece in pieces[2:-1]]
    mates.append(swap(after(pieces[-1], lefts[4])))
    mates[1] = swap(after(pieces[1], lefts[3], *mates[2:]))
    flops = 2 * rows * cols * n_col * cols
    half_width = block_rows * BLK // layers
    panel_bytes = 2 * n_row * layers * rows * half_width
    sum_shape = jax.ShapeDtypeStruct((rows, cols), jnp.float32)
    other_shape = jax.ShapeDtypeStruct((n_row, rows, half_width), jnp.bfloat16)
    met_shape = jax.ShapeDtypeStruct((n_row // n_col, rows, cols), jnp.bfloat16)
    here = block_rows // layers
    give_shape = jax.ShapeDtypeStruct((n_col, here, part_rows, cols), jnp.bfloat16)
    n_left = len(places)
    partial, other, met, give = pl.pallas_call(
        functools.partial(near_square_kernel, places, n_col, n_row),
        out_shape=[sum_shape, other_shape, met_shape, give_shape],
        in_specs=[any_ref()] * (n_left - 2) + [whole_ref()] * n_row + [any_ref()],
        out_specs=[whole_ref()] * 3 + [any_ref()],
        scratch_shapes=[
            pltpu.VMEM((n_row, layers, block_rows, part_rows, half_width), jnp.bfloat16),
            pltpu.SemaphoreType.DMA(((n_left - 2) * (n_row // n_col * layers + 1),)),
        ],
        compiler_params=params(2 * panel_bytes + 16 * rows * cols),
        cost_estimate=cost(0, 0),
        name="near_square",
    )(*lefts[:-2], *pieces, token(lefts[2:3], AHEAD))
    square, give = pl.pallas_call(
        functools.partial(far_square_kernel, n_col, n_row),
        out_shape=[piece_shape, give_shape],
        in_specs=[whole_ref()] * (5 + n_row) + [any_ref()] * 2,
        out_specs=[whole_ref(), any_ref()],
        scratch_shapes=[pltpu.SemaphoreType.DMA((2,))],
        input_output_aliases={5 + n_row: 1},
        compiler_params=params(panel_bytes + 16 * rows * cols),
        cost_estimate=cost(0, 0),
        name="far_square",
    )(partial, other, met, *mates, *lefts[-2:], give, token(lefts[-3:-1], BEHIND))

    pieces = gather(square, "row")
    mates = [swap(piece) for piece in [square] + pieces[1:]]
    received = swap(give)
    partial, mask, other = pl.pallas_call(
        functools.partial(near_cube_kernel, places, n_col, n_row),
        out_shape=[
            sum_shape,
            jax.ShapeDtypeStruct((rows, cols), jnp.bfloat16),
            other_shape,
        ],
        in_specs=[any_ref()] * (n_left + 1) + [whole_ref()] * (2 + n_row),
        out_specs=[whole_ref()] * 3,
        scratch_shapes=[
            pltpu.VMEM((n_row, layers, here, layers, part_rows, half_width), jnp.bfloat16),
            pltpu.VMEM((here, layers, part_rows, cols), jnp.bfloat16),
            pltpu.SemaphoreType.DMA(((n_left + n_col) * (n_row // n_col) * layers,)),
        ],
        compiler_params=params(2 * panel_bytes + 16 * rows * cols),
        cost_estimate=cost(0, 0),
        name="near_cube",
    )(*lefts, received, c_pattern, *pieces, mates[0])
    return pl.pallas_call(
        far_cube_kernel,
        out_shape=sum_shape,
        in_specs=[whole_ref()] * (3 + n_row),
        out_specs=whole_ref(),
        compiler_params=params(16 * rows * cols),
        cost_estimate=cost(flops // 2, 4 * 1024 * 1024),
        name="far_cube",
    )(partial, mask, other, *mates)


def solution(mesh):
    return jax.shard_map(
        on_device,
        mesh=mesh,
        in_specs=(
            P(("row", "col"), None),
            P(("row", "col"), None),
            P(("row", "col")),
            P("row", "col"),
            P("row", "col"),
            P("row"),
        ),
        out_specs=P(("row", "layer"), "col"),
        check_vma=False,
    )
```

```python
import functools

import jax
import jax.numpy as jnp
from jax import lax
from jax.experimental import pallas as pl
from jax.experimental.pallas import tpu as pltpu
from jax.sharding import PartitionSpec as P

BLK = 64
LANES = 128
HEAVY = 10**10
LIGHT = 2*10**9


def params(held):
    return pltpu.CompilerParams(vmem_limit_bytes=held + 6 * 1024 * 1024)


def whole_ref():
    return pl.BlockSpec(memory_space=pltpu.VMEM)


def any_ref():
    return pl.BlockSpec(memory_space=pl.ANY)


def cost(flops, bytes_accessed):
    return pl.CostEstimate(flops=flops, bytes_accessed=bytes_accessed, transcendentals=0)


def pack_kernel(owners, capacity, block_shape, paired, tasks_ref, owner_ref, slot_ref, *refs):
    out_refs, held, sem = refs[:-2], refs[-2], refs[-1]
    count, part = held.shape
    layer = lax.axis_index("layer")
    start = pl.multiple_of(layer * part, part)
    copy = pltpu.make_async_copy(tasks_ref.at[:, pl.ds(start, part)], held, sem)
    copy.start()
    block_rows, block_cols = block_shape
    slot_row = slot_ref[...]
    slot_row = lax.rem(slot_row, block_cols) * block_rows + lax.div(slot_row, block_cols)
    across = lax.broadcasted_iota(jnp.int32, (count, count), 1)
    down = lax.broadcasted_iota(jnp.int32, (count, count), 0)
    slot_col = jnp.sum(
        jnp.where(across == down, slot_row.astype(jnp.float32), 0.0), axis=1, keepdims=True
    )
    owner_row = owner_ref[...]
    if paired:
        owner_row = owner_row ^ (
            lax.axis_index("row") * lax.axis_size("col") + lax.axis_index("col")
        )
    same = (lax.broadcasted_iota(jnp.int32, (owners, count), 0) == owner_row).astype(jnp.float32)
    before = (down < across).astype(jnp.float32).astype(jnp.bfloat16)
    ahead = jnp.dot(same.astype(jnp.bfloat16), before, preferred_element_type=jnp.float32)
    placed = jnp.sum(ahead * same, axis=0, keepdims=True).astype(jnp.int32)
    target = owner_row * capacity + placed
    places = owners * capacity
    move = (
        (lax.broadcasted_iota(jnp.int32, (places, count), 0) == target)
        .astype(jnp.float32)
        .astype(jnp.bfloat16)
    )

    def put(at, end, blocks):
        moved = jnp.dot(move, blocks, preferred_element_type=jnp.float32).astype(jnp.bfloat16)
        if not paired:
            out_refs[0][:, at:end] = moved
            return
        n_row, n_col = lax.axis_size("row"), lax.axis_size("col")
        if at < part // 2 + LANES:
            for over, out_ref in enumerate(out_refs[:n_col]):
                for down in range(n_row):
                    place = (down * n_col + over) * capacity
                    out_ref[down * capacity : (down + 1) * capacity, at:end] = moved[
                        place : place + capacity
                    ]
            return
        at, end = at - (part // 2 + LANES), end - (part // 2 + LANES)
        each = n_col * capacity
        for down, out_ref in enumerate(out_refs[n_col:]):
            out_ref[:, at:end] = moved[down * each : (down + 1) * each]

    slots = jnp.broadcast_to(slot_col, (count, LANES)).astype(jnp.bfloat16)
    put(0, LANES, slots)
    copy.wait()
    step = 512
    for at in range(0, part, step):
        put(LANES + at, LANES + at + step, held[:, at : at + step])


def mix_kernel(arrivals, capacity, *refs):
    for shift, out_ref in enumerate(refs[arrivals:], 1):
        for index, ref in enumerate(refs[:arrivals][::-1]):
            out_ref[index * capacity : (index + 1) * capacity, :] = ref[
                shift * capacity : (shift + 1) * capacity, :
            ]


def token_kernel(*refs):
    refs[-1][...] = jnp.zeros_like(refs[-1])


def build_kernel(half, paired, occ_ref, marks_ref, *refs):
    out_ref, sorted_ref, tall = refs[-3:]
    layers = lax.axis_size("layer")
    block_rows, cols = out_ref.shape[0], out_ref.shape[2]
    part_rows = BLK // layers // 2
    block_cols = cols // BLK
    rows = block_rows * part_rows
    part = part_rows * BLK
    front = 0
    if half:
        got_refs, before = refs[1 if paired else 0 : -5][::-1], refs[-5:-3]
        for ref, old_ref in zip((out_ref, sorted_ref), before):
            ref[:, :part_rows] = old_ref[...]
    else:
        got_refs, held_ref = refs[:-4][::-1], refs[-4]
        front = LANES

    def got(at, end):
        if not paired:
            skip = half * (LANES + part)
            return got_refs[0][:, skip + at : skip + end]
        n_row, n_col = lax.axis_size("row"), lax.axis_size("col")
        if not half:
            capacity = got_refs[0].shape[0] // n_row
            parts = [ref[:capacity, at:end] for ref in got_refs[:n_col]]
            parts += [ref[:, at:end] for ref in got_refs[n_col:]]
        else:
            capacity = got_refs[0].shape[0] // n_col
            parts = []
            for down in range(n_row):
                place = slice(down * capacity, (down + 1) * capacity)
                parts.append(got_refs[down][:capacity, at:end])
                parts += [ref[place, at:end] for ref in got_refs[n_row:]]
        return jnp.concatenate(parts, axis=0)

    if half:
        marks = marks_ref[...]
    else:
        slots = got(0, LANES).astype(jnp.float32)
        lane = lax.broadcasted_iota(jnp.int32, slots.shape, 1).astype(jnp.float32)
        which = lax.broadcasted_iota(jnp.int32, (block_cols, LANES), 1)
        spread = lax.div(which, block_rows) == lax.broadcasted_iota(jnp.int32, which.shape, 0)
        which = lax.broadcasted_iota(jnp.int32, (block_rows, LANES), 1)
        here = lax.rem(which, block_rows) == lax.broadcasted_iota(jnp.int32, which.shape, 0)
        pattern = jnp.dot(
            marks_ref[...].astype(jnp.float32),
            spread.astype(jnp.float32),
            preferred_element_type=jnp.float32,
        )
        pattern = jnp.sum(jnp.where(here, pattern, 0.0), axis=0, keepdims=True)
        marks = jnp.where(slots == lane, pattern, 0.0)
        marks = marks.T[: block_rows * block_cols].astype(jnp.bfloat16)
        held_ref[...] = marks
    low = lax.broadcasted_iota(jnp.int32, (block_rows, LANES), 1) < BLK
    step = 256
    for at in range(0, part, step):
        summed = jnp.dot(
            marks, got(front + at, front + at + step), preferred_element_type=jnp.float32
        )
        for pair in range(step // LANES):
            lanes = slice(pair * LANES, (pair + 1) * LANES)
            row = (at // LANES + pair) * 2
            for twin in range(block_cols // 2):
                left = summed[twin * 2 * block_rows : (twin * 2 + 1) * block_rows, lanes]
                right = summed[(twin * 2 + 1) * block_rows : (twin * 2 + 2) * block_rows, lanes]
                tall[twin, pl.ds(row, block_rows, stride=part_rows), :] = jnp.where(
                    low, left, pltpu.roll(right, BLK, 1)
                )
                tall[twin, pl.ds(row + 1, block_rows, stride=part_rows), :] = jnp.where(
                    low, pltpu.roll(left, BLK, 1), right
                )
    tile_rows = block_rows * BLK
    row_here = (lax.axis_index("layer") * 2 + half) * part_rows
    row_start = lax.axis_index("row") * tile_rows + row_here
    col_start = lax.axis_index("col") * cols
    index = lax.broadcasted_iota(jnp.int32, (rows, LANES), 0)
    inside = lax.div(index, part_rows) * BLK + lax.rem(index, part_rows)
    row_id = row_start + inside
    lane = lax.broadcasted_iota(jnp.int32, (rows, LANES), 1)
    occ = jnp.zeros((rows, 1), jnp.float32)
    for at in range(0, tile_rows, LANES):
        mine = jnp.where(row_here + inside == at + lane, occ_ref[:, at : at + LANES], 0.0)
        occ = occ + jnp.sum(mine, axis=1, keepdims=True)
    values = []
    for twin in range(block_cols // 2):
        diagonal = jnp.where(row_id == col_start + twin * LANES + lane, occ, 0.0)
        values.append(tall[twin] + diagonal)
    here = slice(half * part_rows, (half + 1) * part_rows)

    def put(ref, at, value):
        ref[:, here, at : at + LANES] = value.astype(jnp.bfloat16).reshape(
            block_rows, part_rows, LANES
        )

    for twin, value in enumerate(values):
        put(out_ref, twin * LANES, value)
    quarter = LANES // 4
    spot = lax.div(lane, quarter)
    for twin in range(0, block_cols // 2, 2):
        first, second = values[twin], values[twin + 1]
        at = twin // (block_rows // 2) * tile_rows + twin % (block_rows // 2) // 2 * LANES
        back, ahead = pltpu.roll(first, 3 * quarter, 1), pltpu.roll(second, quarter, 1)
        far_back, far_ahead = pltpu.roll(first, 2 * quarter, 1), pltpu.roll(second, 2 * quarter, 1)
        put(
            sorted_ref,
            at,
            jnp.where(
                spot == 0, first, jnp.where(spot == 1, back, jnp.where(spot == 2, far_ahead, ahead))
            ),
        )
        put(
            sorted_ref,
            at + tile_rows // 2,
            jnp.where(
                spot == 0, back, jnp.where(spot == 1, far_back, jnp.where(spot == 2, ahead, second))
            ),
        )


def start_copies(pairs, sems):
    copies = [
        pltpu.make_async_copy(source, target, sems.at[index])
        for index, (source, target) in enumerate(pairs)
    ]
    for copy in copies:
        copy.start()
    return copies


def split(values, sizes):
    ends = [sum(sizes[: index + 1]) for index in range(len(sizes))]
    return [values[end - size : end] for end, size in zip(ends, sizes)]


def joined(parts):
    return flat(jnp.concatenate([part[...] for part in parts], axis=0))


def left_blocks(tile_rows, cols):
    width = tile_rows // 2
    return [
        (at // tile_rows, at % tile_rows // width, slice(at, at + width))
        for at in range(0, cols, width)
    ]


def flat(value):
    return value.reshape(-1, value.shape[-1])


def near_square_kernel(n_col, n_row, *refs):
    lefts, pieces = refs[: n_col - 1], refs[n_col - 1 : n_col - 1 + n_row]
    sum_ref, other_ref, met_ref, give_ref, left, sems = refs[n_col - 1 + n_row :]
    row, col, layer = (lax.axis_index(axis) for axis in ("row", "col", "layer"))
    cols = sum_ref.shape[1]
    per_col = n_row // n_col
    pairs = [
        (piece.at[:, :, lanes], left.at[(col ^ shift) * per_col + block, which])
        for shift, piece in enumerate(lefts)
        for block, which, lanes in left_blocks(cols // per_col, cols)
    ]
    inner = len(pairs)
    here = give_ref.shape[1]
    pairs += [
        (piece.at[pl.ds((1 - layer) * here, here)], give_ref.at[col ^ shift])
        for shift, piece in enumerate(lefts)
    ]
    copies = start_copies(pairs, sems)
    last = col ^ (n_col - 1)
    for block in range(per_col):
        left[last * per_col + block] = jnp.zeros(left.shape[1:], left.dtype)
    for shift in range(n_row):

        @pl.when(lax.div(row ^ shift, per_col) == last)
        def _(shift=shift):
            met_ref[lax.rem(row ^ shift, per_col)] = flat(pieces[shift][...])

    for copy in copies[:inner]:
        copy.wait()
    total = jnp.zeros(sum_ref.shape, jnp.float32)
    for shift in range(n_row):
        total = total + jnp.dot(
            flat(left[row ^ shift, layer]),
            flat(pieces[shift][...]),
            preferred_element_type=jnp.float32,
        )
        other_ref[shift] = flat(left[row ^ shift, 1 - layer])
    sum_ref[...] = total
    for copy in copies[inner:]:
        copy.wait()


def far_square_kernel(n_col, n_row, *refs):
    sum_ref, other_ref, met_ref = refs[:3]
    mates, left_ref = refs[3 : 3 + n_row], refs[3 + n_row]
    low_ref, give_ref, sem = refs[5 + n_row :]
    row, col, layer = (lax.axis_index(axis) for axis in ("row", "col", "layer"))
    here = give_ref.shape[1]
    copy = pltpu.make_async_copy(
        left_ref.at[pl.ds((1 - layer) * here, here)], give_ref.at[col ^ (n_col - 1)], sem
    )
    copy.start()
    per_col = met_ref.shape[0]
    width = other_ref.shape[2]

    def columns(block, which):
        start = pl.multiple_of((block * 2 + which) * width, width)
        return flat(left_ref[:, :, pl.ds(start, width)])

    total = sum_ref[...]
    for block in range(per_col):
        total = total + jnp.dot(
            columns(block, layer), met_ref[block], preferred_element_type=jnp.float32
        )
    for shift, mate in enumerate(mates):
        met = row ^ shift
        left = jnp.where(
            lax.div(met, per_col) == col ^ (n_col - 1),
            columns(lax.rem(met, per_col), 1 - layer),
            other_ref[shift],
        )
        total = total + jnp.dot(left, flat(mate[...]), preferred_element_type=jnp.float32)
    low_ref[...] = total.astype(jnp.bfloat16).reshape(low_ref.shape)
    copy.wait()


def near_cube_kernel(n_col, sizes, *refs):
    lefts, given, pattern_ref = refs[:n_col], refs[n_col], refs[n_col + 1]
    n_row, count = len(sizes), n_col + 2 + sum(sizes)
    pieces, mate_ref = split(refs[n_col + 2 : count], sizes), refs[count]
    sum_ref, mask_ref, other_ref, left, own, sems = refs[count + 1 :]
    row, col, layer = (lax.axis_index(axis) for axis in ("row", "col", "layer"))
    rows, cols = sum_ref.shape
    per_col = n_row // n_col
    here = given.shape[1]
    mine = pl.ds(layer * here, here)
    pairs = []
    for block, which, lanes in left_blocks(cols // per_col, cols):
        for shift, piece in enumerate(lefts):
            at = (col ^ shift) * per_col + block
            pairs.append((piece.at[mine, :, lanes], left.at[at, which, :, layer]))
            pairs.append(
                (given.at[col ^ shift, :, :, lanes], left.at[at, which, :, 1 - layer])
            )
    copies = start_copies(pairs, sems)
    own[:, layer] = pieces[0][0][mine]
    own[:, 1 - layer] = mate_ref[mine]
    pattern = pattern_ref[...].astype(jnp.float32).astype(jnp.bfloat16)
    block_rows, block_cols = pattern.shape
    across = lax.broadcasted_iota(jnp.int32, (block_cols, cols), 1)
    which = lax.broadcasted_iota(jnp.int32, (block_cols, cols), 0)
    wide = (lax.div(across, BLK) == which).astype(jnp.float32).astype(jnp.bfloat16)
    down = lax.broadcasted_iota(jnp.int32, (rows, block_rows), 0) + layer * rows
    which = lax.broadcasted_iota(jnp.int32, (rows, block_rows), 1)
    tall = (lax.div(down, BLK) == which).astype(jnp.float32).astype(jnp.bfloat16)
    tall = jnp.dot(tall, pattern, preferred_element_type=jnp.float32).astype(jnp.bfloat16)
    mask = jnp.dot(tall, wide, preferred_element_type=jnp.float32)
    mask_ref[...] = mask.astype(jnp.bfloat16)
    total = 1.5 * flat(own[...]).astype(jnp.float32)
    for copy in copies:
        copy.wait()
    for shift in range(n_row):
        total = total - jnp.dot(
            flat(left[row ^ shift, layer]),
            joined(pieces[shift]),
            preferred_element_type=jnp.float32,
        )
        other_ref[shift] = flat(left[row ^ shift, 1 - layer])
    sum_ref[...] = total


def far_cube_kernel(sizes, sum_ref, mask_ref, left_ref, *refs):
    mates, out_ref = split(refs[:-2], sizes), refs[-1]
    total = sum_ref[...]
    for shift, mate in enumerate(mates):
        total = total - jnp.dot(
            left_ref[shift], joined(mate), preferred_element_type=jnp.float32
        )
    out_ref[...] = mask_ref[...].astype(jnp.float32) * (2.0 * total)


def xor_pairs(axis, shift):
    return [(i, i ^ shift) for i in range(lax.axis_size(axis))]


def gather(piece, axis):
    return [piece] + [
        lax.ppermute(piece, axis, xor_pairs(axis, shift))
        for shift in range(1, lax.axis_size(axis))
    ]


def exchange(first, second, capacity):
    def relay(parcels, out_axis, in_axis, weight):
        arrived = [parcels[0]] + [
            lax.ppermute(parcel, out_axis, xor_pairs(out_axis, shift))
            for shift, parcel in enumerate(parcels)
            if shift
        ]
        steps = lax.axis_size(in_axis)
        shape = (len(arrived) * capacity, parcels[0].shape[1])
        mixed = pl.pallas_call(
            functools.partial(mix_kernel, len(arrived), capacity),
            out_shape=[jax.ShapeDtypeStruct(shape, jnp.bfloat16)] * (steps - 1),
            in_specs=[whole_ref()] * len(arrived),
            out_specs=[whole_ref()] * (steps - 1),
            compiler_params=params(4 * steps * shape[0] * shape[1]),
            cost_estimate=cost(weight, 4 * steps * shape[0] * shape[1]),
            name="mix",
        )(*arrived[::-1])
        return arrived + [
            lax.ppermute(parcel, in_axis, xor_pairs(in_axis, shift))
            for shift, parcel in enumerate(mixed, 1)
        ]

    first = relay(first, "col", "row", HEAVY)
    second = relay(second, "row", "col", 0)
    return first, [*second, token(second, LIGHT)]


def after(value, *earlier):
    return lax.optimization_barrier((value, earlier))[0]


def token(values, weight):
    return pl.pallas_call(
        token_kernel,
        out_shape=jax.ShapeDtypeStruct((8, LANES), jnp.float32),
        in_specs=[any_ref()] * len(values),
        out_specs=whole_ref(),
        compiler_params=params(0),
        cost_estimate=cost(weight, 0),
        name="token",
    )(*values)


def gather_line(piece):
    count = lax.axis_size("col")
    pieces = {0: piece}
    step = count // 2
    while step:
        pieces |= {
            shift + step: lax.ppermute(held, "col", xor_pairs("col", step))
            for shift, held in pieces.items()
        }
        step //= 2
    return [pieces[shift] for shift in range(count)]


def gather_square(piece):
    if lax.axis_size("row") != 4:
        return [[held] for held in gather(piece, "row")]
    one, two = (lax.ppermute(piece, "row", xor_pairs("row", shift)) for shift in (1, 2))
    middle = piece.shape[0] // 2
    far = [
        lax.ppermute(two[:middle], "row", xor_pairs("row", 1)),
        lax.ppermute(one[middle:], "row", xor_pairs("row", 2)),
    ]
    return [[piece], [one], [two], far]


def swap(piece):
    return lax.ppermute(piece, "layer", xor_pairs("layer", 1))


def on_device(tasks, task_owner, task_slot, p_pattern, c_pattern, occupations):
    n_row, n_col, layers = (lax.axis_size(axis) for axis in ("row", "col", "layer"))
    owners = n_row * n_col
    count = tasks.shape[0]
    capacity = max(2, 2 * count // owners)
    places = owners * capacity
    block_rows, block_cols = p_pattern.shape
    part_rows = BLK // layers
    part = part_rows * BLK
    rows, cols = block_rows * part_rows, block_cols * BLK
    width = part + LANES
    layer = lax.axis_index("layer")

    paired = capacity % 16 == 0
    if paired:
        parcels = [(n_row * capacity, part // 2 + LANES)] * n_col
        parcels += [(n_col * capacity, part - part // 2)] * n_row
    else:
        parcels = [(places, width)]
    sent = pl.pallas_call(
        functools.partial(pack_kernel, owners, capacity, p_pattern.shape, paired),
        out_shape=[jax.ShapeDtypeStruct(shape, jnp.bfloat16) for shape in parcels],
        in_specs=[pl.BlockSpec(memory_space=pltpu.HBM), whole_ref(), whole_ref()],
        out_specs=[whole_ref()] * len(parcels),
        scratch_shapes=[pltpu.VMEM((count, part), jnp.bfloat16), pltpu.SemaphoreType.DMA],
        compiler_params=params(2 * (places + count) * width),
        cost_estimate=cost(2 * places * count * width, 2 * (places + count) * width),
        name="pack",
    )(tasks, task_owner.reshape(1, count), task_slot.reshape(1, count))
    if paired:
        got = list(exchange(sent[:n_col], sent[n_col:], capacity))
    else:
        got = [
            [
                lax.all_to_all(
                    sent[0].reshape(owners, capacity, width),
                    ("row", "col"),
                    split_axis=0,
                    concat_axis=0,
                    tiled=True,
                ).reshape(places, width)
            ]
        ] * 2

    slots_here = block_rows * block_cols
    half_shape = jax.ShapeDtypeStruct((block_rows, part_rows // 2, cols), jnp.bfloat16)
    piece_shape = jax.ShapeDtypeStruct((block_rows, part_rows, cols), jnp.bfloat16)
    marks_shape = jax.ShapeDtypeStruct((slots_here, places), jnp.bfloat16)

    def build(half, marks, *blocks):
        return pl.pallas_call(
            functools.partial(build_kernel, half, paired),
            out_shape=[piece_shape] * 2 if half else [marks_shape, half_shape, half_shape],
            in_specs=[whole_ref()] * (2 + len(blocks)),
            out_specs=[whole_ref()] * (2 if half else 3),
            scratch_shapes=[pltpu.VMEM((cols // LANES, rows // 2, LANES), jnp.float32)],
            compiler_params=params(2 * places * width + 8 * rows * cols),
            cost_estimate=cost(places * slots_here * part, places * width),
            name="build",
        )(occupations.reshape(1, block_rows * BLK), marks, *blocks)

    marks, *first_half = build(0, p_pattern, *got[0][::-1])
    density, ordered = build(1, marks, *got[1][::-1], *first_half)

    lefts = gather_line(ordered)
    mate = swap(density)
    pieces = gather(after(density, mate), "row")
    pieces[0] = density
    ahead = (lefts[1], lefts[n_col // 2])
    mates = [mate] + [swap(after(piece, *ahead)) for piece in pieces[1:]]
    flops = 2 * rows * cols * n_col * cols
    half_width = block_rows * BLK // layers
    panel_bytes = 2 * n_row * layers * rows * half_width
    sum_shape = jax.ShapeDtypeStruct((rows, cols), jnp.float32)
    other_shape = jax.ShapeDtypeStruct((n_row, rows, half_width), jnp.bfloat16)
    met_shape = jax.ShapeDtypeStruct((n_row // n_col, rows, cols), jnp.bfloat16)
    here = block_rows // layers
    give_shape = jax.ShapeDtypeStruct((n_col, here, part_rows, cols), jnp.bfloat16)
    partial, other, met, give = pl.pallas_call(
        functools.partial(near_square_kernel, n_col, n_row),
        out_shape=[sum_shape, other_shape, met_shape, give_shape],
        in_specs=[any_ref()] * (n_col - 1) + [whole_ref()] * n_row,
        out_specs=[whole_ref()] * 3 + [any_ref()],
        scratch_shapes=[
            pltpu.VMEM((n_row, layers, block_rows, part_rows, half_width), jnp.bfloat16),
            pltpu.SemaphoreType.DMA((n_row * layers + n_col,)),
        ],
        compiler_params=params(2 * panel_bytes + 16 * rows * cols),
        cost_estimate=cost(0, 0),
        name="near_square",
    )(*lefts[:-1], *pieces)
    square, give = pl.pallas_call(
        functools.partial(far_square_kernel, n_col, n_row),
        out_shape=[piece_shape, give_shape],
        in_specs=[whole_ref()] * (4 + n_row) + [any_ref()],
        out_specs=[whole_ref(), any_ref()],
        scratch_shapes=[pltpu.SemaphoreType.DMA],
        input_output_aliases={4 + n_row: 1},
        compiler_params=params(panel_bytes + 16 * rows * cols),
        cost_estimate=cost(0, 0),
        name="far_square",
    )(partial, other, met, *mates, lefts[-1], give)

    pieces = gather_square(square)
    mates = [[swap(part) for part in parts] for parts in pieces]
    if len(pieces[-1]) > 1:
        mates[1:3] = [[swap(after(pieces[shift][0], pieces[3 - shift][0]))] for shift in (1, 2)]
    received = swap(after(give, pieces[1][0], pieces[2][0]))
    sizes = [len(parts) for parts in pieces]
    pieces, mates = ([part for parts in held for part in parts] for held in (pieces, mates))
    partial, mask, other = pl.pallas_call(
        functools.partial(near_cube_kernel, n_col, sizes),
        out_shape=[
            sum_shape,
            jax.ShapeDtypeStruct((rows, cols), jnp.bfloat16),
            other_shape,
        ],
        in_specs=[any_ref()] * (n_col + 1) + [whole_ref()] * (2 + len(pieces)),
        out_specs=[whole_ref()] * 3,
        scratch_shapes=[
            pltpu.VMEM((n_row, layers, here, layers, part_rows, half_width), jnp.bfloat16),
            pltpu.VMEM((here, layers, part_rows, cols), jnp.bfloat16),
            pltpu.SemaphoreType.DMA((2 * n_row * layers,)),
        ],
        compiler_params=params(2 * panel_bytes + 16 * rows * cols),
        cost_estimate=cost(0, 0),
        name="near_cube",
    )(*lefts, received, c_pattern, *pieces, mates[0])
    return pl.pallas_call(
        functools.partial(far_cube_kernel, sizes),
        out_shape=sum_shape,
        in_specs=[whole_ref()] * (3 + len(mates)) + [any_ref()],
        out_specs=whole_ref(),
        compiler_params=params(16 * rows * cols),
        cost_estimate=cost(flops // 2, 4 * 1024 * 1024),
        name="far_cube",
    )(partial, mask, other, *mates, token(pieces[3:], HEAVY))


def solution(mesh):
    return jax.shard_map(
        on_device,
        mesh=mesh,
        in_specs=(
            P(("row", "col"), None),
            P(("row", "col"), None),
            P(("row", "col")),
            P("row", "col"),
            P("row", "col"),
            P("row"),
        ),
        out_specs=P(("row", "layer"), "col"),
        check_vma=False,
    )
```

```python
import functools

import jax
import jax.numpy as jnp
from jax import lax
from jax.experimental import pallas as pl
from jax.experimental.pallas import tpu as pltpu
from jax.sharding import PartitionSpec as P

BLK = 64
LANES = 128
HEAVY = 10**10
EARLY = 0
EXTRA = 0
LATE = 0


def params(held):
    return pltpu.CompilerParams(vmem_limit_bytes=held + 6 * 1024 * 1024)


def whole_ref():
    return pl.BlockSpec(memory_space=pltpu.VMEM)


def any_ref():
    return pl.BlockSpec(memory_space=pl.ANY)


def cost(flops, bytes_accessed):
    return pl.CostEstimate(flops=flops, bytes_accessed=bytes_accessed, transcendentals=0)


def pack_kernel(owners, capacity, block_shape, paired, tasks_ref, owner_ref, slot_ref, *refs):
    out_refs, held, sem = refs[:-2], refs[-2], refs[-1]
    count, part = held.shape
    layer = lax.axis_index("layer")
    start = pl.multiple_of(layer * part, part)
    copy = pltpu.make_async_copy(tasks_ref.at[:, pl.ds(start, part)], held, sem)
    copy.start()
    block_rows, block_cols = block_shape
    slot_row = slot_ref[...]
    slot_row = lax.rem(slot_row, block_cols) * block_rows + lax.div(slot_row, block_cols)
    across = lax.broadcasted_iota(jnp.int32, (count, count), 1)
    down = lax.broadcasted_iota(jnp.int32, (count, count), 0)
    slot_col = jnp.sum(
        jnp.where(across == down, slot_row.astype(jnp.float32), 0.0), axis=1, keepdims=True
    )
    owner_row = owner_ref[...]
    if paired:
        owner_row = owner_row ^ (
            lax.axis_index("row") * lax.axis_size("col") + lax.axis_index("col")
        )
    same = (lax.broadcasted_iota(jnp.int32, (owners, count), 0) == owner_row).astype(jnp.float32)
    before = (down < across).astype(jnp.float32).astype(jnp.bfloat16)
    ahead = jnp.dot(same.astype(jnp.bfloat16), before, preferred_element_type=jnp.float32)
    placed = jnp.sum(ahead * same, axis=0, keepdims=True).astype(jnp.int32)
    target = owner_row * capacity + placed
    places = owners * capacity
    move = (
        (lax.broadcasted_iota(jnp.int32, (places, count), 0) == target)
        .astype(jnp.float32)
        .astype(jnp.bfloat16)
    )

    def put(at, end, blocks):
        moved = jnp.dot(move, blocks, preferred_element_type=jnp.float32).astype(jnp.bfloat16)
        if not paired:
            out_refs[0][:, at:end] = moved
            return
        n_row, n_col = lax.axis_size("row"), lax.axis_size("col")
        if at < part // 2 + LANES:
            each = n_col * capacity
            for down, out_ref in enumerate(out_refs[:n_row]):
                out_ref[:, at:end] = moved[down * each : (down + 1) * each]
            return
        at, end = at - (part // 2 + LANES), end - (part // 2 + LANES)
        for over, out_ref in enumerate(out_refs[n_row:]):
            for down in range(n_row):
                place = (down * n_col + over) * capacity
                out_ref[down * capacity : (down + 1) * capacity, at:end] = moved[
                    place : place + capacity
                ]

    slots = jnp.broadcast_to(slot_col, (count, LANES)).astype(jnp.bfloat16)
    put(0, LANES, slots)
    copy.wait()
    step = 512
    for at in range(0, part, step):
        put(LANES + at, LANES + at + step, held[:, at : at + step])


def mix_kernel(arrivals, capacity, *refs):
    for shift, out_ref in enumerate(refs[arrivals:], 1):
        for index, ref in enumerate(refs[:arrivals][::-1]):
            out_ref[index * capacity : (index + 1) * capacity, :] = ref[
                shift * capacity : (shift + 1) * capacity, :
            ]


def token_kernel(*refs):
    refs[-1][...] = jnp.zeros_like(refs[-1])


def build_kernel(half, paired, occ_ref, marks_ref, *refs):
    out_ref, sorted_ref, tall = refs[-3:]
    layers = lax.axis_size("layer")
    block_rows, cols = out_ref.shape[0], out_ref.shape[2]
    part_rows = BLK // layers // 2
    block_cols = cols // BLK
    rows = block_rows * part_rows
    part = part_rows * BLK
    front = 0
    if half:
        got_refs, before = refs[1 if paired else 0 : -5][::-1], refs[-5:-3]
        for ref, old_ref in zip((out_ref, sorted_ref), before):
            ref[:, :part_rows] = old_ref[...]
    else:
        got_refs, held_ref = refs[:-4][::-1], refs[-4]
        front = LANES

    def got(at, end):
        if not paired:
            skip = half * (LANES + part)
            return got_refs[0][:, skip + at : skip + end]
        n_row, n_col = lax.axis_size("row"), lax.axis_size("col")
        if half:
            capacity = got_refs[0].shape[0] // n_row
            parts = [ref[:capacity, at:end] for ref in got_refs[:n_col]]
            parts += [ref[:, at:end] for ref in got_refs[n_col:]]
        else:
            capacity = got_refs[0].shape[0] // n_col
            parts = []
            for down in range(n_row):
                place = slice(down * capacity, (down + 1) * capacity)
                parts.append(got_refs[down][:capacity, at:end])
                parts += [ref[place, at:end] for ref in got_refs[n_row:]]
        return jnp.concatenate(parts, axis=0)

    if half:
        marks = marks_ref[...]
    else:
        slots = got(0, LANES).astype(jnp.float32)
        lane = lax.broadcasted_iota(jnp.int32, slots.shape, 1).astype(jnp.float32)
        which = lax.broadcasted_iota(jnp.int32, (block_cols, LANES), 1)
        spread = lax.div(which, block_rows) == lax.broadcasted_iota(jnp.int32, which.shape, 0)
        which = lax.broadcasted_iota(jnp.int32, (block_rows, LANES), 1)
        here = lax.rem(which, block_rows) == lax.broadcasted_iota(jnp.int32, which.shape, 0)
        pattern = jnp.dot(
            marks_ref[...].astype(jnp.float32),
            spread.astype(jnp.float32),
            preferred_element_type=jnp.float32,
        )
        pattern = jnp.sum(jnp.where(here, pattern, 0.0), axis=0, keepdims=True)
        marks = jnp.where(slots == lane, pattern, 0.0)
        marks = marks.T[: block_rows * block_cols].astype(jnp.bfloat16)
        held_ref[...] = marks
    low = lax.broadcasted_iota(jnp.int32, (block_rows, LANES), 1) < BLK
    step = 256
    for at in range(0, part, step):
        summed = jnp.dot(
            marks, got(front + at, front + at + step), preferred_element_type=jnp.float32
        )
        for pair in range(step // LANES):
            lanes = slice(pair * LANES, (pair + 1) * LANES)
            row = (at // LANES + pair) * 2
            for twin in range(block_cols // 2):
                left = summed[twin * 2 * block_rows : (twin * 2 + 1) * block_rows, lanes]
                right = summed[(twin * 2 + 1) * block_rows : (twin * 2 + 2) * block_rows, lanes]
                tall[twin, pl.ds(row, block_rows, stride=part_rows), :] = jnp.where(
                    low, left, pltpu.roll(right, BLK, 1)
                )
                tall[twin, pl.ds(row + 1, block_rows, stride=part_rows), :] = jnp.where(
                    low, pltpu.roll(left, BLK, 1), right
                )
    tile_rows = block_rows * BLK
    row_here = (lax.axis_index("layer") * 2 + half) * part_rows
    row_start = lax.axis_index("row") * tile_rows + row_here
    col_start = lax.axis_index("col") * cols
    index = lax.broadcasted_iota(jnp.int32, (rows, LANES), 0)
    inside = lax.div(index, part_rows) * BLK + lax.rem(index, part_rows)
    row_id = row_start + inside
    lane = lax.broadcasted_iota(jnp.int32, (rows, LANES), 1)
    occ = jnp.zeros((rows, 1), jnp.float32)
    for at in range(0, tile_rows, LANES):
        mine = jnp.where(row_here + inside == at + lane, occ_ref[:, at : at + LANES], 0.0)
        occ = occ + jnp.sum(mine, axis=1, keepdims=True)
    values = []
    for twin in range(block_cols // 2):
        diagonal = jnp.where(row_id == col_start + twin * LANES + lane, occ, 0.0)
        values.append(tall[twin] + diagonal)
    here = slice(half * part_rows, (half + 1) * part_rows)

    def put(ref, at, value):
        ref[:, here, at : at + LANES] = value.astype(jnp.bfloat16).reshape(
            block_rows, part_rows, LANES
        )

    for twin, value in enumerate(values):
        put(out_ref, twin * LANES, value)
    quarter = LANES // 4
    spot = lax.div(lane, quarter)
    for twin in range(0, block_cols // 2, 2):
        first, second = values[twin], values[twin + 1]
        at = twin // (block_rows // 2) * tile_rows + twin % (block_rows // 2) // 2 * LANES
        back, ahead = pltpu.roll(first, 3 * quarter, 1), pltpu.roll(second, quarter, 1)
        far_back, far_ahead = pltpu.roll(first, 2 * quarter, 1), pltpu.roll(second, 2 * quarter, 1)
        put(
            sorted_ref,
            at,
            jnp.where(
                spot == 0, first, jnp.where(spot == 1, back, jnp.where(spot == 2, far_ahead, ahead))
            ),
        )
        put(
            sorted_ref,
            at + tile_rows // 2,
            jnp.where(
                spot == 0, back, jnp.where(spot == 1, far_back, jnp.where(spot == 2, ahead, second))
            ),
        )


def start_copies(pairs, sems):
    copies = [
        pltpu.make_async_copy(source, target, sems.at[index])
        for index, (source, target) in enumerate(pairs)
    ]
    for copy in copies:
        copy.start()
    return copies


def split(values, sizes):
    ends = [sum(sizes[: index + 1]) for index in range(len(sizes))]
    return [values[end - size : end] for end, size in zip(ends, sizes)]


def joined(parts):
    return flat(jnp.concatenate([part[...] for part in parts], axis=0))


def left_blocks(tile_rows, cols):
    width = tile_rows // 2
    return [
        (at // tile_rows, at % tile_rows // width, slice(at, at + width))
        for at in range(0, cols, width)
    ]


def flat(value):
    return value.reshape(-1, value.shape[-1])


def near_square_kernel(n_col, n_row, *refs):
    lefts, pieces = refs[: n_col - 1], refs[n_col - 1 : n_col - 1 + n_row]
    sum_ref, other_ref, met_ref, give_ref, left, sems = refs[n_col - 1 + n_row :]
    row, col, layer = (lax.axis_index(axis) for axis in ("row", "col", "layer"))
    cols = sum_ref.shape[1]
    per_col = n_row // n_col
    pairs = [
        (piece.at[:, :, lanes], left.at[(col ^ shift) * per_col + block, which])
        for shift, piece in enumerate(lefts)
        for block, which, lanes in left_blocks(cols // per_col, cols)
    ]
    inner = len(pairs)
    here = give_ref.shape[1]
    pairs += [
        (piece.at[pl.ds((1 - layer) * here, here)], give_ref.at[col ^ shift])
        for shift, piece in enumerate(lefts)
    ]
    copies = start_copies(pairs, sems)
    last = col ^ (n_col - 1)
    for block in range(per_col):
        left[last * per_col + block] = jnp.zeros(left.shape[1:], left.dtype)
    for shift in range(n_row):

        @pl.when(lax.div(row ^ shift, per_col) == last)
        def _(shift=shift):
            met_ref[lax.rem(row ^ shift, per_col)] = flat(pieces[shift][...])

    for copy in copies[:inner]:
        copy.wait()
    total = jnp.zeros(sum_ref.shape, jnp.float32)
    for shift in range(n_row):
        total = total + jnp.dot(
            flat(left[row ^ shift, layer]),
            flat(pieces[shift][...]),
            preferred_element_type=jnp.float32,
        )
        other_ref[shift] = flat(left[row ^ shift, 1 - layer])
    sum_ref[...] = total
    for copy in copies[inner:]:
        copy.wait()


def far_square_kernel(n_col, n_row, *refs):
    sum_ref, other_ref, met_ref = refs[:3]
    mates, left_ref = refs[3 : 3 + n_row], refs[3 + n_row]
    low_ref, give_ref, sem = refs[5 + n_row :]
    row, col, layer = (lax.axis_index(axis) for axis in ("row", "col", "layer"))
    here = give_ref.shape[1]
    copy = pltpu.make_async_copy(
        left_ref.at[pl.ds((1 - layer) * here, here)], give_ref.at[col ^ (n_col - 1)], sem
    )
    copy.start()
    per_col = met_ref.shape[0]
    width = other_ref.shape[2]

    def columns(block, which):
        start = pl.multiple_of((block * 2 + which) * width, width)
        return flat(left_ref[:, :, pl.ds(start, width)])

    total = sum_ref[...]
    for block in range(per_col):
        total = total + jnp.dot(
            columns(block, layer), met_ref[block], preferred_element_type=jnp.float32
        )
    for shift, mate in enumerate(mates):
        met = row ^ shift
        left = jnp.where(
            lax.div(met, per_col) == col ^ (n_col - 1),
            columns(lax.rem(met, per_col), 1 - layer),
            other_ref[shift],
        )
        total = total + jnp.dot(left, flat(mate[...]), preferred_element_type=jnp.float32)
    low_ref[...] = total.astype(jnp.bfloat16).reshape(low_ref.shape)
    copy.wait()


def near_cube_kernel(n_col, sizes, *refs):
    lefts, given, pattern_ref = refs[:n_col], refs[n_col], refs[n_col + 1]
    n_row, count = len(sizes), n_col + 2 + sum(sizes)
    pieces, mate_ref = split(refs[n_col + 2 : count], sizes), refs[count]
    sum_ref, mask_ref, other_ref, left, own, sems = refs[count + 1 :]
    row, col, layer = (lax.axis_index(axis) for axis in ("row", "col", "layer"))
    rows, cols = sum_ref.shape
    per_col = n_row // n_col
    here = given.shape[1]
    mine = pl.ds(layer * here, here)
    pairs = []
    for block, which, lanes in left_blocks(cols // per_col, cols):
        for shift, piece in enumerate(lefts):
            at = (col ^ shift) * per_col + block
            pairs.append((piece.at[mine, :, lanes], left.at[at, which, :, layer]))
            pairs.append(
                (given.at[col ^ shift, :, :, lanes], left.at[at, which, :, 1 - layer])
            )
    copies = start_copies(pairs, sems)
    own[:, layer] = pieces[0][0][mine]
    own[:, 1 - layer] = mate_ref[mine]
    pattern = pattern_ref[...].astype(jnp.float32).astype(jnp.bfloat16)
    block_rows, block_cols = pattern.shape
    across = lax.broadcasted_iota(jnp.int32, (block_cols, cols), 1)
    which = lax.broadcasted_iota(jnp.int32, (block_cols, cols), 0)
    wide = (lax.div(across, BLK) == which).astype(jnp.float32).astype(jnp.bfloat16)
    down = lax.broadcasted_iota(jnp.int32, (rows, block_rows), 0) + layer * rows
    which = lax.broadcasted_iota(jnp.int32, (rows, block_rows), 1)
    tall = (lax.div(down, BLK) == which).astype(jnp.float32).astype(jnp.bfloat16)
    tall = jnp.dot(tall, pattern, preferred_element_type=jnp.float32).astype(jnp.bfloat16)
    mask = jnp.dot(tall, wide, preferred_element_type=jnp.float32)
    mask_ref[...] = mask.astype(jnp.bfloat16)
    total = 1.5 * flat(own[...]).astype(jnp.float32)
    for copy in copies:
        copy.wait()
    for shift in range(n_row):
        total = total - jnp.dot(
            flat(left[row ^ shift, layer]),
            joined(pieces[shift]),
            preferred_element_type=jnp.float32,
        )
        other_ref[shift] = flat(left[row ^ shift, 1 - layer])
    sum_ref[...] = total


def far_cube_kernel(sizes, sum_ref, mask_ref, left_ref, *refs):
    mates, out_ref = split(refs[:-2], sizes), refs[-1]
    total = sum_ref[...]
    for shift, mate in enumerate(mates):
        total = total - jnp.dot(
            left_ref[shift], joined(mate), preferred_element_type=jnp.float32
        )
    out_ref[...] = mask_ref[...].astype(jnp.float32) * (2.0 * total)


def xor_pairs(axis, shift):
    return [(i, i ^ shift) for i in range(lax.axis_size(axis))]


def gather(piece, axis):
    return [piece] + [
        lax.ppermute(piece, axis, xor_pairs(axis, shift))
        for shift in range(1, lax.axis_size(axis))
    ]


def exchange(first, second, capacity):
    def relay(parcels, out_axis, in_axis, weight):
        arrived = [parcels[0]] + [
            lax.ppermute(parcel, out_axis, xor_pairs(out_axis, shift))
            for shift, parcel in enumerate(parcels)
            if shift
        ]
        steps = lax.axis_size(in_axis)
        shape = (len(arrived) * capacity, parcels[0].shape[1])
        mixed = pl.pallas_call(
            functools.partial(mix_kernel, len(arrived), capacity),
            out_shape=[jax.ShapeDtypeStruct(shape, jnp.bfloat16)] * (steps - 1),
            in_specs=[whole_ref()] * len(arrived),
            out_specs=[whole_ref()] * (steps - 1),
            compiler_params=params(4 * steps * shape[0] * shape[1]),
            cost_estimate=cost(weight, 4 * steps * shape[0] * shape[1]),
            name="mix",
        )(*arrived[::-1])
        return arrived + [
            lax.ppermute(parcel, in_axis, xor_pairs(in_axis, shift))
            for shift, parcel in enumerate(mixed, 1)
        ]

    first = relay(first, "row", "col", EARLY)
    second = relay(second, "col", "row", LATE)
    return first, [*second, token(second, EXTRA)]


def after(value, *earlier):
    return lax.optimization_barrier((value, earlier))[0]


def token(values, weight):
    return pl.pallas_call(
        token_kernel,
        out_shape=jax.ShapeDtypeStruct((8, LANES), jnp.float32),
        in_specs=[any_ref()] * len(values),
        out_specs=whole_ref(),
        compiler_params=params(0),
        cost_estimate=cost(weight, 0),
        name="token",
    )(*values)


def gather_line(piece):
    count = lax.axis_size("col")
    pieces = {0: piece}
    step = count // 2
    while step:
        pieces |= {
            shift + step: lax.ppermute(held, "col", xor_pairs("col", step))
            for shift, held in pieces.items()
        }
        step //= 2
    return [pieces[shift] for shift in range(count)]


def gather_square(piece):
    if lax.axis_size("row") != 4:
        return [[held] for held in gather(piece, "row")]
    one, two = (lax.ppermute(piece, "row", xor_pairs("row", shift)) for shift in (1, 2))
    middle = piece.shape[0] // 2
    far = [
        lax.ppermute(two[:middle], "row", xor_pairs("row", 1)),
        lax.ppermute(one[middle:], "row", xor_pairs("row", 2)),
    ]
    return [[piece], [one], [two], far]


def swap(piece):
    return lax.ppermute(piece, "layer", xor_pairs("layer", 1))


def on_device(tasks, task_owner, task_slot, p_pattern, c_pattern, occupations):
    n_row, n_col, layers = (lax.axis_size(axis) for axis in ("row", "col", "layer"))
    owners = n_row * n_col
    count = tasks.shape[0]
    capacity = max(2, 2 * count // owners)
    places = owners * capacity
    block_rows, block_cols = p_pattern.shape
    part_rows = BLK // layers
    part = part_rows * BLK
    rows, cols = block_rows * part_rows, block_cols * BLK
    width = part + LANES
    layer = lax.axis_index("layer")

    paired = capacity % 16 == 0
    if paired:
        parcels = [(n_col * capacity, part // 2 + LANES)] * n_row
        parcels += [(n_row * capacity, part - part // 2)] * n_col
    else:
        parcels = [(places, width)]
    sent = pl.pallas_call(
        functools.partial(pack_kernel, owners, capacity, p_pattern.shape, paired),
        out_shape=[jax.ShapeDtypeStruct(shape, jnp.bfloat16) for shape in parcels],
        in_specs=[pl.BlockSpec(memory_space=pltpu.HBM), whole_ref(), whole_ref()],
        out_specs=[whole_ref()] * len(parcels),
        scratch_shapes=[pltpu.VMEM((count, part), jnp.bfloat16), pltpu.SemaphoreType.DMA],
        compiler_params=params(2 * (places + count) * width),
        cost_estimate=cost(2 * places * count * width, 2 * (places + count) * width),
        name="pack",
    )(tasks, task_owner.reshape(1, count), task_slot.reshape(1, count))
    if paired:
        got = list(exchange(sent[:n_row], sent[n_row:], capacity))
    else:
        got = [
            [
                lax.all_to_all(
                    sent[0].reshape(owners, capacity, width),
                    ("row", "col"),
                    split_axis=0,
                    concat_axis=0,
                    tiled=True,
                ).reshape(places, width)
            ]
        ] * 2

    slots_here = block_rows * block_cols
    half_shape = jax.ShapeDtypeStruct((block_rows, part_rows // 2, cols), jnp.bfloat16)
    piece_shape = jax.ShapeDtypeStruct((block_rows, part_rows, cols), jnp.bfloat16)
    marks_shape = jax.ShapeDtypeStruct((slots_here, places), jnp.bfloat16)

    def build(half, marks, *blocks):
        return pl.pallas_call(
            functools.partial(build_kernel, half, paired),
            out_shape=[piece_shape] * 2 if half else [marks_shape, half_shape, half_shape],
            in_specs=[whole_ref()] * (2 + len(blocks)),
            out_specs=[whole_ref()] * (2 if half else 3),
            scratch_shapes=[pltpu.VMEM((cols // LANES, rows // 2, LANES), jnp.float32)],
            compiler_params=params(2 * places * width + 8 * rows * cols),
            cost_estimate=cost(places * slots_here * part, places * width),
            name="build",
        )(occupations.reshape(1, block_rows * BLK), marks, *blocks)

    marks, *first_half = build(0, p_pattern, *got[0][::-1])
    density, ordered = build(1, marks, *got[1][::-1], *first_half)

    lefts = gather_line(ordered)
    mate = swap(density)
    pieces = gather(after(density, mate), "row")
    pieces[0] = density
    ahead = (lefts[1], lefts[n_col // 2])
    mates = [mate] + [swap(after(piece, *ahead)) for piece in pieces[1:]]
    flops = 2 * rows * cols * n_col * cols
    half_width = block_rows * BLK // layers
    panel_bytes = 2 * n_row * layers * rows * half_width
    sum_shape = jax.ShapeDtypeStruct((rows, cols), jnp.float32)
    other_shape = jax.ShapeDtypeStruct((n_row, rows, half_width), jnp.bfloat16)
    met_shape = jax.ShapeDtypeStruct((n_row // n_col, rows, cols), jnp.bfloat16)
    here = block_rows // layers
    give_shape = jax.ShapeDtypeStruct((n_col, here, part_rows, cols), jnp.bfloat16)
    partial, other, met, give = pl.pallas_call(
        functools.partial(near_square_kernel, n_col, n_row),
        out_shape=[sum_shape, other_shape, met_shape, give_shape],
        in_specs=[any_ref()] * (n_col - 1) + [whole_ref()] * n_row,
        out_specs=[whole_ref()] * 3 + [any_ref()],
        scratch_shapes=[
            pltpu.VMEM((n_row, layers, block_rows, part_rows, half_width), jnp.bfloat16),
            pltpu.SemaphoreType.DMA((n_row * layers + n_col,)),
        ],
        compiler_params=params(2 * panel_bytes + 16 * rows * cols),
        cost_estimate=cost(0, 0),
        name="near_square",
    )(*lefts[:-1], *pieces)
    square, give = pl.pallas_call(
        functools.partial(far_square_kernel, n_col, n_row),
        out_shape=[piece_shape, give_shape],
        in_specs=[whole_ref()] * (4 + n_row) + [any_ref()],
        out_specs=[whole_ref(), any_ref()],
        scratch_shapes=[pltpu.SemaphoreType.DMA],
        input_output_aliases={4 + n_row: 1},
        compiler_params=params(panel_bytes + 16 * rows * cols),
        cost_estimate=cost(0, 0),
        name="far_square",
    )(partial, other, met, *mates, lefts[-1], give)

    pieces = gather_square(square)
    mates = [[swap(part) for part in parts] for parts in pieces]
    if len(pieces[-1]) > 1:
        mates[1:3] = [[swap(after(pieces[shift][0], pieces[3 - shift][0]))] for shift in (1, 2)]
    received = swap(after(give, pieces[1][0], pieces[2][0]))
    sizes = [len(parts) for parts in pieces]
    pieces, mates = ([part for parts in held for part in parts] for held in (pieces, mates))
    partial, mask, other = pl.pallas_call(
        functools.partial(near_cube_kernel, n_col, sizes),
        out_shape=[
            sum_shape,
            jax.ShapeDtypeStruct((rows, cols), jnp.bfloat16),
            other_shape,
        ],
        in_specs=[any_ref()] * (n_col + 1) + [whole_ref()] * (2 + len(pieces)),
        out_specs=[whole_ref()] * 3,
        scratch_shapes=[
            pltpu.VMEM((n_row, layers, here, layers, part_rows, half_width), jnp.bfloat16),
            pltpu.VMEM((here, layers, part_rows, cols), jnp.bfloat16),
            pltpu.SemaphoreType.DMA((2 * n_row * layers,)),
        ],
        compiler_params=params(2 * panel_bytes + 16 * rows * cols),
        cost_estimate=cost(0, 0),
        name="near_cube",
    )(*lefts, received, c_pattern, *pieces, mates[0])
    return pl.pallas_call(
        functools.partial(far_cube_kernel, sizes),
        out_shape=sum_shape,
        in_specs=[whole_ref()] * (3 + len(mates)) + [any_ref()],
        out_specs=whole_ref(),
        compiler_params=params(16 * rows * cols),
        cost_estimate=cost(flops // 2, 4 * 1024 * 1024),
        name="far_cube",
    )(partial, mask, other, *mates, token(pieces[3:], HEAVY))


def solution(mesh):
    return jax.shard_map(
        on_device,
        mesh=mesh,
        in_specs=(
            P(("row", "col"), None),
            P(("row", "col"), None),
            P(("row", "col")),
            P("row", "col"),
            P("row", "col"),
            P("row"),
        ),
        out_specs=P(("row", "layer"), "col"),
        check_vma=False,
    )
```

```python
import functools

import jax
import jax.numpy as jnp
from jax import lax
from jax.experimental import pallas as pl
from jax.experimental.pallas import tpu as pltpu
from jax.sharding import PartitionSpec as P

BLK = 64
LANES = 128
PACK_VMEM = 52 * 1024 * 1024
HEAVY = 10**10
EARLY = 0
EXTRA = 0
LATE = 0


def params(held):
    return pltpu.CompilerParams(vmem_limit_bytes=held + 6 * 1024 * 1024)


def whole_ref():
    return pl.BlockSpec(memory_space=pltpu.VMEM)


def any_ref():
    return pl.BlockSpec(memory_space=pl.ANY)


def cost(flops, bytes_accessed):
    return pl.CostEstimate(flops=flops, bytes_accessed=bytes_accessed, transcendentals=0)


def pack_kernel(owners, capacity, block_shape, paired, tasks_ref, owner_hbm, slot_hbm, *refs):
    out_refs, (held, owner_ref, slot_ref, sems) = refs[:-4], refs[-4:]
    count, part = held.shape
    layer = lax.axis_index("layer")
    start = pl.multiple_of(layer * part, part)
    *small, copy = start_copies(
        [
            (owner_hbm, owner_ref),
            (slot_hbm, slot_ref),
            (tasks_ref.at[:, pl.ds(start, part)], held),
        ],
        sems,
    )
    for each in small:
        each.wait()
    block_rows, block_cols = block_shape
    slot_row = slot_ref[...]
    slot_row = lax.rem(slot_row, block_cols) * block_rows + lax.div(slot_row, block_cols)
    across = lax.broadcasted_iota(jnp.int32, (count, count), 1)
    down = lax.broadcasted_iota(jnp.int32, (count, count), 0)
    slot_col = jnp.sum(
        jnp.where(across == down, slot_row.astype(jnp.float32), 0.0), axis=1, keepdims=True
    )
    owner_row = owner_ref[...]
    if paired:
        owner_row = owner_row ^ (
            lax.axis_index("row") * lax.axis_size("col") + lax.axis_index("col")
        )
    same = (lax.broadcasted_iota(jnp.int32, (owners, count), 0) == owner_row).astype(jnp.float32)
    before = (down < across).astype(jnp.float32).astype(jnp.bfloat16)
    ahead = jnp.dot(same.astype(jnp.bfloat16), before, preferred_element_type=jnp.float32)
    placed = jnp.sum(ahead * same, axis=0, keepdims=True).astype(jnp.int32)
    target = owner_row * capacity + placed
    places = owners * capacity
    move = (
        (lax.broadcasted_iota(jnp.int32, (places, count), 0) == target)
        .astype(jnp.float32)
        .astype(jnp.bfloat16)
    )

    def put(at, end, blocks):
        moved = jnp.dot(move, blocks, preferred_element_type=jnp.float32).astype(jnp.bfloat16)
        if not paired:
            out_refs[0][:, at:end] = moved
            return
        n_row, n_col = lax.axis_size("row"), lax.axis_size("col")
        if at < part // 2 + LANES:
            each = n_col * capacity
            for down, out_ref in enumerate(out_refs[:n_row]):
                out_ref[:, at:end] = moved[down * each : (down + 1) * each]
            return
        at, end = at - (part // 2 + LANES), end - (part // 2 + LANES)
        for over, out_ref in enumerate(out_refs[n_row:]):
            for down in range(n_row):
                place = (down * n_col + over) * capacity
                out_ref[down * capacity : (down + 1) * capacity, at:end] = moved[
                    place : place + capacity
                ]

    slots = jnp.broadcast_to(slot_col, (count, LANES)).astype(jnp.bfloat16)
    put(0, LANES, slots)
    copy.wait()
    step = 512
    for at in range(0, part, step):
        put(LANES + at, LANES + at + step, held[:, at : at + step])


def mix_kernel(arrivals, capacity, *refs):
    for shift, out_ref in enumerate(refs[arrivals:], 1):
        for index, ref in enumerate(refs[:arrivals][::-1]):
            out_ref[index * capacity : (index + 1) * capacity, :] = ref[
                shift * capacity : (shift + 1) * capacity, :
            ]


def token_kernel(*refs):
    refs[-1][...] = jnp.zeros_like(refs[-1])


def build_kernel(half, paired, occ_ref, marks_ref, *refs):
    out_ref, sorted_ref, tall = refs[-3:]
    layers = lax.axis_size("layer")
    block_rows, cols = out_ref.shape[0], out_ref.shape[2]
    part_rows = BLK // layers // 2
    block_cols = cols // BLK
    rows = block_rows * part_rows
    part = part_rows * BLK
    front = 0
    if half:
        got_refs, before = refs[1 if paired else 0 : -5][::-1], refs[-5:-3]
        for ref, old_ref in zip((out_ref, sorted_ref), before):
            ref[:, :part_rows] = old_ref[...]
    else:
        got_refs, held_ref = refs[:-4][::-1], refs[-4]
        front = LANES

    def got(at, end):
        if not paired:
            skip = half * (LANES + part)
            return got_refs[0][:, skip + at : skip + end]
        n_row, n_col = lax.axis_size("row"), lax.axis_size("col")
        if half:
            capacity = got_refs[0].shape[0] // n_row
            parts = [ref[:capacity, at:end] for ref in got_refs[:n_col]]
            parts += [ref[:, at:end] for ref in got_refs[n_col:]]
        else:
            capacity = got_refs[0].shape[0] // n_col
            parts = []
            for down in range(n_row):
                place = slice(down * capacity, (down + 1) * capacity)
                parts.append(got_refs[down][:capacity, at:end])
                parts += [ref[place, at:end] for ref in got_refs[n_row:]]
        return jnp.concatenate(parts, axis=0)

    if half:
        marks = marks_ref[...]
    else:
        slots = got(0, LANES).astype(jnp.float32)
        lane = lax.broadcasted_iota(jnp.int32, slots.shape, 1).astype(jnp.float32)
        which = lax.broadcasted_iota(jnp.int32, (block_cols, LANES), 1)
        spread = lax.div(which, block_rows) == lax.broadcasted_iota(jnp.int32, which.shape, 0)
        which = lax.broadcasted_iota(jnp.int32, (block_rows, LANES), 1)
        here = lax.rem(which, block_rows) == lax.broadcasted_iota(jnp.int32, which.shape, 0)
        pattern = jnp.dot(
            marks_ref[...].astype(jnp.float32),
            spread.astype(jnp.float32),
            preferred_element_type=jnp.float32,
        )
        pattern = jnp.sum(jnp.where(here, pattern, 0.0), axis=0, keepdims=True)
        marks = jnp.where(slots == lane, pattern, 0.0)
        marks = marks.T[: block_rows * block_cols].astype(jnp.bfloat16)
        held_ref[...] = marks
    low = lax.broadcasted_iota(jnp.int32, (block_rows, LANES), 1) < BLK
    step = 256
    for at in range(0, part, step):
        summed = jnp.dot(
            marks, got(front + at, front + at + step), preferred_element_type=jnp.float32
        )
        for pair in range(step // LANES):
            lanes = slice(pair * LANES, (pair + 1) * LANES)
            row = (at // LANES + pair) * 2
            for twin in range(block_cols // 2):
                left = summed[twin * 2 * block_rows : (twin * 2 + 1) * block_rows, lanes]
                right = summed[(twin * 2 + 1) * block_rows : (twin * 2 + 2) * block_rows, lanes]
                tall[twin, pl.ds(row, block_rows, stride=part_rows), :] = jnp.where(
                    low, left, pltpu.roll(right, BLK, 1)
                )
                tall[twin, pl.ds(row + 1, block_rows, stride=part_rows), :] = jnp.where(
                    low, pltpu.roll(left, BLK, 1), right
                )
    tile_rows = block_rows * BLK
    row_here = (lax.axis_index("layer") * 2 + half) * part_rows
    row_start = lax.axis_index("row") * tile_rows + row_here
    col_start = lax.axis_index("col") * cols
    index = lax.broadcasted_iota(jnp.int32, (rows, LANES), 0)
    inside = lax.div(index, part_rows) * BLK + lax.rem(index, part_rows)
    row_id = row_start + inside
    lane = lax.broadcasted_iota(jnp.int32, (rows, LANES), 1)
    occ = jnp.zeros((rows, 1), jnp.float32)
    for at in range(0, tile_rows, LANES):
        mine = jnp.where(row_here + inside == at + lane, occ_ref[:, at : at + LANES], 0.0)
        occ = occ + jnp.sum(mine, axis=1, keepdims=True)
    values = []
    for twin in range(block_cols // 2):
        diagonal = jnp.where(row_id == col_start + twin * LANES + lane, occ, 0.0)
        values.append(tall[twin] + diagonal)
    here = slice(half * part_rows, (half + 1) * part_rows)

    def put(ref, at, value):
        ref[:, here, at : at + LANES] = value.astype(jnp.bfloat16).reshape(
            block_rows, part_rows, LANES
        )

    for twin, value in enumerate(values):
        put(out_ref, twin * LANES, value)
    quarter = LANES // 4
    spot = lax.div(lane, quarter)
    for twin in range(0, block_cols // 2, 2):
        first, second = values[twin], values[twin + 1]
        at = twin // (block_rows // 2) * tile_rows + twin % (block_rows // 2) // 2 * LANES
        back, ahead = pltpu.roll(first, 3 * quarter, 1), pltpu.roll(second, quarter, 1)
        far_back, far_ahead = pltpu.roll(first, 2 * quarter, 1), pltpu.roll(second, 2 * quarter, 1)
        put(
            sorted_ref,
            at,
            jnp.where(
                spot == 0, first, jnp.where(spot == 1, back, jnp.where(spot == 2, far_ahead, ahead))
            ),
        )
        put(
            sorted_ref,
            at + tile_rows // 2,
            jnp.where(
                spot == 0, back, jnp.where(spot == 1, far_back, jnp.where(spot == 2, ahead, second))
            ),
        )


def start_copies(pairs, sems):
    copies = [
        pltpu.make_async_copy(source, target, sems.at[index])
        for index, (source, target) in enumerate(pairs)
    ]
    for copy in copies:
        copy.start()
    return copies


def split(values, sizes):
    ends = [sum(sizes[: index + 1]) for index in range(len(sizes))]
    return [values[end - size : end] for end, size in zip(ends, sizes)]


def joined(parts):
    return flat(jnp.concatenate([part[...] for part in parts], axis=0))


def left_blocks(tile_rows, cols):
    width = tile_rows // 2
    return [
        (at // tile_rows, at % tile_rows // width, slice(at, at + width))
        for at in range(0, cols, width)
    ]


def flat(value):
    return value.reshape(-1, value.shape[-1])


def near_square_kernel(n_col, n_row, *refs):
    lefts, pieces = refs[: n_col - 1], refs[n_col - 1 : n_col - 1 + n_row]
    sum_ref, other_ref, met_ref, give_ref, left, sems = refs[n_col - 1 + n_row :]
    row, col, layer = (lax.axis_index(axis) for axis in ("row", "col", "layer"))
    cols = sum_ref.shape[1]
    per_col = n_row // n_col
    pairs = [
        (piece.at[:, :, lanes], left.at[(col ^ shift) * per_col + block, which])
        for shift, piece in enumerate(lefts)
        for block, which, lanes in left_blocks(cols // per_col, cols)
    ]
    inner = len(pairs)
    here = give_ref.shape[1]
    pairs += [
        (piece.at[pl.ds((1 - layer) * here, here)], give_ref.at[col ^ shift])
        for shift, piece in enumerate(lefts)
    ]
    copies = start_copies(pairs, sems)
    last = col ^ (n_col - 1)
    for block in range(per_col):
        left[last * per_col + block] = jnp.zeros(left.shape[1:], left.dtype)
    for shift in range(n_row):

        @pl.when(lax.div(row ^ shift, per_col) == last)
        def _(shift=shift):
            met_ref[lax.rem(row ^ shift, per_col)] = flat(pieces[shift][...])

    for copy in copies[:inner]:
        copy.wait()
    total = jnp.zeros(sum_ref.shape, jnp.float32)
    for shift in range(n_row):
        total = total + jnp.dot(
            flat(left[row ^ shift, layer]),
            flat(pieces[shift][...]),
            preferred_element_type=jnp.float32,
        )
        other_ref[shift] = flat(left[row ^ shift, 1 - layer])
    sum_ref[...] = total
    for copy in copies[inner:]:
        copy.wait()


def far_square_kernel(n_col, n_row, *refs):
    sum_ref, other_ref, met_ref = refs[:3]
    mates, left_ref = refs[3 : 3 + n_row], refs[3 + n_row]
    low_ref, give_ref, sem = refs[5 + n_row :]
    row, col, layer = (lax.axis_index(axis) for axis in ("row", "col", "layer"))
    here = give_ref.shape[1]
    copy = pltpu.make_async_copy(
        left_ref.at[pl.ds((1 - layer) * here, here)], give_ref.at[col ^ (n_col - 1)], sem
    )
    copy.start()
    per_col = met_ref.shape[0]
    width = other_ref.shape[2]

    def columns(block, which):
        start = pl.multiple_of((block * 2 + which) * width, width)
        return flat(left_ref[:, :, pl.ds(start, width)])

    total = sum_ref[...]
    for block in range(per_col):
        total = total + jnp.dot(
            columns(block, layer), met_ref[block], preferred_element_type=jnp.float32
        )
    for shift, mate in enumerate(mates):
        met = row ^ shift
        left = jnp.where(
            lax.div(met, per_col) == col ^ (n_col - 1),
            columns(lax.rem(met, per_col), 1 - layer),
            other_ref[shift],
        )
        total = total + jnp.dot(left, flat(mate[...]), preferred_element_type=jnp.float32)
    low_ref[...] = total.astype(jnp.bfloat16).reshape(low_ref.shape)
    copy.wait()


def near_cube_kernel(n_col, sizes, *refs):
    lefts, given, pattern_ref = refs[:n_col], refs[n_col], refs[n_col + 1]
    n_row, count = len(sizes), n_col + 2 + sum(sizes)
    pieces, mates = split(refs[n_col + 2 : count], sizes), refs[count : count + n_row - 1]
    sum_ref, mask_ref, other_ref, left, own, sems = refs[count + n_row - 1 :]
    row, col, layer = (lax.axis_index(axis) for axis in ("row", "col", "layer"))
    rows, cols = sum_ref.shape
    per_col = n_row // n_col
    here = given.shape[1]
    mine = pl.ds(layer * here, here)
    pairs = []
    for block, which, lanes in left_blocks(cols // per_col, cols):
        for shift, piece in enumerate(lefts):
            at = (col ^ shift) * per_col + block
            pairs.append((piece.at[mine, :, lanes], left.at[at, which, :, layer]))
            pairs.append(
                (given.at[col ^ shift, :, :, lanes], left.at[at, which, :, 1 - layer])
            )
    copies = start_copies(pairs, sems)
    own[:, layer] = pieces[0][0][mine]
    own[:, 1 - layer] = mates[0][mine]
    pattern = pattern_ref[...].astype(jnp.float32).astype(jnp.bfloat16)
    block_rows, block_cols = pattern.shape
    across = lax.broadcasted_iota(jnp.int32, (block_cols, cols), 1)
    which = lax.broadcasted_iota(jnp.int32, (block_cols, cols), 0)
    wide = (lax.div(across, BLK) == which).astype(jnp.float32).astype(jnp.bfloat16)
    down = lax.broadcasted_iota(jnp.int32, (rows, block_rows), 0) + layer * rows
    which = lax.broadcasted_iota(jnp.int32, (rows, block_rows), 1)
    tall = (lax.div(down, BLK) == which).astype(jnp.float32).astype(jnp.bfloat16)
    tall = jnp.dot(tall, pattern, preferred_element_type=jnp.float32).astype(jnp.bfloat16)
    mask = jnp.dot(tall, wide, preferred_element_type=jnp.float32)
    mask_ref[...] = mask.astype(jnp.bfloat16)
    total = 1.5 * flat(own[...]).astype(jnp.float32)
    for copy in copies:
        copy.wait()
    for shift in range(n_row):
        total = total - jnp.dot(
            flat(left[row ^ shift, layer]),
            joined(pieces[shift]),
            preferred_element_type=jnp.float32,
        )
    for shift, mate in enumerate(mates):
        total = total - jnp.dot(
            flat(left[row ^ shift, 1 - layer]),
            flat(mate[...]),
            preferred_element_type=jnp.float32,
        )
    other_ref[...] = flat(left[row ^ (n_row - 1), 1 - layer])
    sum_ref[...] = total


def far_cube_kernel(sum_ref, mask_ref, left_ref, *refs):
    mates, out_ref = refs[:-2], refs[-1]
    total = sum_ref[...] - jnp.dot(
        left_ref[...], joined(mates), preferred_element_type=jnp.float32
    )
    out_ref[...] = mask_ref[...].astype(jnp.float32) * (2.0 * total)


def xor_pairs(axis, shift):
    return [(i, i ^ shift) for i in range(lax.axis_size(axis))]


def gather(piece, axis):
    return [piece] + [
        lax.ppermute(piece, axis, xor_pairs(axis, shift))
        for shift in range(1, lax.axis_size(axis))
    ]


def exchange(first, second, capacity):
    def relay(parcels, out_axis, in_axis, weight):
        arrived = [parcels[0]] + [
            lax.ppermute(parcel, out_axis, xor_pairs(out_axis, shift))
            for shift, parcel in enumerate(parcels)
            if shift
        ]
        steps = lax.axis_size(in_axis)
        shape = (len(arrived) * capacity, parcels[0].shape[1])
        mixed = pl.pallas_call(
            functools.partial(mix_kernel, len(arrived), capacity),
            out_shape=[jax.ShapeDtypeStruct(shape, jnp.bfloat16)] * (steps - 1),
            in_specs=[whole_ref()] * len(arrived),
            out_specs=[whole_ref()] * (steps - 1),
            compiler_params=params(4 * steps * shape[0] * shape[1]),
            cost_estimate=cost(weight, 4 * steps * shape[0] * shape[1]),
            name="mix",
        )(*arrived[::-1])
        return arrived + [
            lax.ppermute(parcel, in_axis, xor_pairs(in_axis, shift))
            for shift, parcel in enumerate(mixed, 1)
        ]

    first = relay(first, "row", "col", EARLY)
    second = relay(second, "col", "row", LATE)
    return first, [*second, token(second, EXTRA)]


def after(value, *earlier):
    return lax.optimization_barrier((value, earlier))[0]


def token(values, weight):
    return pl.pallas_call(
        token_kernel,
        out_shape=jax.ShapeDtypeStruct((8, LANES), jnp.float32),
        in_specs=[any_ref()] * len(values),
        out_specs=whole_ref(),
        compiler_params=params(0),
        cost_estimate=cost(weight, 0),
        name="token",
    )(*values)


def gather_line(piece):
    count = lax.axis_size("col")
    pieces = {0: piece}
    step = count // 2
    while step:
        pieces |= {
            shift + step: lax.ppermute(held, "col", xor_pairs("col", step))
            for shift, held in pieces.items()
        }
        step //= 2
    return [pieces[shift] for shift in range(count)]


def gather_square(piece):
    if lax.axis_size("row") != 4:
        return [[held] for held in gather(piece, "row")]
    one, two = (lax.ppermute(piece, "row", xor_pairs("row", shift)) for shift in (1, 2))
    middle = piece.shape[0] // 2
    far = [
        lax.ppermute(two[:middle], "row", xor_pairs("row", 1)),
        lax.ppermute(one[middle:], "row", xor_pairs("row", 2)),
    ]
    return [[piece], [one], [two], far]


def swap(piece):
    return lax.ppermute(piece, "layer", xor_pairs("layer", 1))


def on_device(tasks, task_owner, task_slot, p_pattern, c_pattern, occupations):
    n_row, n_col, layers = (lax.axis_size(axis) for axis in ("row", "col", "layer"))
    owners = n_row * n_col
    count = tasks.shape[0]
    capacity = max(2, 2 * count // owners)
    places = owners * capacity
    block_rows, block_cols = p_pattern.shape
    part_rows = BLK // layers
    part = part_rows * BLK
    rows, cols = block_rows * part_rows, block_cols * BLK
    width = part + LANES
    layer = lax.axis_index("layer")

    paired = capacity % 16 == 0
    if paired:
        parcels = [(n_col * capacity, part // 2 + LANES)] * n_row
        parcels += [(n_row * capacity, part - part // 2)] * n_col
    else:
        parcels = [(places, width)]
    sent = pl.pallas_call(
        functools.partial(pack_kernel, owners, capacity, p_pattern.shape, paired),
        out_shape=[jax.ShapeDtypeStruct(shape, jnp.bfloat16) for shape in parcels],
        in_specs=[any_ref()] * 3,
        out_specs=[whole_ref()] * len(parcels),
        scratch_shapes=[
            pltpu.VMEM((count, part), jnp.bfloat16),
            pltpu.VMEM((1, count), jnp.int32),
            pltpu.VMEM((1, count), jnp.int32),
            pltpu.SemaphoreType.DMA((3,)),
        ],
        compiler_params=pltpu.CompilerParams(vmem_limit_bytes=PACK_VMEM),
        cost_estimate=cost(2 * places * count * width, 2 * (places + count) * width),
        name="pack",
    )(tasks, task_owner.reshape(1, count), task_slot.reshape(1, count))
    if paired:
        got = list(exchange(sent[:n_row], sent[n_row:], capacity))
    else:
        got = [
            [
                lax.all_to_all(
                    sent[0].reshape(owners, capacity, width),
                    ("row", "col"),
                    split_axis=0,
                    concat_axis=0,
                    tiled=True,
                ).reshape(places, width)
            ]
        ] * 2

    slots_here = block_rows * block_cols
    half_shape = jax.ShapeDtypeStruct((block_rows, part_rows // 2, cols), jnp.bfloat16)
    piece_shape = jax.ShapeDtypeStruct((block_rows, part_rows, cols), jnp.bfloat16)
    marks_shape = jax.ShapeDtypeStruct((slots_here, places), jnp.bfloat16)

    def build(half, marks, *blocks):
        return pl.pallas_call(
            functools.partial(build_kernel, half, paired),
            out_shape=[piece_shape] * 2 if half else [marks_shape, half_shape, half_shape],
            in_specs=[whole_ref()] * (2 + len(blocks)),
            out_specs=[whole_ref()] * (2 if half else 3),
            scratch_shapes=[pltpu.VMEM((cols // LANES, rows // 2, LANES), jnp.float32)],
            compiler_params=params(2 * places * width + 8 * rows * cols),
            cost_estimate=cost(places * slots_here * part, places * width),
            name="build",
        )(occupations.reshape(1, block_rows * BLK), marks, *blocks)

    marks, *first_half = build(0, p_pattern, *got[0][::-1])
    density, ordered = build(1, marks, *got[1][::-1], *first_half)

    lefts = gather_line(ordered)
    mate = swap(density)
    pieces = gather(after(density, mate), "row")
    pieces[0] = density
    ahead = (lefts[1], lefts[n_col // 2])
    mates = [mate] + [swap(after(piece, *ahead)) for piece in pieces[1:]]
    flops = 2 * rows * cols * n_col * cols
    half_width = block_rows * BLK // layers
    panel_bytes = 2 * n_row * layers * rows * half_width
    sum_shape = jax.ShapeDtypeStruct((rows, cols), jnp.float32)
    other_shape = jax.ShapeDtypeStruct((n_row, rows, half_width), jnp.bfloat16)
    met_shape = jax.ShapeDtypeStruct((n_row // n_col, rows, cols), jnp.bfloat16)
    here = block_rows // layers
    give_shape = jax.ShapeDtypeStruct((n_col, here, part_rows, cols), jnp.bfloat16)
    partial, other, met, give = pl.pallas_call(
        functools.partial(near_square_kernel, n_col, n_row),
        out_shape=[sum_shape, other_shape, met_shape, give_shape],
        in_specs=[any_ref()] * (n_col - 1) + [whole_ref()] * n_row,
        out_specs=[whole_ref()] * 3 + [any_ref()],
        scratch_shapes=[
            pltpu.VMEM((n_row, layers, block_rows, part_rows, half_width), jnp.bfloat16),
            pltpu.SemaphoreType.DMA((n_row * layers + n_col,)),
        ],
        compiler_params=params(2 * panel_bytes + 16 * rows * cols),
        cost_estimate=cost(0, 0),
        name="near_square",
    )(*lefts[:-1], *pieces)
    square, give = pl.pallas_call(
        functools.partial(far_square_kernel, n_col, n_row),
        out_shape=[piece_shape, give_shape],
        in_specs=[whole_ref()] * (4 + n_row) + [any_ref()],
        out_specs=[whole_ref(), any_ref()],
        scratch_shapes=[pltpu.SemaphoreType.DMA],
        input_output_aliases={4 + n_row: 1},
        compiler_params=params(panel_bytes + 16 * rows * cols),
        cost_estimate=cost(0, 0),
        name="far_square",
    )(partial, other, met, *mates, lefts[-1], give)

    pieces = gather_square(square)
    mates = [[swap(part) for part in parts] for parts in pieces]
    if len(pieces[-1]) > 1:
        mates[1:3] = [[swap(after(pieces[shift][0], pieces[3 - shift][0]))] for shift in (1, 2)]
    received = swap(after(give, pieces[1][0], pieces[2][0]))
    sizes = [len(parts) for parts in pieces]
    pieces, mates = ([part for parts in held for part in parts] for held in (pieces, mates))
    partial, mask, other = pl.pallas_call(
        functools.partial(near_cube_kernel, n_col, sizes),
        out_shape=[
            sum_shape,
            jax.ShapeDtypeStruct((rows, cols), jnp.bfloat16),
            jax.ShapeDtypeStruct((rows, half_width), jnp.bfloat16),
        ],
        in_specs=[any_ref()] * (n_col + 1) + [whole_ref()] * (n_row + len(pieces)),
        out_specs=[whole_ref()] * 3,
        scratch_shapes=[
            pltpu.VMEM((n_row, layers, here, layers, part_rows, half_width), jnp.bfloat16),
            pltpu.VMEM((here, layers, part_rows, cols), jnp.bfloat16),
            pltpu.SemaphoreType.DMA((2 * n_row * layers,)),
        ],
        compiler_params=params(2 * panel_bytes + 16 * rows * cols),
        cost_estimate=cost(0, 0),
        name="near_cube",
    )(*lefts, received, c_pattern, *pieces, *mates[: n_row - 1])
    return pl.pallas_call(
        far_cube_kernel,
        out_shape=sum_shape,
        in_specs=[whole_ref()] * (3 + sizes[-1]) + [any_ref()],
        out_specs=whole_ref(),
        compiler_params=params(16 * rows * cols),
        cost_estimate=cost(flops // 2, 4 * 1024 * 1024),
        name="far_cube",
    )(partial, mask, other, *mates[n_row - 1 :], token(pieces[n_row - 1 :], HEAVY))


def solution(mesh):
    return jax.shard_map(
        on_device,
        mesh=mesh,
        in_specs=(
            P(("row", "col"), None),
            P(("row", "col"), None),
            P(("row", "col")),
            P("row", "col"),
            P("row", "col"),
            P("row"),
        ),
        out_specs=P(("row", "layer"), "col"),
        check_vma=False,
    )
```

```python
import functools

import jax
import jax.numpy as jnp
from jax import lax
from jax.experimental import pallas as pl
from jax.experimental.pallas import tpu as pltpu
from jax.sharding import PartitionSpec as P

BLK = 64
LANES = 128
PACK_VMEM = 52 * 1024 * 1024
HEAVY = 10**10
EARLY = 0
EXTRA = 0
LATE = 0


def params(held):
    return pltpu.CompilerParams(vmem_limit_bytes=held + 6 * 1024 * 1024)


def whole_ref():
    return pl.BlockSpec(memory_space=pltpu.VMEM)


def any_ref():
    return pl.BlockSpec(memory_space=pl.ANY)


def cost(flops, bytes_accessed):
    return pl.CostEstimate(flops=flops, bytes_accessed=bytes_accessed, transcendentals=0)


def pack_kernel(owners, capacity, block_shape, paired, tasks_ref, owner_hbm, slot_hbm, *refs):
    out_refs, (held, owner_ref, slot_ref, sems) = refs[:-4], refs[-4:]
    count, part = held.shape
    layer = lax.axis_index("layer")
    start = pl.multiple_of(layer * part, part)
    *small, copy = start_copies(
        [
            (owner_hbm, owner_ref),
            (slot_hbm, slot_ref),
            (tasks_ref.at[:, pl.ds(start, part)], held),
        ],
        sems,
    )
    for each in small:
        each.wait()
    block_rows, block_cols = block_shape
    slot_row = slot_ref[...]
    slot_row = lax.rem(slot_row, block_cols) * block_rows + lax.div(slot_row, block_cols)
    across = lax.broadcasted_iota(jnp.int32, (count, count), 1)
    down = lax.broadcasted_iota(jnp.int32, (count, count), 0)
    slot_col = jnp.sum(
        jnp.where(across == down, slot_row.astype(jnp.float32), 0.0), axis=1, keepdims=True
    )
    owner_row = owner_ref[...]
    if paired:
        owner_row = owner_row ^ (
            lax.axis_index("row") * lax.axis_size("col") + lax.axis_index("col")
        )
    same = (lax.broadcasted_iota(jnp.int32, (owners, count), 0) == owner_row).astype(jnp.float32)
    before = (down < across).astype(jnp.float32).astype(jnp.bfloat16)
    ahead = jnp.dot(same.astype(jnp.bfloat16), before, preferred_element_type=jnp.float32)
    placed = jnp.sum(ahead * same, axis=0, keepdims=True).astype(jnp.int32)
    target = owner_row * capacity + placed
    places = owners * capacity
    move = (
        (lax.broadcasted_iota(jnp.int32, (places, count), 0) == target)
        .astype(jnp.float32)
        .astype(jnp.bfloat16)
    )

    def put(at, end, blocks):
        moved = jnp.dot(move, blocks, preferred_element_type=jnp.float32).astype(jnp.bfloat16)
        if not paired:
            out_refs[0][:, at:end] = moved
            return
        n_row, n_col = lax.axis_size("row"), lax.axis_size("col")
        if at < part // 2 + LANES:
            each = n_col * capacity
            for down, out_ref in enumerate(out_refs[:n_row]):
                out_ref[:, at:end] = moved[down * each : (down + 1) * each]
            return
        at, end = at - (part // 2 + LANES), end - (part // 2 + LANES)
        for over, out_ref in enumerate(out_refs[n_row:]):
            for down in range(n_row):
                place = (down * n_col + over) * capacity
                out_ref[down * capacity : (down + 1) * capacity, at:end] = moved[
                    place : place + capacity
                ]

    slots = jnp.broadcast_to(slot_col, (count, LANES)).astype(jnp.bfloat16)
    put(0, LANES, slots)
    copy.wait()
    step = 512
    for at in range(0, part, step):
        put(LANES + at, LANES + at + step, held[:, at : at + step])


def mix_kernel(arrivals, capacity, *refs):
    for shift, out_ref in enumerate(refs[arrivals:], 1):
        for index, ref in enumerate(refs[:arrivals][::-1]):
            out_ref[index * capacity : (index + 1) * capacity, :] = ref[
                shift * capacity : (shift + 1) * capacity, :
            ]


def token_kernel(*refs):
    refs[-1][...] = jnp.zeros_like(refs[-1])


def build_kernel(half, paired, occ_ref, marks_ref, *refs):
    out_ref, sorted_ref, tall = refs[-3:]
    layers = lax.axis_size("layer")
    block_rows, cols = out_ref.shape[0], out_ref.shape[2]
    part_rows = BLK // layers // 2
    block_cols = cols // BLK
    rows = block_rows * part_rows
    part = part_rows * BLK
    front = 0
    if half:
        got_refs, before = refs[1 if paired else 0 : -5][::-1], refs[-5:-3]
        for ref, old_ref in zip((out_ref, sorted_ref), before):
            ref[:, :part_rows] = old_ref[...]
    else:
        got_refs, held_ref = refs[:-4][::-1], refs[-4]
        front = LANES

    def got(at, end):
        if not paired:
            skip = half * (LANES + part)
            return got_refs[0][:, skip + at : skip + end]
        n_row, n_col = lax.axis_size("row"), lax.axis_size("col")
        if half:
            capacity = got_refs[0].shape[0] // n_row
            parts = [ref[:capacity, at:end] for ref in got_refs[:n_col]]
            parts += [ref[:, at:end] for ref in got_refs[n_col:]]
        else:
            capacity = got_refs[0].shape[0] // n_col
            parts = []
            for down in range(n_row):
                place = slice(down * capacity, (down + 1) * capacity)
                parts.append(got_refs[down][:capacity, at:end])
                parts += [ref[place, at:end] for ref in got_refs[n_row:]]
        return jnp.concatenate(parts, axis=0)

    if half:
        marks = marks_ref[...]
    else:
        slots = got(0, LANES).astype(jnp.float32)
        lane = lax.broadcasted_iota(jnp.int32, slots.shape, 1).astype(jnp.float32)
        which = lax.broadcasted_iota(jnp.int32, (block_cols, LANES), 1)
        spread = lax.div(which, block_rows) == lax.broadcasted_iota(jnp.int32, which.shape, 0)
        which = lax.broadcasted_iota(jnp.int32, (block_rows, LANES), 1)
        here = lax.rem(which, block_rows) == lax.broadcasted_iota(jnp.int32, which.shape, 0)
        pattern = jnp.dot(
            marks_ref[...].astype(jnp.float32),
            spread.astype(jnp.float32),
            preferred_element_type=jnp.float32,
        )
        pattern = jnp.sum(jnp.where(here, pattern, 0.0), axis=0, keepdims=True)
        marks = jnp.where(slots == lane, pattern, 0.0)
        marks = marks.T[: block_rows * block_cols].astype(jnp.bfloat16)
        held_ref[...] = marks
    low = lax.broadcasted_iota(jnp.int32, (block_rows, LANES), 1) < BLK
    step = 256
    for at in range(0, part, step):
        summed = jnp.dot(
            marks, got(front + at, front + at + step), preferred_element_type=jnp.float32
        )
        for pair in range(step // LANES):
            lanes = slice(pair * LANES, (pair + 1) * LANES)
            row = (at // LANES + pair) * 2
            for twin in range(block_cols // 2):
                left = summed[twin * 2 * block_rows : (twin * 2 + 1) * block_rows, lanes]
                right = summed[(twin * 2 + 1) * block_rows : (twin * 2 + 2) * block_rows, lanes]
                tall[twin, pl.ds(row, block_rows, stride=part_rows), :] = jnp.where(
                    low, left, pltpu.roll(right, BLK, 1)
                )
                tall[twin, pl.ds(row + 1, block_rows, stride=part_rows), :] = jnp.where(
                    low, pltpu.roll(left, BLK, 1), right
                )
    tile_rows = block_rows * BLK
    row_here = (lax.axis_index("layer") * 2 + half) * part_rows
    row_start = lax.axis_index("row") * tile_rows + row_here
    col_start = lax.axis_index("col") * cols
    index = lax.broadcasted_iota(jnp.int32, (rows, LANES), 0)
    inside = lax.div(index, part_rows) * BLK + lax.rem(index, part_rows)
    row_id = row_start + inside
    lane = lax.broadcasted_iota(jnp.int32, (rows, LANES), 1)
    occ = jnp.zeros((rows, 1), jnp.float32)
    for at in range(0, tile_rows, LANES):
        mine = jnp.where(row_here + inside == at + lane, occ_ref[:, at : at + LANES], 0.0)
        occ = occ + jnp.sum(mine, axis=1, keepdims=True)
    values = []
    for twin in range(block_cols // 2):
        diagonal = jnp.where(row_id == col_start + twin * LANES + lane, occ, 0.0)
        values.append(tall[twin] + diagonal)
    here = slice(half * part_rows, (half + 1) * part_rows)

    def put(ref, at, value):
        ref[:, here, at : at + LANES] = value.astype(jnp.bfloat16).reshape(
            block_rows, part_rows, LANES
        )

    for twin, value in enumerate(values):
        put(out_ref, twin * LANES, value)
    quarter = LANES // 4
    spot = lax.div(lane, quarter)
    for twin in range(0, block_cols // 2, 2):
        first, second = values[twin], values[twin + 1]
        at = twin // (block_rows // 2) * tile_rows + twin % (block_rows // 2) // 2 * LANES
        back, ahead = pltpu.roll(first, 3 * quarter, 1), pltpu.roll(second, quarter, 1)
        far_back, far_ahead = pltpu.roll(first, 2 * quarter, 1), pltpu.roll(second, 2 * quarter, 1)
        put(
            sorted_ref,
            at,
            jnp.where(
                spot == 0, first, jnp.where(spot == 1, back, jnp.where(spot == 2, far_ahead, ahead))
            ),
        )
        put(
            sorted_ref,
            at + tile_rows // 2,
            jnp.where(
                spot == 0, back, jnp.where(spot == 1, far_back, jnp.where(spot == 2, ahead, second))
            ),
        )


def start_copies(pairs, sems):
    copies = [
        pltpu.make_async_copy(source, target, sems.at[index])
        for index, (source, target) in enumerate(pairs)
    ]
    for copy in copies:
        copy.start()
    return copies


def split(values, sizes):
    ends = [sum(sizes[: index + 1]) for index in range(len(sizes))]
    return [values[end - size : end] for end, size in zip(ends, sizes)]


def joined(parts):
    return flat(jnp.concatenate([part[...] for part in parts], axis=0))


def left_blocks(tile_rows, cols):
    width = tile_rows // 2
    return [
        (at // tile_rows, at % tile_rows // width, slice(at, at + width))
        for at in range(0, cols, width)
    ]


def flat(value):
    return value.reshape(-1, value.shape[-1])


def near_square_kernel(n_col, n_row, *refs):
    lefts, pieces = refs[: n_col - 1], refs[n_col - 1 : n_col - 1 + n_row]
    sum_ref, other_ref, met_ref, give_ref, left, sems = refs[n_col - 1 + n_row :]
    row, col, layer = (lax.axis_index(axis) for axis in ("row", "col", "layer"))
    cols = sum_ref.shape[1]
    per_col = n_row // n_col
    pairs = [
        (piece.at[:, :, lanes], left.at[(col ^ shift) * per_col + block, which])
        for shift, piece in enumerate(lefts)
        for block, which, lanes in left_blocks(cols // per_col, cols)
    ]
    inner = len(pairs)
    here = give_ref.shape[1]
    pairs += [
        (piece.at[pl.ds((1 - layer) * here, here)], give_ref.at[col ^ shift])
        for shift, piece in enumerate(lefts)
    ]
    copies = start_copies(pairs, sems)
    last = col ^ (n_col - 1)
    for block in range(per_col):
        left[last * per_col + block] = jnp.zeros(left.shape[1:], left.dtype)
    for shift in range(n_row):

        @pl.when(lax.div(row ^ shift, per_col) == last)
        def _(shift=shift):
            met_ref[lax.rem(row ^ shift, per_col)] = flat(pieces[shift][...])

    for copy in copies[:inner]:
        copy.wait()
    total = jnp.zeros(sum_ref.shape, jnp.float32)
    for shift in range(n_row):
        total = total + jnp.dot(
            flat(left[row ^ shift, layer]),
            flat(pieces[shift][...]),
            preferred_element_type=jnp.float32,
        )
        other_ref[shift] = flat(left[row ^ shift, 1 - layer])
    sum_ref[...] = total
    for copy in copies[inner:]:
        copy.wait()


def far_square_kernel(n_col, n_row, *refs):
    sum_ref, other_ref, met_ref = refs[:3]
    mates, left_ref = refs[3 : 3 + n_row], refs[3 + n_row]
    low_ref, give_ref, sem = refs[5 + n_row :]
    row, col, layer = (lax.axis_index(axis) for axis in ("row", "col", "layer"))
    here = give_ref.shape[1]
    copy = pltpu.make_async_copy(
        left_ref.at[pl.ds((1 - layer) * here, here)], give_ref.at[col ^ (n_col - 1)], sem
    )
    copy.start()
    per_col = met_ref.shape[0]
    width = other_ref.shape[2]

    def columns(block, which):
        start = pl.multiple_of((block * 2 + which) * width, width)
        return flat(left_ref[:, :, pl.ds(start, width)])

    total = sum_ref[...]
    for block in range(per_col):
        total = total + jnp.dot(
            columns(block, layer), met_ref[block], preferred_element_type=jnp.float32
        )
    for shift, mate in enumerate(mates):
        met = row ^ shift
        left = jnp.where(
            lax.div(met, per_col) == col ^ (n_col - 1),
            columns(lax.rem(met, per_col), 1 - layer),
            other_ref[shift],
        )
        total = total + jnp.dot(left, flat(mate[...]), preferred_element_type=jnp.float32)
    low_ref[...] = total.astype(jnp.bfloat16).reshape(low_ref.shape)
    copy.wait()


def near_cube_kernel(n_col, sizes, *refs):
    lefts, given, pattern_ref = refs[:n_col], refs[n_col], refs[n_col + 1]
    n_row, count = len(sizes), n_col + 2 + sum(sizes)
    pieces, mates = split(refs[n_col + 2 : count], sizes), refs[count : count + n_row - 1]
    sum_ref, mask_ref, other_ref, left, own, sems = refs[count + n_row - 1 :]
    row, col, layer = (lax.axis_index(axis) for axis in ("row", "col", "layer"))
    rows, cols = sum_ref.shape
    per_col = n_row // n_col
    here = given.shape[1]
    mine = pl.ds(layer * here, here)
    pairs = []
    for block, which, lanes in left_blocks(cols // per_col, cols):
        for shift, piece in enumerate(lefts):
            at = (col ^ shift) * per_col + block
            pairs.append((piece.at[mine, :, lanes], left.at[at, which, :, layer]))
            pairs.append(
                (given.at[col ^ shift, :, :, lanes], left.at[at, which, :, 1 - layer])
            )
    copies = start_copies(pairs, sems)
    own[:, layer] = pieces[0][0][mine]
    own[:, 1 - layer] = mates[0][mine]
    pattern = pattern_ref[...].astype(jnp.float32).astype(jnp.bfloat16)
    block_rows, block_cols = pattern.shape
    across = lax.broadcasted_iota(jnp.int32, (block_cols, cols), 1)
    which = lax.broadcasted_iota(jnp.int32, (block_cols, cols), 0)
    wide = (lax.div(across, BLK) == which).astype(jnp.float32).astype(jnp.bfloat16)
    down = lax.broadcasted_iota(jnp.int32, (rows, block_rows), 0) + layer * rows
    which = lax.broadcasted_iota(jnp.int32, (rows, block_rows), 1)
    tall = (lax.div(down, BLK) == which).astype(jnp.float32).astype(jnp.bfloat16)
    tall = jnp.dot(tall, pattern, preferred_element_type=jnp.float32).astype(jnp.bfloat16)
    mask = jnp.dot(tall, wide, preferred_element_type=jnp.float32)
    mask_ref[...] = mask.astype(jnp.bfloat16)
    total = 1.5 * flat(own[...]).astype(jnp.float32)
    for copy in copies:
        copy.wait()
    for shift in range(n_row):
        total = total - jnp.dot(
            flat(left[row ^ shift, layer]),
            joined(pieces[shift]),
            preferred_element_type=jnp.float32,
        )
    for shift, mate in enumerate(mates):
        total = total - jnp.dot(
            flat(left[row ^ shift, 1 - layer]),
            flat(mate[...]),
            preferred_element_type=jnp.float32,
        )
    other_ref[...] = flat(left[row ^ (n_row - 1), 1 - layer])
    sum_ref[...] = total


def far_cube_kernel(sum_ref, mask_ref, left_ref, *refs):
    mates, out_ref = refs[:-2], refs[-1]
    total = sum_ref[...] - jnp.dot(
        left_ref[...], joined(mates), preferred_element_type=jnp.float32
    )
    out_ref[...] = mask_ref[...].astype(jnp.float32) * (2.0 * total)


def xor_pairs(axis, shift):
    return [(i, i ^ shift) for i in range(lax.axis_size(axis))]


def gather(piece, axis):
    return [piece] + [
        lax.ppermute(piece, axis, xor_pairs(axis, shift))
        for shift in range(1, lax.axis_size(axis))
    ]


def exchange(first, second, capacity):
    def relay(parcels, out_axis, in_axis, weight):
        arrived = [parcels[0]] + [
            lax.ppermute(parcel, out_axis, xor_pairs(out_axis, shift))
            for shift, parcel in enumerate(parcels)
            if shift
        ]
        steps = lax.axis_size(in_axis)
        shape = (len(arrived) * capacity, parcels[0].shape[1])
        mixed = pl.pallas_call(
            functools.partial(mix_kernel, len(arrived), capacity),
            out_shape=[jax.ShapeDtypeStruct(shape, jnp.bfloat16)] * (steps - 1),
            in_specs=[whole_ref()] * len(arrived),
            out_specs=[whole_ref()] * (steps - 1),
            compiler_params=params(4 * steps * shape[0] * shape[1]),
            cost_estimate=cost(weight, 4 * steps * shape[0] * shape[1]),
            name="mix",
        )(*arrived[::-1])
        return arrived + [
            lax.ppermute(parcel, in_axis, xor_pairs(in_axis, shift))
            for shift, parcel in enumerate(mixed, 1)
        ]

    first = relay(first, "row", "col", EARLY)
    second = relay(second, "col", "row", LATE)
    return first, [*second, token(second, EXTRA)]


def after(value, *earlier):
    return lax.optimization_barrier((value, earlier))[0]


def token(values, weight):
    return pl.pallas_call(
        token_kernel,
        out_shape=jax.ShapeDtypeStruct((8, LANES), jnp.float32),
        in_specs=[any_ref()] * len(values),
        out_specs=whole_ref(),
        compiler_params=params(0),
        cost_estimate=cost(weight, 0),
        name="token",
    )(*values)


def gather_line(piece):
    count = lax.axis_size("col")
    pieces = {0: piece}
    step = count // 2
    while step:
        pieces |= {
            shift + step: lax.ppermute(held, "col", xor_pairs("col", step))
            for shift, held in pieces.items()
        }
        step //= 2
    return [pieces[shift] for shift in range(count)]


def gather_square(piece):
    if lax.axis_size("row") != 4:
        return [[held] for held in gather(piece, "row")]
    one, two = (lax.ppermute(piece, "row", xor_pairs("row", shift)) for shift in (1, 2))
    middle = piece.shape[0] // 2
    far = [
        lax.ppermute(two[:middle], "row", xor_pairs("row", 1)),
        lax.ppermute(one[middle:], "row", xor_pairs("row", 2)),
    ]
    return [[piece], [one], [two], far]


def swap(piece):
    return lax.ppermute(piece, "layer", xor_pairs("layer", 1))


def on_device(tasks, task_owner, task_slot, p_pattern, c_pattern, occupations):
    n_row, n_col, layers = (lax.axis_size(axis) for axis in ("row", "col", "layer"))
    owners = n_row * n_col
    count = tasks.shape[0]
    capacity = max(2, 2 * count // owners)
    places = owners * capacity
    block_rows, block_cols = p_pattern.shape
    part_rows = BLK // layers
    part = part_rows * BLK
    rows, cols = block_rows * part_rows, block_cols * BLK
    width = part + LANES
    layer = lax.axis_index("layer")

    paired = capacity % 16 == 0
    if paired:
        parcels = [(n_col * capacity, part // 2 + LANES)] * n_row
        parcels += [(n_row * capacity, part - part // 2)] * n_col
    else:
        parcels = [(places, width)]
    sent = pl.pallas_call(
        functools.partial(pack_kernel, owners, capacity, p_pattern.shape, paired),
        out_shape=[jax.ShapeDtypeStruct(shape, jnp.bfloat16) for shape in parcels],
        in_specs=[any_ref()] * 3,
        out_specs=[whole_ref()] * len(parcels),
        scratch_shapes=[
            pltpu.VMEM((count, part), jnp.bfloat16),
            pltpu.VMEM((1, count), jnp.int32),
            pltpu.VMEM((1, count), jnp.int32),
            pltpu.SemaphoreType.DMA((3,)),
        ],
        compiler_params=pltpu.CompilerParams(vmem_limit_bytes=PACK_VMEM),
        cost_estimate=cost(2 * places * count * width, 2 * (places + count) * width),
        name="pack",
    )(tasks, task_owner.reshape(1, count), task_slot.reshape(1, count))
    if paired:
        got = list(exchange(sent[:n_row], sent[n_row:], capacity))
    else:
        got = [
            [
                lax.all_to_all(
                    sent[0].reshape(owners, capacity, width),
                    ("row", "col"),
                    split_axis=0,
                    concat_axis=0,
                    tiled=True,
                ).reshape(places, width)
            ]
        ] * 2

    slots_here = block_rows * block_cols
    half_shape = jax.ShapeDtypeStruct((block_rows, part_rows // 2, cols), jnp.bfloat16)
    piece_shape = jax.ShapeDtypeStruct((block_rows, part_rows, cols), jnp.bfloat16)
    marks_shape = jax.ShapeDtypeStruct((slots_here, places), jnp.bfloat16)

    def build(half, marks, *blocks):
        return pl.pallas_call(
            functools.partial(build_kernel, half, paired),
            out_shape=[piece_shape] * 2 if half else [marks_shape, half_shape, half_shape],
            in_specs=[whole_ref()] * (2 + len(blocks)),
            out_specs=[whole_ref()] * (2 if half else 3),
            scratch_shapes=[pltpu.VMEM((cols // LANES, rows // 2, LANES), jnp.float32)],
            compiler_params=params(2 * places * width + 8 * rows * cols),
            cost_estimate=cost(places * slots_here * part, places * width),
            name="build",
        )(occupations.reshape(1, block_rows * BLK), marks, *blocks)

    marks, *first_half = build(0, p_pattern, *got[0][::-1])
    density, ordered = build(1, marks, *got[1][::-1], *first_half)

    lefts = gather_line(ordered)
    mate = swap(density)
    pieces = gather(after(density, mate), "row")
    pieces[0] = density
    ahead = (lefts[n_col // 2],)
    mates = [mate] + [swap(after(piece, *ahead)) for piece in pieces[1:]]
    flops = 2 * rows * cols * n_col * cols
    half_width = block_rows * BLK // layers
    panel_bytes = 2 * n_row * layers * rows * half_width
    sum_shape = jax.ShapeDtypeStruct((rows, cols), jnp.float32)
    other_shape = jax.ShapeDtypeStruct((n_row, rows, half_width), jnp.bfloat16)
    met_shape = jax.ShapeDtypeStruct((n_row // n_col, rows, cols), jnp.bfloat16)
    here = block_rows // layers
    give_shape = jax.ShapeDtypeStruct((n_col, here, part_rows, cols), jnp.bfloat16)
    partial, other, met, give = pl.pallas_call(
        functools.partial(near_square_kernel, n_col, n_row),
        out_shape=[sum_shape, other_shape, met_shape, give_shape],
        in_specs=[any_ref()] * (n_col - 1) + [whole_ref()] * n_row,
        out_specs=[whole_ref()] * 3 + [any_ref()],
        scratch_shapes=[
            pltpu.VMEM((n_row, layers, block_rows, part_rows, half_width), jnp.bfloat16),
            pltpu.SemaphoreType.DMA((n_row * layers + n_col,)),
        ],
        compiler_params=params(2 * panel_bytes + 16 * rows * cols),
        cost_estimate=cost(0, 0),
        name="near_square",
    )(*lefts[:-1], *pieces)
    square, give = pl.pallas_call(
        functools.partial(far_square_kernel, n_col, n_row),
        out_shape=[piece_shape, give_shape],
        in_specs=[whole_ref()] * (4 + n_row) + [any_ref()],
        out_specs=[whole_ref(), any_ref()],
        scratch_shapes=[pltpu.SemaphoreType.DMA],
        input_output_aliases={4 + n_row: 1},
        compiler_params=params(panel_bytes + 16 * rows * cols),
        cost_estimate=cost(0, 0),
        name="far_square",
    )(partial, other, met, *mates, lefts[-1], give)

    pieces = gather_square(square)
    mates = [[swap(part) for part in parts] for parts in pieces]
    if len(pieces[-1]) > 1:
        mates[1:3] = [[swap(after(pieces[shift][0], pieces[3 - shift][0]))] for shift in (1, 2)]
    received = swap(after(give, pieces[1][0], pieces[2][0]))
    sizes = [len(parts) for parts in pieces]
    pieces, mates = ([part for parts in held for part in parts] for held in (pieces, mates))
    partial, mask, other = pl.pallas_call(
        functools.partial(near_cube_kernel, n_col, sizes),
        out_shape=[
            sum_shape,
            jax.ShapeDtypeStruct((rows, cols), jnp.bfloat16),
            jax.ShapeDtypeStruct((rows, half_width), jnp.bfloat16),
        ],
        in_specs=[any_ref()] * (n_col + 1) + [whole_ref()] * (n_row + len(pieces)),
        out_specs=[whole_ref()] * 3,
        scratch_shapes=[
            pltpu.VMEM((n_row, layers, here, layers, part_rows, half_width), jnp.bfloat16),
            pltpu.VMEM((here, layers, part_rows, cols), jnp.bfloat16),
            pltpu.SemaphoreType.DMA((2 * n_row * layers,)),
        ],
        compiler_params=params(2 * panel_bytes + 16 * rows * cols),
        cost_estimate=cost(0, 0),
        name="near_cube",
    )(*lefts, received, c_pattern, *pieces, *mates[: n_row - 1])
    return pl.pallas_call(
        far_cube_kernel,
        out_shape=sum_shape,
        in_specs=[whole_ref()] * (3 + sizes[-1]) + [any_ref()],
        out_specs=whole_ref(),
        compiler_params=params(16 * rows * cols),
        cost_estimate=cost(flops // 2, 4 * 1024 * 1024),
        name="far_cube",
    )(partial, mask, other, *mates[n_row - 1 :], token(pieces[n_row - 1 :], HEAVY))


def solution(mesh):
    return jax.shard_map(
        on_device,
        mesh=mesh,
        in_specs=(
            P(("row", "col"), None),
            P(("row", "col"), None),
            P(("row", "col")),
            P("row", "col"),
            P("row", "col"),
            P("row"),
        ),
        out_specs=P(("row", "layer"), "col"),
        check_vma=False,
    )
```

```python
import functools

import jax
import jax.numpy as jnp
from jax import lax
from jax.experimental import pallas as pl
from jax.experimental.pallas import tpu as pltpu
from jax.sharding import PartitionSpec as P

BLK = 64
LANES = 128
PACK_VMEM = 52 * 1024 * 1024
HEAVY = 10**10
GIVE = 0
EARLY = 0
EXTRA = 0
LATE = 0


def params(held):
    return pltpu.CompilerParams(vmem_limit_bytes=held + 6 * 1024 * 1024)


def whole_ref():
    return pl.BlockSpec(memory_space=pltpu.VMEM)


def any_ref():
    return pl.BlockSpec(memory_space=pl.ANY)


def cost(flops, bytes_accessed):
    return pl.CostEstimate(flops=flops, bytes_accessed=bytes_accessed, transcendentals=0)


def pack_kernel(owners, capacity, block_shape, paired, tasks_ref, owner_hbm, slot_hbm, *refs):
    out_refs, (held, owner_ref, slot_ref, sems) = refs[:-4], refs[-4:]
    count, part = held.shape
    layer = lax.axis_index("layer")
    start = pl.multiple_of(layer * part, part)
    *small, copy = start_copies(
        [
            (owner_hbm, owner_ref),
            (slot_hbm, slot_ref),
            (tasks_ref.at[:, pl.ds(start, part)], held),
        ],
        sems,
    )
    for each in small:
        each.wait()
    block_rows, block_cols = block_shape
    slot_row = slot_ref[...]
    slot_row = lax.rem(slot_row, block_cols) * block_rows + lax.div(slot_row, block_cols)
    across = lax.broadcasted_iota(jnp.int32, (count, count), 1)
    down = lax.broadcasted_iota(jnp.int32, (count, count), 0)
    slot_col = jnp.sum(
        jnp.where(across == down, slot_row.astype(jnp.float32), 0.0), axis=1, keepdims=True
    )
    owner_row = owner_ref[...]
    if paired:
        owner_row = owner_row ^ (
            lax.axis_index("row") * lax.axis_size("col") + lax.axis_index("col")
        )
    same = (lax.broadcasted_iota(jnp.int32, (owners, count), 0) == owner_row).astype(jnp.float32)
    before = (down < across).astype(jnp.float32).astype(jnp.bfloat16)
    ahead = jnp.dot(same.astype(jnp.bfloat16), before, preferred_element_type=jnp.float32)
    placed = jnp.sum(ahead * same, axis=0, keepdims=True).astype(jnp.int32)
    target = owner_row * capacity + placed
    places = owners * capacity
    move = (
        (lax.broadcasted_iota(jnp.int32, (places, count), 0) == target)
        .astype(jnp.float32)
        .astype(jnp.bfloat16)
    )

    def put(at, end, blocks):
        moved = jnp.dot(move, blocks, preferred_element_type=jnp.float32).astype(jnp.bfloat16)
        if not paired:
            out_refs[0][:, at:end] = moved
            return
        n_row, n_col = lax.axis_size("row"), lax.axis_size("col")
        if at < part // 2 + LANES:
            each = n_col * capacity
            for down, out_ref in enumerate(out_refs[:n_row]):
                out_ref[:, at:end] = moved[down * each : (down + 1) * each]
            return
        at, end = at - (part // 2 + LANES), end - (part // 2 + LANES)
        for over, out_ref in enumerate(out_refs[n_row:]):
            for down in range(n_row):
                place = (down * n_col + over) * capacity
                out_ref[down * capacity : (down + 1) * capacity, at:end] = moved[
                    place : place + capacity
                ]

    slots = jnp.broadcast_to(slot_col, (count, LANES)).astype(jnp.bfloat16)
    put(0, LANES, slots)
    copy.wait()
    step = 512
    for at in range(0, part, step):
        put(LANES + at, LANES + at + step, held[:, at : at + step])


def mix_kernel(arrivals, capacity, *refs):
    for shift, out_ref in enumerate(refs[arrivals:], 1):
        for index, ref in enumerate(refs[:arrivals][::-1]):
            out_ref[index * capacity : (index + 1) * capacity, :] = ref[
                shift * capacity : (shift + 1) * capacity, :
            ]


def token_kernel(*refs):
    refs[-1][...] = jnp.zeros_like(refs[-1])


def build_kernel(half, paired, occ_ref, marks_ref, *refs):
    out_ref, sorted_ref, tall = refs[-3:]
    layers = lax.axis_size("layer")
    block_rows, cols = out_ref.shape[0], out_ref.shape[2]
    part_rows = BLK // layers // 2
    block_cols = cols // BLK
    rows = block_rows * part_rows
    part = part_rows * BLK
    front = 0
    if half:
        got_refs, before = refs[1 if paired else 0 : -5][::-1], refs[-5:-3]
        for ref, old_ref in zip((out_ref, sorted_ref), before):
            ref[:, :part_rows] = old_ref[...]
    else:
        got_refs, held_ref = refs[:-4][::-1], refs[-4]
        front = LANES

    def got(at, end):
        if not paired:
            skip = half * (LANES + part)
            return got_refs[0][:, skip + at : skip + end]
        n_row, n_col = lax.axis_size("row"), lax.axis_size("col")
        if half:
            capacity = got_refs[0].shape[0] // n_row
            parts = [ref[:capacity, at:end] for ref in got_refs[:n_col]]
            parts += [ref[:, at:end] for ref in got_refs[n_col:]]
        else:
            capacity = got_refs[0].shape[0] // n_col
            parts = []
            for down in range(n_row):
                place = slice(down * capacity, (down + 1) * capacity)
                parts.append(got_refs[down][:capacity, at:end])
                parts += [ref[place, at:end] for ref in got_refs[n_row:]]
        return jnp.concatenate(parts, axis=0)

    if half:
        marks = marks_ref[...]
    else:
        slots = got(0, LANES).astype(jnp.float32)
        lane = lax.broadcasted_iota(jnp.int32, slots.shape, 1).astype(jnp.float32)
        which = lax.broadcasted_iota(jnp.int32, (block_cols, LANES), 1)
        spread = lax.div(which, block_rows) == lax.broadcasted_iota(jnp.int32, which.shape, 0)
        which = lax.broadcasted_iota(jnp.int32, (block_rows, LANES), 1)
        here = lax.rem(which, block_rows) == lax.broadcasted_iota(jnp.int32, which.shape, 0)
        pattern = jnp.dot(
            marks_ref[...].astype(jnp.float32),
            spread.astype(jnp.float32),
            preferred_element_type=jnp.float32,
        )
        pattern = jnp.sum(jnp.where(here, pattern, 0.0), axis=0, keepdims=True)
        marks = jnp.where(slots == lane, pattern, 0.0)
        marks = marks.T[: block_rows * block_cols].astype(jnp.bfloat16)
        held_ref[...] = marks
    low = lax.broadcasted_iota(jnp.int32, (block_rows, LANES), 1) < BLK
    step = 256
    for at in range(0, part, step):
        summed = jnp.dot(
            marks, got(front + at, front + at + step), preferred_element_type=jnp.float32
        )
        for pair in range(step // LANES):
            lanes = slice(pair * LANES, (pair + 1) * LANES)
            row = (at // LANES + pair) * 2
            for twin in range(block_cols // 2):
                left = summed[twin * 2 * block_rows : (twin * 2 + 1) * block_rows, lanes]
                right = summed[(twin * 2 + 1) * block_rows : (twin * 2 + 2) * block_rows, lanes]
                tall[twin, pl.ds(row, block_rows, stride=part_rows), :] = jnp.where(
                    low, left, pltpu.roll(right, BLK, 1)
                )
                tall[twin, pl.ds(row + 1, block_rows, stride=part_rows), :] = jnp.where(
                    low, pltpu.roll(left, BLK, 1), right
                )
    tile_rows = block_rows * BLK
    row_here = (lax.axis_index("layer") * 2 + half) * part_rows
    row_start = lax.axis_index("row") * tile_rows + row_here
    col_start = lax.axis_index("col") * cols
    index = lax.broadcasted_iota(jnp.int32, (rows, LANES), 0)
    inside = lax.div(index, part_rows) * BLK + lax.rem(index, part_rows)
    row_id = row_start + inside
    lane = lax.broadcasted_iota(jnp.int32, (rows, LANES), 1)
    occ = jnp.zeros((rows, 1), jnp.float32)
    for at in range(0, tile_rows, LANES):
        mine = jnp.where(row_here + inside == at + lane, occ_ref[:, at : at + LANES], 0.0)
        occ = occ + jnp.sum(mine, axis=1, keepdims=True)
    values = []
    for twin in range(block_cols // 2):
        diagonal = jnp.where(row_id == col_start + twin * LANES + lane, occ, 0.0)
        values.append(tall[twin] + diagonal)
    here = slice(half * part_rows, (half + 1) * part_rows)

    def put(ref, at, value):
        ref[:, here, at : at + LANES] = value.astype(jnp.bfloat16).reshape(
            block_rows, part_rows, LANES
        )

    for twin, value in enumerate(values):
        put(out_ref, twin * LANES, value)
    quarter = LANES // 4
    spot = lax.div(lane, quarter)
    for twin in range(0, block_cols // 2, 2):
        first, second = values[twin], values[twin + 1]
        at = twin // (block_rows // 2) * tile_rows + twin % (block_rows // 2) // 2 * LANES
        back, ahead = pltpu.roll(first, 3 * quarter, 1), pltpu.roll(second, quarter, 1)
        far_back, far_ahead = pltpu.roll(first, 2 * quarter, 1), pltpu.roll(second, 2 * quarter, 1)
        put(
            sorted_ref,
            at,
            jnp.where(
                spot == 0, first, jnp.where(spot == 1, back, jnp.where(spot == 2, far_ahead, ahead))
            ),
        )
        put(
            sorted_ref,
            at + tile_rows // 2,
            jnp.where(
                spot == 0, back, jnp.where(spot == 1, far_back, jnp.where(spot == 2, ahead, second))
            ),
        )


def start_copies(pairs, sems):
    copies = [
        pltpu.make_async_copy(source, target, sems.at[index])
        for index, (source, target) in enumerate(pairs)
    ]
    for copy in copies:
        copy.start()
    return copies


def split(values, sizes):
    ends = [sum(sizes[: index + 1]) for index in range(len(sizes))]
    return [values[end - size : end] for end, size in zip(ends, sizes)]


def joined(parts):
    return flat(jnp.concatenate([part[...] for part in parts], axis=0))


def left_blocks(tile_rows, cols):
    width = tile_rows // 2
    return [
        (at // tile_rows, at % tile_rows // width, slice(at, at + width))
        for at in range(0, cols, width)
    ]


def flat(value):
    return value.reshape(-1, value.shape[-1])


def near_square_kernel(n_col, n_row, *refs):
    lefts, pieces = refs[: n_col - 1], refs[n_col - 1 : n_col - 1 + n_row]
    sum_ref, other_ref, met_ref, give_ref, left, sems = refs[n_col - 1 + n_row :]
    row, col, layer = (lax.axis_index(axis) for axis in ("row", "col", "layer"))
    cols = sum_ref.shape[1]
    per_col = n_row // n_col
    pairs = [
        (piece.at[:, :, lanes], left.at[(col ^ shift) * per_col + block, which])
        for shift, piece in enumerate(lefts)
        for block, which, lanes in left_blocks(cols // per_col, cols)
    ]
    inner = len(pairs)
    here = give_ref.shape[1]
    pairs += [
        (piece.at[pl.ds((1 - layer) * here, here)], give_ref.at[col ^ shift])
        for shift, piece in enumerate(lefts)
    ]
    copies = start_copies(pairs, sems)
    last = col ^ (n_col - 1)
    for block in range(per_col):
        left[last * per_col + block] = jnp.zeros(left.shape[1:], left.dtype)
    for shift in range(n_row):

        @pl.when(lax.div(row ^ shift, per_col) == last)
        def _(shift=shift):
            met_ref[lax.rem(row ^ shift, per_col)] = flat(pieces[shift][...])

    for copy in copies[:inner]:
        copy.wait()
    total = jnp.zeros(sum_ref.shape, jnp.float32)
    for shift in range(n_row):
        total = total + jnp.dot(
            flat(left[row ^ shift, layer]),
            flat(pieces[shift][...]),
            preferred_element_type=jnp.float32,
        )
        other_ref[shift] = flat(left[row ^ shift, 1 - layer])
    sum_ref[...] = total
    for copy in copies[inner:]:
        copy.wait()


def far_square_kernel(n_col, n_row, *refs):
    sum_ref, other_ref, met_ref = refs[:3]
    mates, left_ref = refs[3 : 3 + n_row], refs[3 + n_row]
    low_ref, give_ref, sem = refs[5 + n_row :]
    row, col, layer = (lax.axis_index(axis) for axis in ("row", "col", "layer"))
    here = give_ref.shape[1]
    copy = pltpu.make_async_copy(
        left_ref.at[pl.ds((1 - layer) * here, here)], give_ref.at[col ^ (n_col - 1)], sem
    )
    copy.start()
    per_col = met_ref.shape[0]
    width = other_ref.shape[2]

    def columns(block, which):
        start = pl.multiple_of((block * 2 + which) * width, width)
        return flat(left_ref[:, :, pl.ds(start, width)])

    total = sum_ref[...]
    for block in range(per_col):
        total = total + jnp.dot(
            columns(block, layer), met_ref[block], preferred_element_type=jnp.float32
        )
    for shift, mate in enumerate(mates):
        met = row ^ shift
        left = jnp.where(
            lax.div(met, per_col) == col ^ (n_col - 1),
            columns(lax.rem(met, per_col), 1 - layer),
            other_ref[shift],
        )
        total = total + jnp.dot(left, flat(mate[...]), preferred_element_type=jnp.float32)
    low_ref[...] = total.astype(jnp.bfloat16).reshape(low_ref.shape)
    copy.wait()


def near_cube_kernel(n_col, sizes, *refs):
    lefts, given, pattern_ref = refs[:n_col], refs[n_col], refs[n_col + 1]
    n_row, count = len(sizes), n_col + 2 + sum(sizes)
    pieces, mates = split(refs[n_col + 2 : count], sizes), refs[count : count + n_row - 1]
    sum_ref, mask_ref, other_ref, left, own, sems = refs[count + n_row :]
    row, col, layer = (lax.axis_index(axis) for axis in ("row", "col", "layer"))
    rows, cols = sum_ref.shape
    per_col = n_row // n_col
    here = given.shape[1]
    mine = pl.ds(layer * here, here)
    pairs = []
    for block, which, lanes in left_blocks(cols // per_col, cols):
        for shift, piece in enumerate(lefts):
            at = (col ^ shift) * per_col + block
            pairs.append((piece.at[mine, :, lanes], left.at[at, which, :, layer]))
            pairs.append(
                (given.at[col ^ shift, :, :, lanes], left.at[at, which, :, 1 - layer])
            )
    copies = start_copies(pairs, sems)
    own[:, layer] = pieces[0][0][mine]
    own[:, 1 - layer] = mates[0][mine]
    pattern = pattern_ref[...].astype(jnp.float32).astype(jnp.bfloat16)
    block_rows, block_cols = pattern.shape
    across = lax.broadcasted_iota(jnp.int32, (block_cols, cols), 1)
    which = lax.broadcasted_iota(jnp.int32, (block_cols, cols), 0)
    wide = (lax.div(across, BLK) == which).astype(jnp.float32).astype(jnp.bfloat16)
    down = lax.broadcasted_iota(jnp.int32, (rows, block_rows), 0) + layer * rows
    which = lax.broadcasted_iota(jnp.int32, (rows, block_rows), 1)
    tall = (lax.div(down, BLK) == which).astype(jnp.float32).astype(jnp.bfloat16)
    tall = jnp.dot(tall, pattern, preferred_element_type=jnp.float32).astype(jnp.bfloat16)
    mask = jnp.dot(tall, wide, preferred_element_type=jnp.float32)
    mask_ref[...] = mask.astype(jnp.bfloat16)
    total = 1.5 * flat(own[...]).astype(jnp.float32)
    for copy in copies:
        copy.wait()
    for shift in range(n_row):
        total = total - jnp.dot(
            flat(left[row ^ shift, layer]),
            joined(pieces[shift]),
            preferred_element_type=jnp.float32,
        )
    for shift, mate in enumerate(mates):
        total = total - jnp.dot(
            flat(left[row ^ shift, 1 - layer]),
            flat(mate[...]),
            preferred_element_type=jnp.float32,
        )
    other_ref[...] = flat(left[row ^ (n_row - 1), 1 - layer])
    sum_ref[...] = total


def far_cube_kernel(sum_ref, mask_ref, left_ref, *refs):
    mates, out_ref = refs[:-2], refs[-1]
    total = sum_ref[...] - jnp.dot(
        left_ref[...], joined(mates), preferred_element_type=jnp.float32
    )
    out_ref[...] = mask_ref[...].astype(jnp.float32) * (2.0 * total)


def xor_pairs(axis, shift):
    return [(i, i ^ shift) for i in range(lax.axis_size(axis))]


def gather(piece, axis):
    return [piece] + [
        lax.ppermute(piece, axis, xor_pairs(axis, shift))
        for shift in range(1, lax.axis_size(axis))
    ]


def exchange(first, second, capacity):
    def relay(parcels, out_axis, in_axis, weight):
        arrived = [parcels[0]] + [
            lax.ppermute(parcel, out_axis, xor_pairs(out_axis, shift))
            for shift, parcel in enumerate(parcels)
            if shift
        ]
        steps = lax.axis_size(in_axis)
        shape = (len(arrived) * capacity, parcels[0].shape[1])
        mixed = pl.pallas_call(
            functools.partial(mix_kernel, len(arrived), capacity),
            out_shape=[jax.ShapeDtypeStruct(shape, jnp.bfloat16)] * (steps - 1),
            in_specs=[whole_ref()] * len(arrived),
            out_specs=[whole_ref()] * (steps - 1),
            compiler_params=params(4 * steps * shape[0] * shape[1]),
            cost_estimate=cost(weight, 4 * steps * shape[0] * shape[1]),
            name="mix",
        )(*arrived[::-1])
        return arrived + [
            lax.ppermute(parcel, in_axis, xor_pairs(in_axis, shift))
            for shift, parcel in enumerate(mixed, 1)
        ]

    first = relay(first, "row", "col", EARLY)
    second = relay(second, "col", "row", LATE)
    return first, [*second, token(second, EXTRA)]


def after(value, *earlier):
    return lax.optimization_barrier((value, earlier))[0]


def token(values, weight):
    return pl.pallas_call(
        token_kernel,
        out_shape=jax.ShapeDtypeStruct((8, LANES), jnp.float32),
        in_specs=[any_ref()] * len(values),
        out_specs=whole_ref(),
        compiler_params=params(0),
        cost_estimate=cost(weight, 0),
        name="token",
    )(*values)


def gather_line(piece):
    count = lax.axis_size("col")
    pieces = {0: piece}
    step = count // 2
    while step:
        pieces |= {
            shift + step: lax.ppermute(held, "col", xor_pairs("col", step))
            for shift, held in pieces.items()
        }
        step //= 2
    return [pieces[shift] for shift in range(count)]


def gather_square(piece):
    if lax.axis_size("row") != 4:
        return [[held] for held in gather(piece, "row")]
    one, two = (lax.ppermute(piece, "row", xor_pairs("row", shift)) for shift in (1, 2))
    middle = piece.shape[0] // 2
    far = [
        lax.ppermute(two[:middle], "row", xor_pairs("row", 1)),
        lax.ppermute(one[middle:], "row", xor_pairs("row", 2)),
    ]
    return [[piece], [one], [two], far]


def swap(piece):
    return lax.ppermute(piece, "layer", xor_pairs("layer", 1))


def on_device(tasks, task_owner, task_slot, p_pattern, c_pattern, occupations):
    n_row, n_col, layers = (lax.axis_size(axis) for axis in ("row", "col", "layer"))
    owners = n_row * n_col
    count = tasks.shape[0]
    capacity = max(2, 2 * count // owners)
    places = owners * capacity
    block_rows, block_cols = p_pattern.shape
    part_rows = BLK // layers
    part = part_rows * BLK
    rows, cols = block_rows * part_rows, block_cols * BLK
    width = part + LANES
    layer = lax.axis_index("layer")

    paired = capacity % 16 == 0
    if paired:
        parcels = [(n_col * capacity, part // 2 + LANES)] * n_row
        parcels += [(n_row * capacity, part - part // 2)] * n_col
    else:
        parcels = [(places, width)]
    sent = pl.pallas_call(
        functools.partial(pack_kernel, owners, capacity, p_pattern.shape, paired),
        out_shape=[jax.ShapeDtypeStruct(shape, jnp.bfloat16) for shape in parcels],
        in_specs=[any_ref()] * 3,
        out_specs=[whole_ref()] * len(parcels),
        scratch_shapes=[
            pltpu.VMEM((count, part), jnp.bfloat16),
            pltpu.VMEM((1, count), jnp.int32),
            pltpu.VMEM((1, count), jnp.int32),
            pltpu.SemaphoreType.DMA((3,)),
        ],
        compiler_params=pltpu.CompilerParams(vmem_limit_bytes=PACK_VMEM),
        cost_estimate=cost(2 * places * count * width, 2 * (places + count) * width),
        name="pack",
    )(tasks, task_owner.reshape(1, count), task_slot.reshape(1, count))
    if paired:
        got = list(exchange(sent[:n_row], sent[n_row:], capacity))
    else:
        got = [
            [
                lax.all_to_all(
                    sent[0].reshape(owners, capacity, width),
                    ("row", "col"),
                    split_axis=0,
                    concat_axis=0,
                    tiled=True,
                ).reshape(places, width)
            ]
        ] * 2

    slots_here = block_rows * block_cols
    half_shape = jax.ShapeDtypeStruct((block_rows, part_rows // 2, cols), jnp.bfloat16)
    piece_shape = jax.ShapeDtypeStruct((block_rows, part_rows, cols), jnp.bfloat16)
    marks_shape = jax.ShapeDtypeStruct((slots_here, places), jnp.bfloat16)

    def build(half, marks, *blocks):
        return pl.pallas_call(
            functools.partial(build_kernel, half, paired),
            out_shape=[piece_shape] * 2 if half else [marks_shape, half_shape, half_shape],
            in_specs=[whole_ref()] * (2 + len(blocks)),
            out_specs=[whole_ref()] * (2 if half else 3),
            scratch_shapes=[pltpu.VMEM((cols // LANES, rows // 2, LANES), jnp.float32)],
            compiler_params=params(2 * places * width + 8 * rows * cols),
            cost_estimate=cost(places * slots_here * part, places * width),
            name="build",
        )(occupations.reshape(1, block_rows * BLK), marks, *blocks)

    marks, *first_half = build(0, p_pattern, *got[0][::-1])
    density, ordered = build(1, marks, *got[1][::-1], *first_half)

    lefts = gather_line(ordered)
    mate = swap(density)
    pieces = gather(after(density, mate), "row")
    pieces[0] = density
    ahead = (lefts[1], lefts[n_col // 2])
    mates = [mate] + [swap(after(piece, *ahead)) for piece in pieces[1:]]
    flops = 2 * rows * cols * n_col * cols
    half_width = block_rows * BLK // layers
    panel_bytes = 2 * n_row * layers * rows * half_width
    sum_shape = jax.ShapeDtypeStruct((rows, cols), jnp.float32)
    other_shape = jax.ShapeDtypeStruct((n_row, rows, half_width), jnp.bfloat16)
    met_shape = jax.ShapeDtypeStruct((n_row // n_col, rows, cols), jnp.bfloat16)
    here = block_rows // layers
    give_shape = jax.ShapeDtypeStruct((n_col, here, part_rows, cols), jnp.bfloat16)
    partial, other, met, give = pl.pallas_call(
        functools.partial(near_square_kernel, n_col, n_row),
        out_shape=[sum_shape, other_shape, met_shape, give_shape],
        in_specs=[any_ref()] * (n_col - 1) + [whole_ref()] * n_row,
        out_specs=[whole_ref()] * 3 + [any_ref()],
        scratch_shapes=[
            pltpu.VMEM((n_row, layers, block_rows, part_rows, half_width), jnp.bfloat16),
            pltpu.SemaphoreType.DMA((n_row * layers + n_col,)),
        ],
        compiler_params=params(2 * panel_bytes + 16 * rows * cols),
        cost_estimate=cost(0, 0),
        name="near_square",
    )(*lefts[:-1], *pieces)
    square, give = pl.pallas_call(
        functools.partial(far_square_kernel, n_col, n_row),
        out_shape=[piece_shape, give_shape],
        in_specs=[whole_ref()] * (4 + n_row) + [any_ref()],
        out_specs=[whole_ref(), any_ref()],
        scratch_shapes=[pltpu.SemaphoreType.DMA],
        input_output_aliases={4 + n_row: 1},
        compiler_params=params(panel_bytes + 16 * rows * cols),
        cost_estimate=cost(0, 0),
        name="far_square",
    )(partial, other, met, *mates, lefts[-1], give)

    pieces = gather_square(square)
    mates = [[swap(part) for part in parts] for parts in pieces]
    if len(pieces[-1]) > 1:
        mates[1:3] = [[swap(after(pieces[shift][0], pieces[3 - shift][0]))] for shift in (1, 2)]
    received = swap(give)
    sizes = [len(parts) for parts in pieces]
    pieces, mates = ([part for parts in held for part in parts] for held in (pieces, mates))
    partial, mask, other = pl.pallas_call(
        functools.partial(near_cube_kernel, n_col, sizes),
        out_shape=[
            sum_shape,
            jax.ShapeDtypeStruct((rows, cols), jnp.bfloat16),
            jax.ShapeDtypeStruct((rows, half_width), jnp.bfloat16),
        ],
        in_specs=[any_ref()] * (n_col + 1)
        + [whole_ref()] * (n_row + len(pieces))
        + [any_ref()],
        out_specs=[whole_ref()] * 3,
        scratch_shapes=[
            pltpu.VMEM((n_row, layers, here, layers, part_rows, half_width), jnp.bfloat16),
            pltpu.VMEM((here, layers, part_rows, cols), jnp.bfloat16),
            pltpu.SemaphoreType.DMA((2 * n_row * layers,)),
        ],
        compiler_params=params(2 * panel_bytes + 16 * rows * cols),
        cost_estimate=cost(0, 0),
        name="near_cube",
    )(*lefts, received, c_pattern, *pieces, *mates[: n_row - 1], token([received], GIVE))
    return pl.pallas_call(
        far_cube_kernel,
        out_shape=sum_shape,
        in_specs=[whole_ref()] * (3 + sizes[-1]) + [any_ref()],
        out_specs=whole_ref(),
        compiler_params=params(16 * rows * cols),
        cost_estimate=cost(flops // 2, 4 * 1024 * 1024),
        name="far_cube",
    )(partial, mask, other, *mates[n_row - 1 :], token(pieces[n_row - 1 :], HEAVY))


def solution(mesh):
    return jax.shard_map(
        on_device,
        mesh=mesh,
        in_specs=(
            P(("row", "col"), None),
            P(("row", "col"), None),
            P(("row", "col")),
            P("row", "col"),
            P("row", "col"),
            P("row"),
        ),
        out_specs=P(("row", "layer"), "col"),
        check_vma=False,
    )
```

```python
import functools

import jax
import jax.numpy as jnp
from jax import lax
from jax.experimental import pallas as pl
from jax.experimental.pallas import tpu as pltpu
from jax.sharding import PartitionSpec as P

BLK = 64
LANES = 128
PACK_VMEM = 52 * 1024 * 1024
HEAVY = 10**10
EARLY = 0
EXTRA = 0
LATE = 0


def params(held):
    return pltpu.CompilerParams(vmem_limit_bytes=held + 6 * 1024 * 1024)


def whole_ref():
    return pl.BlockSpec(memory_space=pltpu.VMEM)


def any_ref():
    return pl.BlockSpec(memory_space=pl.ANY)


def cost(flops, bytes_accessed):
    return pl.CostEstimate(flops=flops, bytes_accessed=bytes_accessed, transcendentals=0)


def pack_kernel(owners, capacity, block_shape, paired, tasks_ref, owner_hbm, slot_hbm, *refs):
    out_refs, (held, owner_ref, slot_ref, sems) = refs[:-4], refs[-4:]
    count, part = held.shape
    layer = lax.axis_index("layer")
    start = pl.multiple_of(layer * part, part)
    *small, copy = start_copies(
        [
            (owner_hbm, owner_ref),
            (slot_hbm, slot_ref),
            (tasks_ref.at[:, pl.ds(start, part)], held),
        ],
        sems,
    )
    for each in small:
        each.wait()
    block_rows, block_cols = block_shape
    slot_row = slot_ref[...]
    slot_row = lax.rem(slot_row, block_cols) * block_rows + lax.div(slot_row, block_cols)
    across = lax.broadcasted_iota(jnp.int32, (count, count), 1)
    down = lax.broadcasted_iota(jnp.int32, (count, count), 0)
    slot_col = jnp.sum(
        jnp.where(across == down, slot_row.astype(jnp.float32), 0.0), axis=1, keepdims=True
    )
    owner_row = owner_ref[...]
    if paired:
        owner_row = owner_row ^ (
            lax.axis_index("row") * lax.axis_size("col") + lax.axis_index("col")
        )
    same = (lax.broadcasted_iota(jnp.int32, (owners, count), 0) == owner_row).astype(jnp.float32)
    before = (down < across).astype(jnp.float32).astype(jnp.bfloat16)
    ahead = jnp.dot(same.astype(jnp.bfloat16), before, preferred_element_type=jnp.float32)
    placed = jnp.sum(ahead * same, axis=0, keepdims=True).astype(jnp.int32)
    target = owner_row * capacity + placed
    places = owners * capacity
    move = (
        (lax.broadcasted_iota(jnp.int32, (places, count), 0) == target)
        .astype(jnp.float32)
        .astype(jnp.bfloat16)
    )

    def put(at, end, blocks):
        moved = jnp.dot(move, blocks, preferred_element_type=jnp.float32).astype(jnp.bfloat16)
        if not paired:
            out_refs[0][:, at:end] = moved
            return
        n_row, n_col = lax.axis_size("row"), lax.axis_size("col")
        if at < part // 2 + LANES:
            each = n_col * capacity
            for down, out_ref in enumerate(out_refs[:n_row]):
                out_ref[:, at:end] = moved[down * each : (down + 1) * each]
            return
        at, end = at - (part // 2 + LANES), end - (part // 2 + LANES)
        for over, out_ref in enumerate(out_refs[n_row:]):
            for down in range(n_row):
                place = (down * n_col + over) * capacity
                out_ref[down * capacity : (down + 1) * capacity, at:end] = moved[
                    place : place + capacity
                ]

    slots = jnp.broadcast_to(slot_col, (count, LANES)).astype(jnp.bfloat16)
    put(0, LANES, slots)
    copy.wait()
    step = 512
    for at in range(0, part, step):
        put(LANES + at, LANES + at + step, held[:, at : at + step])


def mix_kernel(arrivals, capacity, *refs):
    for shift, out_ref in enumerate(refs[arrivals:], 1):
        for index, ref in enumerate(refs[:arrivals][::-1]):
            out_ref[index * capacity : (index + 1) * capacity, :] = ref[
                shift * capacity : (shift + 1) * capacity, :
            ]


def token_kernel(*refs):
    refs[-1][...] = jnp.zeros_like(refs[-1])


def build_kernel(half, paired, occ_ref, marks_ref, *refs):
    out_ref, sorted_ref, tall = refs[-3:]
    layers = lax.axis_size("layer")
    block_rows, cols = out_ref.shape[0], out_ref.shape[2]
    part_rows = BLK // layers // 2
    block_cols = cols // BLK
    rows = block_rows * part_rows
    part = part_rows * BLK
    front = 0
    if half:
        got_refs, before = refs[1 if paired else 0 : -5][::-1], refs[-5:-3]
        for ref, old_ref in zip((out_ref, sorted_ref), before):
            ref[:, :part_rows] = old_ref[...]
    else:
        got_refs, held_ref = refs[:-4][::-1], refs[-4]
        front = LANES

    def got(at, end):
        if not paired:
            skip = half * (LANES + part)
            return got_refs[0][:, skip + at : skip + end]
        n_row, n_col = lax.axis_size("row"), lax.axis_size("col")
        if half:
            capacity = got_refs[0].shape[0] // n_row
            parts = [ref[:capacity, at:end] for ref in got_refs[:n_col]]
            parts += [ref[:, at:end] for ref in got_refs[n_col:]]
        else:
            capacity = got_refs[0].shape[0] // n_col
            parts = []
            for down in range(n_row):
                place = slice(down * capacity, (down + 1) * capacity)
                parts.append(got_refs[down][:capacity, at:end])
                parts += [ref[place, at:end] for ref in got_refs[n_row:]]
        return jnp.concatenate(parts, axis=0)

    if half:
        marks = marks_ref[...]
    else:
        slots = got(0, LANES).astype(jnp.float32)
        lane = lax.broadcasted_iota(jnp.int32, slots.shape, 1).astype(jnp.float32)
        which = lax.broadcasted_iota(jnp.int32, (block_cols, LANES), 1)
        spread = lax.div(which, block_rows) == lax.broadcasted_iota(jnp.int32, which.shape, 0)
        which = lax.broadcasted_iota(jnp.int32, (block_rows, LANES), 1)
        here = lax.rem(which, block_rows) == lax.broadcasted_iota(jnp.int32, which.shape, 0)
        pattern = jnp.dot(
            marks_ref[...].astype(jnp.float32),
            spread.astype(jnp.float32),
            preferred_element_type=jnp.float32,
        )
        pattern = jnp.sum(jnp.where(here, pattern, 0.0), axis=0, keepdims=True)
        marks = jnp.where(slots == lane, pattern, 0.0)
        marks = marks.T[: block_rows * block_cols].astype(jnp.bfloat16)
        held_ref[...] = marks
    low = lax.broadcasted_iota(jnp.int32, (block_rows, LANES), 1) < BLK
    step = 256
    for at in range(0, part, step):
        summed = jnp.dot(
            marks, got(front + at, front + at + step), preferred_element_type=jnp.float32
        )
        for pair in range(step // LANES):
            lanes = slice(pair * LANES, (pair + 1) * LANES)
            row = (at // LANES + pair) * 2
            for twin in range(block_cols // 2):
                left = summed[twin * 2 * block_rows : (twin * 2 + 1) * block_rows, lanes]
                right = summed[(twin * 2 + 1) * block_rows : (twin * 2 + 2) * block_rows, lanes]
                tall[twin, pl.ds(row, block_rows, stride=part_rows), :] = jnp.where(
                    low, left, pltpu.roll(right, BLK, 1)
                )
                tall[twin, pl.ds(row + 1, block_rows, stride=part_rows), :] = jnp.where(
                    low, pltpu.roll(left, BLK, 1), right
                )
    tile_rows = block_rows * BLK
    row_here = (lax.axis_index("layer") * 2 + half) * part_rows
    row_start = lax.axis_index("row") * tile_rows + row_here
    col_start = lax.axis_index("col") * cols
    index = lax.broadcasted_iota(jnp.int32, (rows, LANES), 0)
    inside = lax.div(index, part_rows) * BLK + lax.rem(index, part_rows)
    row_id = row_start + inside
    lane = lax.broadcasted_iota(jnp.int32, (rows, LANES), 1)
    occ = jnp.zeros((rows, 1), jnp.float32)
    for at in range(0, tile_rows, LANES):
        mine = jnp.where(row_here + inside == at + lane, occ_ref[:, at : at + LANES], 0.0)
        occ = occ + jnp.sum(mine, axis=1, keepdims=True)
    values = []
    for twin in range(block_cols // 2):
        diagonal = jnp.where(row_id == col_start + twin * LANES + lane, occ, 0.0)
        values.append(tall[twin, :rows] + diagonal)
    here = slice(half * part_rows, (half + 1) * part_rows)

    def put(ref, at, value):
        ref[:, here, at : at + LANES] = value.astype(jnp.bfloat16).reshape(
            block_rows, part_rows, LANES
        )

    for twin, value in enumerate(values):
        put(out_ref, twin * LANES, value)
    quarter = LANES // 4
    spot = lax.div(lane, quarter)
    for twin in range(0, block_cols // 2, 2):
        first, second = values[twin], values[twin + 1]
        at = twin // (block_rows // 2) * tile_rows + twin % (block_rows // 2) // 2 * LANES
        back, ahead = pltpu.roll(first, 3 * quarter, 1), pltpu.roll(second, quarter, 1)
        far_back, far_ahead = pltpu.roll(first, 2 * quarter, 1), pltpu.roll(second, 2 * quarter, 1)
        put(
            sorted_ref,
            at,
            jnp.where(
                spot == 0, first, jnp.where(spot == 1, back, jnp.where(spot == 2, far_ahead, ahead))
            ),
        )
        put(
            sorted_ref,
            at + tile_rows // 2,
            jnp.where(
                spot == 0, back, jnp.where(spot == 1, far_back, jnp.where(spot == 2, ahead, second))
            ),
        )


def start_copies(pairs, sems):
    copies = [
        pltpu.make_async_copy(source, target, sems.at[index])
        for index, (source, target) in enumerate(pairs)
    ]
    for copy in copies:
        copy.start()
    return copies


def split(values, sizes):
    ends = [sum(sizes[: index + 1]) for index in range(len(sizes))]
    return [values[end - size : end] for end, size in zip(ends, sizes)]


def joined(parts):
    return flat(jnp.concatenate([part[...] for part in parts], axis=0))


def left_blocks(tile_rows, cols):
    width = tile_rows // 2
    return [
        (at // tile_rows, at % tile_rows // width, slice(at, at + width))
        for at in range(0, cols, width)
    ]


def flat(value):
    return value.reshape(-1, value.shape[-1])


def near_square_kernel(n_col, n_row, *refs):
    lefts, pieces = refs[: n_col - 1], refs[n_col - 1 : n_col - 1 + n_row]
    sum_ref, other_ref, met_ref, give_ref, left, sems = refs[n_col - 1 + n_row :]
    row, col, layer = (lax.axis_index(axis) for axis in ("row", "col", "layer"))
    cols = sum_ref.shape[1]
    per_col = n_row // n_col
    pairs = [
        (piece.at[:, :, lanes], left.at[(col ^ shift) * per_col + block, which])
        for shift, piece in enumerate(lefts)
        for block, which, lanes in left_blocks(cols // per_col, cols)
    ]
    inner = len(pairs)
    here = give_ref.shape[1]
    pairs += [
        (piece.at[pl.ds((1 - layer) * here, here)], give_ref.at[col ^ shift])
        for shift, piece in enumerate(lefts)
    ]
    copies = start_copies(pairs, sems)
    last = col ^ (n_col - 1)
    for block in range(per_col):
        left[last * per_col + block] = jnp.zeros(left.shape[1:], left.dtype)
    for shift in range(n_row):

        @pl.when(lax.div(row ^ shift, per_col) == last)
        def _(shift=shift):
            met_ref[lax.rem(row ^ shift, per_col)] = flat(pieces[shift][...])

    for copy in copies[:inner]:
        copy.wait()
    total = jnp.zeros(sum_ref.shape, jnp.float32)
    for shift in range(n_row):
        total = total + jnp.dot(
            flat(left[row ^ shift, layer]),
            flat(pieces[shift][...]),
            preferred_element_type=jnp.float32,
        )
        other_ref[shift] = flat(left[row ^ shift, 1 - layer])
    sum_ref[...] = total
    for copy in copies[inner:]:
        copy.wait()


def far_square_kernel(n_col, n_row, *refs):
    sum_ref, other_ref, met_ref = refs[:3]
    mates, left_ref = refs[3 : 3 + n_row], refs[3 + n_row]
    low_ref, give_ref, sem = refs[5 + n_row :]
    row, col, layer = (lax.axis_index(axis) for axis in ("row", "col", "layer"))
    here = give_ref.shape[1]
    copy = pltpu.make_async_copy(
        left_ref.at[pl.ds((1 - layer) * here, here)], give_ref.at[col ^ (n_col - 1)], sem
    )
    copy.start()
    per_col = met_ref.shape[0]
    width = other_ref.shape[2]

    def columns(block, which):
        start = pl.multiple_of((block * 2 + which) * width, width)
        return flat(left_ref[:, :, pl.ds(start, width)])

    total = sum_ref[...]
    for block in range(per_col):
        total = total + jnp.dot(
            columns(block, layer), met_ref[block], preferred_element_type=jnp.float32
        )
    for shift, mate in enumerate(mates):
        met = row ^ shift
        left = jnp.where(
            lax.div(met, per_col) == col ^ (n_col - 1),
            columns(lax.rem(met, per_col), 1 - layer),
            other_ref[shift],
        )
        total = total + jnp.dot(left, flat(mate[...]), preferred_element_type=jnp.float32)
    low_ref[...] = total.astype(jnp.bfloat16).reshape(low_ref.shape)
    copy.wait()


def near_cube_kernel(n_col, sizes, *refs):
    lefts, given, pattern_ref = refs[:n_col], refs[n_col], refs[n_col + 1]
    n_row, count = len(sizes), n_col + 2 + sum(sizes)
    pieces, mates = split(refs[n_col + 2 : count], sizes), refs[count : count + n_row - 1]
    sum_ref, mask_ref, other_ref, left, own, sems = refs[count + n_row - 1 :]
    row, col, layer = (lax.axis_index(axis) for axis in ("row", "col", "layer"))
    rows, cols = sum_ref.shape
    per_col = n_row // n_col
    here = given.shape[1]
    mine = pl.ds(layer * here, here)
    pairs = []
    for block, which, lanes in left_blocks(cols // per_col, cols):
        for shift, piece in enumerate(lefts):
            at = (col ^ shift) * per_col + block
            pairs.append((piece.at[mine, :, lanes], left.at[at, which, :, layer]))
            pairs.append(
                (given.at[col ^ shift, :, :, lanes], left.at[at, which, :, 1 - layer])
            )
    copies = start_copies(pairs, sems)
    own[:, layer] = pieces[0][0][mine]
    own[:, 1 - layer] = mates[0][mine]
    pattern = pattern_ref[...].astype(jnp.float32).astype(jnp.bfloat16)
    block_rows, block_cols = pattern.shape
    across = lax.broadcasted_iota(jnp.int32, (block_cols, cols), 1)
    which = lax.broadcasted_iota(jnp.int32, (block_cols, cols), 0)
    wide = (lax.div(across, BLK) == which).astype(jnp.float32).astype(jnp.bfloat16)
    down = lax.broadcasted_iota(jnp.int32, (rows, block_rows), 0) + layer * rows
    which = lax.broadcasted_iota(jnp.int32, (rows, block_rows), 1)
    tall = (lax.div(down, BLK) == which).astype(jnp.float32).astype(jnp.bfloat16)
    tall = jnp.dot(tall, pattern, preferred_element_type=jnp.float32).astype(jnp.bfloat16)
    mask = jnp.dot(tall, wide, preferred_element_type=jnp.float32)
    mask_ref[...] = mask.astype(jnp.bfloat16)
    total = 1.5 * flat(own[...]).astype(jnp.float32)
    for copy in copies:
        copy.wait()
    for shift in range(n_row):
        total = total - jnp.dot(
            flat(left[row ^ shift, layer]),
            joined(pieces[shift]),
            preferred_element_type=jnp.float32,
        )
    for shift, mate in enumerate(mates):
        total = total - jnp.dot(
            flat(left[row ^ shift, 1 - layer]),
            flat(mate[...]),
            preferred_element_type=jnp.float32,
        )
    other_ref[...] = flat(left[row ^ (n_row - 1), 1 - layer])
    sum_ref[...] = total


def far_cube_kernel(sum_ref, mask_ref, left_ref, *refs):
    mates, out_ref = refs[:-2], refs[-1]
    total = sum_ref[...] - jnp.dot(
        left_ref[...], joined(mates), preferred_element_type=jnp.float32
    )
    out_ref[...] = mask_ref[...].astype(jnp.float32) * (2.0 * total)


def xor_pairs(axis, shift):
    return [(i, i ^ shift) for i in range(lax.axis_size(axis))]


def gather(piece, axis):
    return [piece] + [
        lax.ppermute(piece, axis, xor_pairs(axis, shift))
        for shift in range(1, lax.axis_size(axis))
    ]


def exchange(first, second, capacity):
    def relay(parcels, out_axis, in_axis, weight):
        arrived = [parcels[0]] + [
            lax.ppermute(parcel, out_axis, xor_pairs(out_axis, shift))
            for shift, parcel in enumerate(parcels)
            if shift
        ]
        steps = lax.axis_size(in_axis)
        shape = (len(arrived) * capacity, parcels[0].shape[1])
        mixed = pl.pallas_call(
            functools.partial(mix_kernel, len(arrived), capacity),
            out_shape=[jax.ShapeDtypeStruct(shape, jnp.bfloat16)] * (steps - 1),
            in_specs=[whole_ref()] * len(arrived),
            out_specs=[whole_ref()] * (steps - 1),
            compiler_params=params(4 * steps * shape[0] * shape[1]),
            cost_estimate=cost(weight, 4 * steps * shape[0] * shape[1]),
            name="mix",
        )(*arrived[::-1])
        return arrived + [
            lax.ppermute(parcel, in_axis, xor_pairs(in_axis, shift))
            for shift, parcel in enumerate(mixed, 1)
        ]

    first = relay(first, "row", "col", EARLY)
    second = relay(second, "col", "row", LATE)
    return first, [*second, token(second, EXTRA)]


def after(value, *earlier):
    return lax.optimization_barrier((value, earlier))[0]


def token(values, weight):
    return pl.pallas_call(
        token_kernel,
        out_shape=jax.ShapeDtypeStruct((8, LANES), jnp.float32),
        in_specs=[any_ref()] * len(values),
        out_specs=whole_ref(),
        compiler_params=params(0),
        cost_estimate=cost(weight, 0),
        name="token",
    )(*values)


def gather_line(piece):
    count = lax.axis_size("col")
    pieces = {0: piece}
    step = count // 2
    while step:
        pieces |= {
            shift + step: lax.ppermute(held, "col", xor_pairs("col", step))
            for shift, held in pieces.items()
        }
        step //= 2
    return [pieces[shift] for shift in range(count)]


def gather_square(piece):
    if lax.axis_size("row") != 4:
        return [[held] for held in gather(piece, "row")]
    one, two = (lax.ppermute(piece, "row", xor_pairs("row", shift)) for shift in (1, 2))
    middle = piece.shape[0] // 2
    far = [
        lax.ppermute(two[:middle], "row", xor_pairs("row", 1)),
        lax.ppermute(one[middle:], "row", xor_pairs("row", 2)),
    ]
    return [[piece], [one], [two], far]


def swap(piece):
    return lax.ppermute(piece, "layer", xor_pairs("layer", 1))


def on_device(tasks, task_owner, task_slot, p_pattern, c_pattern, occupations):
    n_row, n_col, layers = (lax.axis_size(axis) for axis in ("row", "col", "layer"))
    owners = n_row * n_col
    count = tasks.shape[0]
    capacity = max(2, 2 * count // owners)
    places = owners * capacity
    block_rows, block_cols = p_pattern.shape
    part_rows = BLK // layers
    part = part_rows * BLK
    rows, cols = block_rows * part_rows, block_cols * BLK
    width = part + LANES
    layer = lax.axis_index("layer")

    paired = capacity % 16 == 0
    if paired:
        parcels = [(n_col * capacity, part // 2 + LANES)] * n_row
        parcels += [(n_row * capacity, part - part // 2)] * n_col
    else:
        parcels = [(places, width)]
    sent = pl.pallas_call(
        functools.partial(pack_kernel, owners, capacity, p_pattern.shape, paired),
        out_shape=[jax.ShapeDtypeStruct(shape, jnp.bfloat16) for shape in parcels],
        in_specs=[any_ref()] * 3,
        out_specs=[whole_ref()] * len(parcels),
        scratch_shapes=[
            pltpu.VMEM((count, part), jnp.bfloat16),
            pltpu.VMEM((1, count), jnp.int32),
            pltpu.VMEM((1, count), jnp.int32),
            pltpu.SemaphoreType.DMA((3,)),
        ],
        compiler_params=pltpu.CompilerParams(vmem_limit_bytes=PACK_VMEM),
        cost_estimate=cost(2 * places * count * width, 2 * (places + count) * width),
        name="pack",
    )(tasks, task_owner.reshape(1, count), task_slot.reshape(1, count))
    if paired:
        got = list(exchange(sent[:n_row], sent[n_row:], capacity))
    else:
        got = [
            [
                lax.all_to_all(
                    sent[0].reshape(owners, capacity, width),
                    ("row", "col"),
                    split_axis=0,
                    concat_axis=0,
                    tiled=True,
                ).reshape(places, width)
            ]
        ] * 2

    slots_here = block_rows * block_cols
    half_shape = jax.ShapeDtypeStruct((block_rows, part_rows // 2, cols), jnp.bfloat16)
    piece_shape = jax.ShapeDtypeStruct((block_rows, part_rows, cols), jnp.bfloat16)
    marks_shape = jax.ShapeDtypeStruct((slots_here, places), jnp.bfloat16)

    def build(half, marks, *blocks):
        return pl.pallas_call(
            functools.partial(build_kernel, half, paired),
            out_shape=[piece_shape] * 2 if half else [marks_shape, half_shape, half_shape],
            in_specs=[whole_ref()] * (2 + len(blocks)),
            out_specs=[whole_ref()] * (2 if half else 3),
            scratch_shapes=[
                pltpu.VMEM((cols // LANES, (rows + part_rows) // 2, LANES), jnp.float32)
            ],
            compiler_params=params(2 * places * width + 8 * rows * cols),
            cost_estimate=cost(places * slots_here * part, places * width),
            name="build",
        )(occupations.reshape(1, block_rows * BLK), marks, *blocks)

    marks, *first_half = build(0, p_pattern, *got[0][::-1])
    density, ordered = build(1, marks, *got[1][::-1], *first_half)

    lefts = gather_line(ordered)
    mate = swap(density)
    pieces = gather(after(density, mate), "row")
    pieces[0] = density
    ahead = (lefts[1], lefts[n_col // 2])
    mates = [mate] + [swap(after(piece, *ahead)) for piece in pieces[1:]]
    flops = 2 * rows * cols * n_col * cols
    half_width = block_rows * BLK // layers
    panel_bytes = 2 * n_row * layers * rows * half_width
    sum_shape = jax.ShapeDtypeStruct((rows, cols), jnp.float32)
    other_shape = jax.ShapeDtypeStruct((n_row, rows, half_width), jnp.bfloat16)
    met_shape = jax.ShapeDtypeStruct((n_row // n_col, rows, cols), jnp.bfloat16)
    here = block_rows // layers
    give_shape = jax.ShapeDtypeStruct((n_col, here, part_rows, cols), jnp.bfloat16)
    partial, other, met, give = pl.pallas_call(
        functools.partial(near_square_kernel, n_col, n_row),
        out_shape=[sum_shape, other_shape, met_shape, give_shape],
        in_specs=[any_ref()] * (n_col - 1) + [whole_ref()] * n_row,
        out_specs=[whole_ref()] * 3 + [any_ref()],
        scratch_shapes=[
            pltpu.VMEM((n_row, layers, block_rows, part_rows, half_width), jnp.bfloat16),
            pltpu.SemaphoreType.DMA((n_row * layers + n_col,)),
        ],
        compiler_params=params(2 * panel_bytes + 16 * rows * cols),
        cost_estimate=cost(0, 0),
        name="near_square",
    )(*lefts[:-1], *pieces)
    square, give = pl.pallas_call(
        functools.partial(far_square_kernel, n_col, n_row),
        out_shape=[piece_shape, give_shape],
        in_specs=[whole_ref()] * (4 + n_row) + [any_ref()],
        out_specs=[whole_ref(), any_ref()],
        scratch_shapes=[pltpu.SemaphoreType.DMA],
        input_output_aliases={4 + n_row: 1},
        compiler_params=params(panel_bytes + 16 * rows * cols),
        cost_estimate=cost(0, 0),
        name="far_square",
    )(partial, other, met, *mates, lefts[-1], give)

    pieces = gather_square(square)
    mates = [[swap(part) for part in parts] for parts in pieces]
    if len(pieces[-1]) > 1:
        mates[1:3] = [[swap(after(pieces[shift][0], pieces[3 - shift][0]))] for shift in (1, 2)]
    received = swap(after(give, pieces[1][0], pieces[2][0]))
    sizes = [len(parts) for parts in pieces]
    pieces, mates = ([part for parts in held for part in parts] for held in (pieces, mates))
    partial, mask, other = pl.pallas_call(
        functools.partial(near_cube_kernel, n_col, sizes),
        out_shape=[
            sum_shape,
            jax.ShapeDtypeStruct((rows, cols), jnp.bfloat16),
            jax.ShapeDtypeStruct((rows, half_width), jnp.bfloat16),
        ],
        in_specs=[any_ref()] * (n_col + 1) + [whole_ref()] * (n_row + len(pieces)),
        out_specs=[whole_ref()] * 3,
        scratch_shapes=[
            pltpu.VMEM((n_row, layers, here, layers, part_rows, half_width), jnp.bfloat16),
            pltpu.VMEM((here, layers, part_rows, cols), jnp.bfloat16),
            pltpu.SemaphoreType.DMA((2 * n_row * layers,)),
        ],
        compiler_params=params(2 * panel_bytes + 16 * rows * cols),
        cost_estimate=cost(0, 0),
        name="near_cube",
    )(*lefts, received, c_pattern, *pieces, *mates[: n_row - 1])
    return pl.pallas_call(
        far_cube_kernel,
        out_shape=sum_shape,
        in_specs=[whole_ref()] * (3 + sizes[-1]) + [any_ref()],
        out_specs=whole_ref(),
        compiler_params=params(16 * rows * cols),
        cost_estimate=cost(flops // 2, 4 * 1024 * 1024),
        name="far_cube",
    )(partial, mask, other, *mates[n_row - 1 :], token(pieces[n_row - 1 :], HEAVY))


def solution(mesh):
    return jax.shard_map(
        on_device,
        mesh=mesh,
        in_specs=(
            P(("row", "col"), None),
            P(("row", "col"), None),
            P(("row", "col")),
            P("row", "col"),
            P("row", "col"),
            P("row"),
        ),
        out_specs=P(("row", "layer"), "col"),
        check_vma=False,
    )
```

```python
import functools

import jax
import jax.numpy as jnp
from jax import lax
from jax.experimental import pallas as pl
from jax.experimental.pallas import tpu as pltpu
from jax.sharding import PartitionSpec as P

BLK = 64
LANES = 128
PACK_VMEM = 52 * 1024 * 1024
HEAVY = 10**10
EARLY = 0
EXTRA = 0
LATE = 0


def params(held):
    return pltpu.CompilerParams(vmem_limit_bytes=held + 6 * 1024 * 1024)


def whole_ref():
    return pl.BlockSpec(memory_space=pltpu.VMEM)


def any_ref():
    return pl.BlockSpec(memory_space=pl.ANY)


def cost(flops, bytes_accessed):
    return pl.CostEstimate(flops=flops, bytes_accessed=bytes_accessed, transcendentals=0)


def pack_kernel(owners, capacity, block_shape, paired, tasks_ref, owner_hbm, slot_hbm, *refs):
    out_refs, (held, owner_ref, slot_ref, sems) = refs[:-4], refs[-4:]
    count, part = held.shape
    layer = lax.axis_index("layer")
    start = pl.multiple_of(layer * part, part)
    *small, copy = start_copies(
        [
            (owner_hbm, owner_ref),
            (slot_hbm, slot_ref),
            (tasks_ref.at[:, pl.ds(start, part)], held),
        ],
        sems,
    )
    for each in small:
        each.wait()
    block_rows, block_cols = block_shape
    slot_row = slot_ref[...]
    slot_row = lax.rem(slot_row, block_cols) * block_rows + lax.div(slot_row, block_cols)
    across = lax.broadcasted_iota(jnp.int32, (count, count), 1)
    down = lax.broadcasted_iota(jnp.int32, (count, count), 0)
    slot_col = jnp.sum(
        jnp.where(across == down, slot_row.astype(jnp.float32), 0.0), axis=1, keepdims=True
    )
    owner_row = owner_ref[...]
    if paired:
        owner_row = owner_row ^ (
            lax.axis_index("row") * lax.axis_size("col") + lax.axis_index("col")
        )
    same = (lax.broadcasted_iota(jnp.int32, (owners, count), 0) == owner_row).astype(jnp.float32)
    before = (down < across).astype(jnp.float32).astype(jnp.bfloat16)
    ahead = jnp.dot(same.astype(jnp.bfloat16), before, preferred_element_type=jnp.float32)
    placed = jnp.sum(ahead * same, axis=0, keepdims=True).astype(jnp.int32)
    target = owner_row * capacity + placed
    places = owners * capacity
    move = (
        (lax.broadcasted_iota(jnp.int32, (places, count), 0) == target)
        .astype(jnp.float32)
        .astype(jnp.bfloat16)
    )

    def put(at, end, blocks):
        moved = jnp.dot(move, blocks, preferred_element_type=jnp.float32).astype(jnp.bfloat16)
        if not paired:
            out_refs[0][:, at:end] = moved
            return
        n_row, n_col = lax.axis_size("row"), lax.axis_size("col")
        if at < part // 2 + LANES:
            each = n_col * capacity
            for down, out_ref in enumerate(out_refs[:n_row]):
                out_ref[:, at:end] = moved[down * each : (down + 1) * each]
            return
        at, end = at - (part // 2 + LANES), end - (part // 2 + LANES)
        for over, out_ref in enumerate(out_refs[n_row:]):
            for down in range(n_row):
                place = (down * n_col + over) * capacity
                out_ref[down * capacity : (down + 1) * capacity, at:end] = moved[
                    place : place + capacity
                ]

    slots = jnp.broadcast_to(slot_col, (count, LANES)).astype(jnp.bfloat16)
    put(0, LANES, slots)
    copy.wait()
    step = 512
    for at in range(0, part, step):
        put(LANES + at, LANES + at + step, held[:, at : at + step])


def mix_kernel(arrivals, capacity, *refs):
    for shift, out_ref in enumerate(refs[arrivals:], 1):
        for index, ref in enumerate(refs[:arrivals][::-1]):
            out_ref[index * capacity : (index + 1) * capacity, :] = ref[
                shift * capacity : (shift + 1) * capacity, :
            ]


def token_kernel(*refs):
    refs[-1][...] = jnp.zeros_like(refs[-1])


def build_kernel(half, paired, occ_ref, marks_ref, *refs):
    out_ref, sorted_ref, tall = refs[-3:]
    layers = lax.axis_size("layer")
    block_rows, cols = out_ref.shape[0], out_ref.shape[2]
    part_rows = BLK // layers // 2
    block_cols = cols // BLK
    rows = block_rows * part_rows
    part = part_rows * BLK
    front = 0
    if half:
        got_refs, before = refs[1 if paired else 0 : -5][::-1], refs[-5:-3]
        for ref, old_ref in zip((out_ref, sorted_ref), before):
            ref[:, :part_rows] = old_ref[...]
    else:
        got_refs, held_ref = refs[:-4][::-1], refs[-4]
        front = LANES

    def got(at, end):
        if not paired:
            skip = half * (LANES + part)
            return got_refs[0][:, skip + at : skip + end]
        n_row, n_col = lax.axis_size("row"), lax.axis_size("col")
        if half:
            capacity = got_refs[0].shape[0] // n_row
            parts = [ref[:capacity, at:end] for ref in got_refs[:n_col]]
            parts += [ref[:, at:end] for ref in got_refs[n_col:]]
        else:
            capacity = got_refs[0].shape[0] // n_col
            parts = []
            for down in range(n_row):
                place = slice(down * capacity, (down + 1) * capacity)
                parts.append(got_refs[down][:capacity, at:end])
                parts += [ref[place, at:end] for ref in got_refs[n_row:]]
        return jnp.concatenate(parts, axis=0)

    if half:
        marks = marks_ref[...]
    else:
        slots = got(0, LANES).astype(jnp.float32)
        lane = lax.broadcasted_iota(jnp.int32, slots.shape, 1).astype(jnp.float32)
        which = lax.broadcasted_iota(jnp.int32, (block_cols, LANES), 1)
        spread = lax.div(which, block_rows) == lax.broadcasted_iota(jnp.int32, which.shape, 0)
        which = lax.broadcasted_iota(jnp.int32, (block_rows, LANES), 1)
        here = lax.rem(which, block_rows) == lax.broadcasted_iota(jnp.int32, which.shape, 0)
        pattern = jnp.dot(
            marks_ref[...].astype(jnp.float32),
            spread.astype(jnp.float32),
            preferred_element_type=jnp.float32,
        )
        pattern = jnp.sum(jnp.where(here, pattern, 0.0), axis=0, keepdims=True)
        marks = jnp.where(slots == lane, pattern, 0.0)
        marks = marks.T[: block_rows * block_cols].astype(jnp.bfloat16)
        held_ref[...] = marks
    low = lax.broadcasted_iota(jnp.int32, (block_rows, LANES), 1) < BLK
    step = 256
    for at in range(0, part, step):
        summed = jnp.dot(
            marks, got(front + at, front + at + step), preferred_element_type=jnp.float32
        )
        for pair in range(step // LANES):
            lanes = slice(pair * LANES, (pair + 1) * LANES)
            row = (at // LANES + pair) * 2
            for twin in range(block_cols // 2):
                left = summed[twin * 2 * block_rows : (twin * 2 + 1) * block_rows, lanes]
                right = summed[(twin * 2 + 1) * block_rows : (twin * 2 + 2) * block_rows, lanes]
                tall[twin, pl.ds(row, block_rows, stride=part_rows), :] = jnp.where(
                    low, left, pltpu.roll(right, BLK, 1)
                )
                tall[twin, pl.ds(row + 1, block_rows, stride=part_rows), :] = jnp.where(
                    low, pltpu.roll(left, BLK, 1), right
                )
    tile_rows = block_rows * BLK
    row_here = (lax.axis_index("layer") * 2 + half) * part_rows
    row_start = lax.axis_index("row") * tile_rows + row_here
    col_start = lax.axis_index("col") * cols
    index = lax.broadcasted_iota(jnp.int32, (rows, LANES), 0)
    inside = lax.div(index, part_rows) * BLK + lax.rem(index, part_rows)
    row_id = row_start + inside
    lane = lax.broadcasted_iota(jnp.int32, (rows, LANES), 1)
    occ = jnp.zeros((rows, 1), jnp.float32)
    for at in range(0, tile_rows, LANES):
        mine = jnp.where(row_here + inside == at + lane, occ_ref[:, at : at + LANES], 0.0)
        occ = occ + jnp.sum(mine, axis=1, keepdims=True)
    values = []
    for twin in range(block_cols // 2):
        diagonal = jnp.where(row_id == col_start + twin * LANES + lane, occ, 0.0)
        values.append(tall[twin, :rows] + diagonal)
    here = slice(half * part_rows, (half + 1) * part_rows)

    def put(ref, at, value):
        ref[:, here, at : at + LANES] = value.astype(jnp.bfloat16).reshape(
            block_rows, part_rows, LANES
        )

    for twin, value in enumerate(values):
        put(out_ref, twin * LANES, value)
    quarter = LANES // 4
    spot = lax.div(lane, quarter)
    for twin in range(0, block_cols // 2, 2):
        first, second = values[twin], values[twin + 1]
        at = twin // (block_rows // 2) * tile_rows + twin % (block_rows // 2) // 2 * LANES
        back, ahead = pltpu.roll(first, 3 * quarter, 1), pltpu.roll(second, quarter, 1)
        far_back, far_ahead = pltpu.roll(first, 2 * quarter, 1), pltpu.roll(second, 2 * quarter, 1)
        put(
            sorted_ref,
            at,
            jnp.where(
                spot == 0, first, jnp.where(spot == 1, back, jnp.where(spot == 2, far_ahead, ahead))
            ),
        )
        put(
            sorted_ref,
            at + tile_rows // 2,
            jnp.where(
                spot == 0, back, jnp.where(spot == 1, far_back, jnp.where(spot == 2, ahead, second))
            ),
        )


def start_copies(pairs, sems):
    copies = [
        pltpu.make_async_copy(source, target, sems.at[index])
        for index, (source, target) in enumerate(pairs)
    ]
    for copy in copies:
        copy.start()
    return copies


def split(values, sizes):
    ends = [sum(sizes[: index + 1]) for index in range(len(sizes))]
    return [values[end - size : end] for end, size in zip(ends, sizes)]


def joined(parts):
    return flat(jnp.concatenate([part[...] for part in parts], axis=0))


def left_blocks(tile_rows, cols):
    width = tile_rows // 2
    return [
        (at // tile_rows, at % tile_rows // width, slice(at, at + width))
        for at in range(0, cols, width)
    ]


def flat(value):
    return value.reshape(-1, value.shape[-1])


def near_square_kernel(n_col, n_row, *refs):
    lefts, pieces = refs[: n_col - 1], refs[n_col - 1 : n_col - 1 + n_row]
    sum_ref, other_ref, met_ref, give_ref, left, sems = refs[n_col - 1 + n_row :]
    row, col, layer = (lax.axis_index(axis) for axis in ("row", "col", "layer"))
    cols = sum_ref.shape[1]
    per_col = n_row // n_col
    pairs = [
        (piece.at[:, :, lanes], left.at[(col ^ shift) * per_col + block, which])
        for shift, piece in enumerate(lefts)
        for block, which, lanes in left_blocks(cols // per_col, cols)
    ]
    inner = len(pairs)
    here = give_ref.shape[1]
    pairs += [
        (piece.at[pl.ds((1 - layer) * here, here)], give_ref.at[shift])
        for shift, piece in enumerate(lefts)
    ]
    copies = start_copies(pairs, sems)
    last = col ^ (n_col - 1)
    for block in range(per_col):
        left[last * per_col + block] = jnp.zeros(left.shape[1:], left.dtype)
    for shift in range(n_row):

        @pl.when(lax.div(row ^ shift, per_col) == last)
        def _(shift=shift):
            met_ref[lax.rem(row ^ shift, per_col)] = flat(pieces[shift][...])

    for copy in copies[:inner]:
        copy.wait()
    total = jnp.zeros(sum_ref.shape, jnp.float32)
    for shift in range(n_row):
        total = total + jnp.dot(
            flat(left[row ^ shift, layer]),
            flat(pieces[shift][...]),
            preferred_element_type=jnp.float32,
        )
        other_ref[shift] = flat(left[row ^ shift, 1 - layer])
    sum_ref[...] = total
    for copy in copies[inner:]:
        copy.wait()


def far_square_kernel(n_col, n_row, *refs):
    sum_ref, other_ref, met_ref = refs[:3]
    mates, left_ref = refs[3 : 3 + n_row], refs[3 + n_row]
    low_ref, give_ref, sem = refs[6 + n_row :]
    row, col, layer = (lax.axis_index(axis) for axis in ("row", "col", "layer"))
    here = give_ref.shape[0]
    copy = pltpu.make_async_copy(
        left_ref.at[pl.ds((1 - layer) * here, here)], give_ref, sem
    )
    copy.start()
    per_col = met_ref.shape[0]
    width = other_ref.shape[2]

    def columns(block, which):
        start = pl.multiple_of((block * 2 + which) * width, width)
        return flat(left_ref[:, :, pl.ds(start, width)])

    total = sum_ref[...]
    for block in range(per_col):
        total = total + jnp.dot(
            columns(block, layer), met_ref[block], preferred_element_type=jnp.float32
        )
    for shift, mate in enumerate(mates):
        met = row ^ shift
        left = jnp.where(
            lax.div(met, per_col) == col ^ (n_col - 1),
            columns(lax.rem(met, per_col), 1 - layer),
            other_ref[shift],
        )
        total = total + jnp.dot(left, flat(mate[...]), preferred_element_type=jnp.float32)
    low_ref[...] = total.astype(jnp.bfloat16).reshape(low_ref.shape)
    copy.wait()


def near_cube_kernel(n_col, sizes, *refs):
    lefts, given, pattern_ref = refs[:n_col], refs[n_col : n_col + 2], refs[n_col + 2]
    n_row, count = len(sizes), n_col + 3 + sum(sizes)
    pieces, mates = split(refs[n_col + 3 : count], sizes), refs[count : count + n_row - 1]
    sum_ref, mask_ref, other_ref, left, own, sems = refs[count + n_row - 1 :]
    row, col, layer = (lax.axis_index(axis) for axis in ("row", "col", "layer"))
    rows, cols = sum_ref.shape
    per_col = n_row // n_col
    here = given[1].shape[0]
    given = [given[0].at[shift] for shift in range(n_col - 1)] + [given[1]]
    mine = pl.ds(layer * here, here)
    pairs = []
    for block, which, lanes in left_blocks(cols // per_col, cols):
        for shift, piece in enumerate(lefts):
            at = (col ^ shift) * per_col + block
            pairs.append((piece.at[mine, :, lanes], left.at[at, which, :, layer]))
            pairs.append(
                (given[shift].at[:, :, lanes], left.at[at, which, :, 1 - layer])
            )
    copies = start_copies(pairs, sems)
    own[:, layer] = pieces[0][0][mine]
    own[:, 1 - layer] = mates[0][mine]
    pattern = pattern_ref[...].astype(jnp.float32).astype(jnp.bfloat16)
    block_rows, block_cols = pattern.shape
    across = lax.broadcasted_iota(jnp.int32, (block_cols, cols), 1)
    which = lax.broadcasted_iota(jnp.int32, (block_cols, cols), 0)
    wide = (lax.div(across, BLK) == which).astype(jnp.float32).astype(jnp.bfloat16)
    down = lax.broadcasted_iota(jnp.int32, (rows, block_rows), 0) + layer * rows
    which = lax.broadcasted_iota(jnp.int32, (rows, block_rows), 1)
    tall = (lax.div(down, BLK) == which).astype(jnp.float32).astype(jnp.bfloat16)
    tall = jnp.dot(tall, pattern, preferred_element_type=jnp.float32).astype(jnp.bfloat16)
    mask = jnp.dot(tall, wide, preferred_element_type=jnp.float32)
    mask_ref[...] = mask.astype(jnp.bfloat16)
    total = 1.5 * flat(own[...]).astype(jnp.float32)
    for copy in copies:
        copy.wait()
    for shift in range(n_row):
        total = total - jnp.dot(
            flat(left[row ^ shift, layer]),
            joined(pieces[shift]),
            preferred_element_type=jnp.float32,
        )
    for shift, mate in enumerate(mates):
        total = total - jnp.dot(
            flat(left[row ^ shift, 1 - layer]),
            flat(mate[...]),
            preferred_element_type=jnp.float32,
        )
    other_ref[...] = flat(left[row ^ (n_row - 1), 1 - layer])
    sum_ref[...] = total


def far_cube_kernel(sum_ref, mask_ref, left_ref, *refs):
    mates, out_ref = refs[:-2], refs[-1]
    total = sum_ref[...] - jnp.dot(
        left_ref[...], joined(mates), preferred_element_type=jnp.float32
    )
    out_ref[...] = mask_ref[...].astype(jnp.float32) * (2.0 * total)


def xor_pairs(axis, shift):
    return [(i, i ^ shift) for i in range(lax.axis_size(axis))]


def gather(piece, axis):
    return [piece] + [
        lax.ppermute(piece, axis, xor_pairs(axis, shift))
        for shift in range(1, lax.axis_size(axis))
    ]


def exchange(first, second, capacity):
    def relay(parcels, out_axis, in_axis, weight):
        arrived = [parcels[0]] + [
            lax.ppermute(parcel, out_axis, xor_pairs(out_axis, shift))
            for shift, parcel in enumerate(parcels)
            if shift
        ]
        steps = lax.axis_size(in_axis)
        shape = (len(arrived) * capacity, parcels[0].shape[1])
        mixed = pl.pallas_call(
            functools.partial(mix_kernel, len(arrived), capacity),
            out_shape=[jax.ShapeDtypeStruct(shape, jnp.bfloat16)] * (steps - 1),
            in_specs=[whole_ref()] * len(arrived),
            out_specs=[whole_ref()] * (steps - 1),
            compiler_params=params(4 * steps * shape[0] * shape[1]),
            cost_estimate=cost(weight, 4 * steps * shape[0] * shape[1]),
            name="mix",
        )(*arrived[::-1])
        return arrived + [
            lax.ppermute(parcel, in_axis, xor_pairs(in_axis, shift))
            for shift, parcel in enumerate(mixed, 1)
        ]

    first = relay(first, "row", "col", EARLY)
    second = relay(second, "col", "row", LATE)
    return first, [*second, token(second, EXTRA)]


def after(value, *earlier):
    return lax.optimization_barrier((value, earlier))[0]


def token(values, weight):
    return pl.pallas_call(
        token_kernel,
        out_shape=jax.ShapeDtypeStruct((8, LANES), jnp.float32),
        in_specs=[any_ref()] * len(values),
        out_specs=whole_ref(),
        compiler_params=params(0),
        cost_estimate=cost(weight, 0),
        name="token",
    )(*values)


def gather_line(piece):
    count = lax.axis_size("col")
    pieces = {0: piece}
    step = count // 2
    while step:
        pieces |= {
            shift + step: lax.ppermute(held, "col", xor_pairs("col", step))
            for shift, held in pieces.items()
        }
        step //= 2
    return [pieces[shift] for shift in range(count)]


def gather_square(piece):
    if lax.axis_size("row") != 4:
        return [[held] for held in gather(piece, "row")]
    one, two = (lax.ppermute(piece, "row", xor_pairs("row", shift)) for shift in (1, 2))
    middle = piece.shape[0] // 2
    far = [
        lax.ppermute(two[:middle], "row", xor_pairs("row", 1)),
        lax.ppermute(one[middle:], "row", xor_pairs("row", 2)),
    ]
    return [[piece], [one], [two], far]


def swap(piece):
    return lax.ppermute(piece, "layer", xor_pairs("layer", 1))


def on_device(tasks, task_owner, task_slot, p_pattern, c_pattern, occupations):
    n_row, n_col, layers = (lax.axis_size(axis) for axis in ("row", "col", "layer"))
    owners = n_row * n_col
    count = tasks.shape[0]
    capacity = max(2, 2 * count // owners)
    places = owners * capacity
    block_rows, block_cols = p_pattern.shape
    part_rows = BLK // layers
    part = part_rows * BLK
    rows, cols = block_rows * part_rows, block_cols * BLK
    width = part + LANES
    layer = lax.axis_index("layer")

    paired = capacity % 16 == 0
    if paired:
        parcels = [(n_col * capacity, part // 2 + LANES)] * n_row
        parcels += [(n_row * capacity, part - part // 2)] * n_col
    else:
        parcels = [(places, width)]
    sent = pl.pallas_call(
        functools.partial(pack_kernel, owners, capacity, p_pattern.shape, paired),
        out_shape=[jax.ShapeDtypeStruct(shape, jnp.bfloat16) for shape in parcels],
        in_specs=[any_ref()] * 3,
        out_specs=[whole_ref()] * len(parcels),
        scratch_shapes=[
            pltpu.VMEM((count, part), jnp.bfloat16),
            pltpu.VMEM((1, count), jnp.int32),
            pltpu.VMEM((1, count), jnp.int32),
            pltpu.SemaphoreType.DMA((3,)),
        ],
        compiler_params=pltpu.CompilerParams(vmem_limit_bytes=PACK_VMEM),
        cost_estimate=cost(2 * places * count * width, 2 * (places + count) * width),
        name="pack",
    )(tasks, task_owner.reshape(1, count), task_slot.reshape(1, count))
    if paired:
        got = list(exchange(sent[:n_row], sent[n_row:], capacity))
    else:
        got = [
            [
                lax.all_to_all(
                    sent[0].reshape(owners, capacity, width),
                    ("row", "col"),
                    split_axis=0,
                    concat_axis=0,
                    tiled=True,
                ).reshape(places, width)
            ]
        ] * 2

    slots_here = block_rows * block_cols
    half_shape = jax.ShapeDtypeStruct((block_rows, part_rows // 2, cols), jnp.bfloat16)
    piece_shape = jax.ShapeDtypeStruct((block_rows, part_rows, cols), jnp.bfloat16)
    marks_shape = jax.ShapeDtypeStruct((slots_here, places), jnp.bfloat16)

    def build(half, marks, *blocks):
        return pl.pallas_call(
            functools.partial(build_kernel, half, paired),
            out_shape=[piece_shape] * 2 if half else [marks_shape, half_shape, half_shape],
            in_specs=[whole_ref()] * (2 + len(blocks)),
            out_specs=[whole_ref()] * (2 if half else 3),
            scratch_shapes=[
                pltpu.VMEM((cols // LANES, (rows + part_rows) // 2, LANES), jnp.float32)
            ],
            compiler_params=params(2 * places * width + 8 * rows * cols),
            cost_estimate=cost(places * slots_here * part, places * width),
            name="build",
        )(occupations.reshape(1, block_rows * BLK), marks, *blocks)

    marks, *first_half = build(0, p_pattern, *got[0][::-1])
    density, ordered = build(1, marks, *got[1][::-1], *first_half)

    lefts = gather_line(ordered)
    mate = swap(density)
    pieces = gather(after(density, mate), "row")
    pieces[0] = density
    ahead = (lefts[1], lefts[n_col // 2])
    mates = [mate] + [swap(after(piece, *ahead)) for piece in pieces[1:]]
    flops = 2 * rows * cols * n_col * cols
    half_width = block_rows * BLK // layers
    panel_bytes = 2 * n_row * layers * rows * half_width
    sum_shape = jax.ShapeDtypeStruct((rows, cols), jnp.float32)
    other_shape = jax.ShapeDtypeStruct((n_row, rows, half_width), jnp.bfloat16)
    met_shape = jax.ShapeDtypeStruct((n_row // n_col, rows, cols), jnp.bfloat16)
    here = block_rows // layers
    give_shape = (here, part_rows, cols)
    partial, other, met, give = pl.pallas_call(
        functools.partial(near_square_kernel, n_col, n_row),
        out_shape=[
            sum_shape,
            other_shape,
            met_shape,
            jax.ShapeDtypeStruct((n_col - 1, *give_shape), jnp.bfloat16),
        ],
        in_specs=[any_ref()] * (n_col - 1) + [whole_ref()] * n_row,
        out_specs=[whole_ref()] * 3 + [any_ref()],
        scratch_shapes=[
            pltpu.VMEM((n_row, layers, block_rows, part_rows, half_width), jnp.bfloat16),
            pltpu.SemaphoreType.DMA((n_row * layers + n_col,)),
        ],
        compiler_params=params(2 * panel_bytes + 16 * rows * cols),
        cost_estimate=cost(0, 0),
        name="near_square",
    )(*lefts[:-1], *pieces)
    received = swap(give)
    square, give = pl.pallas_call(
        functools.partial(far_square_kernel, n_col, n_row),
        out_shape=[piece_shape, jax.ShapeDtypeStruct(give_shape, jnp.bfloat16)],
        in_specs=[whole_ref()] * (4 + n_row) + [any_ref()] * 2,
        out_specs=[whole_ref(), any_ref()],
        scratch_shapes=[pltpu.SemaphoreType.DMA],
        compiler_params=params(panel_bytes + 16 * rows * cols),
        cost_estimate=cost(0, 0),
        name="far_square",
    )(partial, other, met, *mates, lefts[-1], received, token(lefts[-1:], HEAVY))

    pieces = gather_square(square)
    mates = [[swap(part) for part in parts] for parts in pieces]
    if len(pieces[-1]) > 1:
        mates[1:3] = [[swap(after(pieces[shift][0], pieces[3 - shift][0]))] for shift in (1, 2)]
    received = [received, swap(after(give, pieces[1][0], pieces[2][0]))]
    sizes = [len(parts) for parts in pieces]
    pieces, mates = ([part for parts in held for part in parts] for held in (pieces, mates))
    partial, mask, other = pl.pallas_call(
        functools.partial(near_cube_kernel, n_col, sizes),
        out_shape=[
            sum_shape,
            jax.ShapeDtypeStruct((rows, cols), jnp.bfloat16),
            jax.ShapeDtypeStruct((rows, half_width), jnp.bfloat16),
        ],
        in_specs=[any_ref()] * (n_col + 2) + [whole_ref()] * (n_row + len(pieces)),
        out_specs=[whole_ref()] * 3,
        scratch_shapes=[
            pltpu.VMEM((n_row, layers, here, layers, part_rows, half_width), jnp.bfloat16),
            pltpu.VMEM((here, layers, part_rows, cols), jnp.bfloat16),
            pltpu.SemaphoreType.DMA((2 * n_row * layers,)),
        ],
        compiler_params=params(2 * panel_bytes + 16 * rows * cols),
        cost_estimate=cost(0, 0),
        name="near_cube",
    )(*lefts, *received, c_pattern, *pieces, *mates[: n_row - 1])
    return pl.pallas_call(
        far_cube_kernel,
        out_shape=sum_shape,
        in_specs=[whole_ref()] * (3 + sizes[-1]) + [any_ref()],
        out_specs=whole_ref(),
        compiler_params=params(16 * rows * cols),
        cost_estimate=cost(flops // 2, 4 * 1024 * 1024),
        name="far_cube",
    )(partial, mask, other, *mates[n_row - 1 :], token(pieces[n_row - 1 :], HEAVY))


def solution(mesh):
    return jax.shard_map(
        on_device,
        mesh=mesh,
        in_specs=(
            P(("row", "col"), None),
            P(("row", "col"), None),
            P(("row", "col")),
            P("row", "col"),
            P("row", "col"),
            P("row"),
        ),
        out_specs=P(("row", "layer"), "col"),
        check_vma=False,
    )
```

```python
import functools

import jax
import jax.numpy as jnp
from jax import lax
from jax.experimental import pallas as pl
from jax.experimental.pallas import tpu as pltpu
from jax.sharding import PartitionSpec as P

BLK = 64
LANES = 128
PACK_VMEM = 52 * 1024 * 1024
HEAVY = 10**10
EARLY = 0
EXTRA = 0
LATE = 0


def params(held):
    return pltpu.CompilerParams(vmem_limit_bytes=held + 6 * 1024 * 1024)


def whole_ref():
    return pl.BlockSpec(memory_space=pltpu.VMEM)


def any_ref():
    return pl.BlockSpec(memory_space=pl.ANY)


def cost(flops, bytes_accessed):
    return pl.CostEstimate(flops=flops, bytes_accessed=bytes_accessed, transcendentals=0)


def pack_kernel(owners, capacity, block_shape, paired, tasks_ref, owner_hbm, slot_hbm, *refs):
    out_refs, (held, owner_ref, slot_ref, sems) = refs[:-4], refs[-4:]
    count, part = held.shape
    layer = lax.axis_index("layer")
    start = pl.multiple_of(layer * part, part)
    *small, copy = start_copies(
        [
            (owner_hbm, owner_ref),
            (slot_hbm, slot_ref),
            (tasks_ref.at[:, pl.ds(start, part)], held),
        ],
        sems,
    )
    for each in small:
        each.wait()
    block_rows, block_cols = block_shape
    slot_row = slot_ref[...]
    slot_row = lax.rem(slot_row, block_cols) * block_rows + lax.div(slot_row, block_cols)
    across = lax.broadcasted_iota(jnp.int32, (count, count), 1)
    down = lax.broadcasted_iota(jnp.int32, (count, count), 0)
    slot_col = jnp.sum(
        jnp.where(across == down, slot_row.astype(jnp.float32), 0.0), axis=1, keepdims=True
    )
    owner_row = owner_ref[...]
    if paired:
        owner_row = owner_row ^ (
            lax.axis_index("row") * lax.axis_size("col") + lax.axis_index("col")
        )
    same = (lax.broadcasted_iota(jnp.int32, (owners, count), 0) == owner_row).astype(jnp.float32)
    before = (down < across).astype(jnp.float32).astype(jnp.bfloat16)
    ahead = jnp.dot(same.astype(jnp.bfloat16), before, preferred_element_type=jnp.float32)
    placed = jnp.sum(ahead * same, axis=0, keepdims=True).astype(jnp.int32)
    target = owner_row * capacity + placed
    places = owners * capacity
    move = (
        (lax.broadcasted_iota(jnp.int32, (places, count), 0) == target)
        .astype(jnp.float32)
        .astype(jnp.bfloat16)
    )

    def put(at, end, blocks):
        moved = jnp.dot(move, blocks, preferred_element_type=jnp.float32).astype(jnp.bfloat16)
        if not paired:
            out_refs[0][:, at:end] = moved
            return
        n_row, n_col = lax.axis_size("row"), lax.axis_size("col")
        if at < part // 2 + LANES:
            each = n_col * capacity
            for down, out_ref in enumerate(out_refs[:n_row]):
                out_ref[:, at:end] = moved[down * each : (down + 1) * each]
            return
        at, end = at - (part // 2 + LANES), end - (part // 2 + LANES)
        for over, out_ref in enumerate(out_refs[n_row:]):
            for down in range(n_row):
                place = (down * n_col + over) * capacity
                out_ref[down * capacity : (down + 1) * capacity, at:end] = moved[
                    place : place + capacity
                ]

    slots = jnp.broadcast_to(slot_col, (count, LANES)).astype(jnp.bfloat16)
    put(0, LANES, slots)
    copy.wait()
    step = 512
    for at in range(0, part, step):
        put(LANES + at, LANES + at + step, held[:, at : at + step])


def mix_kernel(arrivals, capacity, *refs):
    for shift, out_ref in enumerate(refs[arrivals:], 1):
        for index, ref in enumerate(refs[:arrivals][::-1]):
            out_ref[index * capacity : (index + 1) * capacity, :] = ref[
                shift * capacity : (shift + 1) * capacity, :
            ]


def token_kernel(*refs):
    refs[-1][...] = jnp.zeros_like(refs[-1])


def build_kernel(half, paired, occ_ref, marks_ref, *refs):
    out_ref, sorted_ref, tall = refs[-3:]
    layers = lax.axis_size("layer")
    block_rows, cols = out_ref.shape[0], out_ref.shape[2]
    part_rows = BLK // layers // 2
    block_cols = cols // BLK
    rows = block_rows * part_rows
    part = part_rows * BLK
    front = 0
    if half:
        got_refs, before = refs[1 if paired else 0 : -5][::-1], refs[-5:-3]
        for ref, old_ref in zip((out_ref, sorted_ref), before):
            ref[:, :part_rows] = old_ref[...]
    else:
        got_refs, held_ref = refs[:-4][::-1], refs[-4]
        front = LANES

    def got(at, end):
        if not paired:
            skip = half * (LANES + part)
            return got_refs[0][:, skip + at : skip + end]
        n_row, n_col = lax.axis_size("row"), lax.axis_size("col")
        if half:
            capacity = got_refs[0].shape[0] // n_row
            parts = [ref[:capacity, at:end] for ref in got_refs[:n_col]]
            parts += [ref[:, at:end] for ref in got_refs[n_col:]]
        else:
            capacity = got_refs[0].shape[0] // n_col
            parts = []
            for down in range(n_row):
                place = slice(down * capacity, (down + 1) * capacity)
                parts.append(got_refs[down][:capacity, at:end])
                parts += [ref[place, at:end] for ref in got_refs[n_row:]]
        return jnp.concatenate(parts, axis=0)

    if half:
        marks = marks_ref[...]
    else:
        slots = got(0, LANES).astype(jnp.float32)
        lane = lax.broadcasted_iota(jnp.int32, slots.shape, 1).astype(jnp.float32)
        which = lax.broadcasted_iota(jnp.int32, (block_cols, LANES), 1)
        spread = lax.div(which, block_rows) == lax.broadcasted_iota(jnp.int32, which.shape, 0)
        which = lax.broadcasted_iota(jnp.int32, (block_rows, LANES), 1)
        here = lax.rem(which, block_rows) == lax.broadcasted_iota(jnp.int32, which.shape, 0)
        pattern = jnp.dot(
            marks_ref[...].astype(jnp.float32),
            spread.astype(jnp.float32),
            preferred_element_type=jnp.float32,
        )
        pattern = jnp.sum(jnp.where(here, pattern, 0.0), axis=0, keepdims=True)
        marks = jnp.where(slots == lane, pattern, 0.0)
        marks = marks.T[: block_rows * block_cols].astype(jnp.bfloat16)
        held_ref[...] = marks
    low = lax.broadcasted_iota(jnp.int32, (block_rows, LANES), 1) < BLK
    step = 256
    for at in range(0, part, step):
        summed = jnp.dot(
            marks, got(front + at, front + at + step), preferred_element_type=jnp.float32
        )
        for pair in range(step // LANES):
            lanes = slice(pair * LANES, (pair + 1) * LANES)
            row = (at // LANES + pair) * 2
            for twin in range(block_cols // 2):
                left = summed[twin * 2 * block_rows : (twin * 2 + 1) * block_rows, lanes]
                right = summed[(twin * 2 + 1) * block_rows : (twin * 2 + 2) * block_rows, lanes]
                tall[twin, pl.ds(row, block_rows, stride=part_rows), :] = jnp.where(
                    low, left, pltpu.roll(right, BLK, 1)
                )
                tall[twin, pl.ds(row + 1, block_rows, stride=part_rows), :] = jnp.where(
                    low, pltpu.roll(left, BLK, 1), right
                )
    tile_rows = block_rows * BLK
    row_here = (lax.axis_index("layer") * 2 + half) * part_rows
    row_start = lax.axis_index("row") * tile_rows + row_here
    col_start = lax.axis_index("col") * cols
    index = lax.broadcasted_iota(jnp.int32, (rows, LANES), 0)
    inside = lax.div(index, part_rows) * BLK + lax.rem(index, part_rows)
    row_id = row_start + inside
    lane = lax.broadcasted_iota(jnp.int32, (rows, LANES), 1)
    occ = jnp.zeros((rows, 1), jnp.float32)
    for at in range(0, tile_rows, LANES):
        mine = jnp.where(row_here + inside == at + lane, occ_ref[:, at : at + LANES], 0.0)
        occ = occ + jnp.sum(mine, axis=1, keepdims=True)
    values = []
    for twin in range(block_cols // 2):
        diagonal = jnp.where(row_id == col_start + twin * LANES + lane, occ, 0.0)
        values.append(tall[twin, :rows] + diagonal)
    here = slice(half * part_rows, (half + 1) * part_rows)

    def put(ref, at, value):
        ref[:, here, at : at + LANES] = value.astype(jnp.bfloat16).reshape(
            block_rows, part_rows, LANES
        )

    for twin, value in enumerate(values):
        put(out_ref, twin * LANES, value)
    quarter = LANES // 4
    spot = lax.div(lane, quarter)
    for twin in range(0, block_cols // 2, 2):
        first, second = values[twin], values[twin + 1]
        at = twin // (block_rows // 2) * tile_rows + twin % (block_rows // 2) // 2 * LANES
        back, ahead = pltpu.roll(first, 3 * quarter, 1), pltpu.roll(second, quarter, 1)
        far_back, far_ahead = pltpu.roll(first, 2 * quarter, 1), pltpu.roll(second, 2 * quarter, 1)
        put(
            sorted_ref,
            at,
            jnp.where(
                spot == 0, first, jnp.where(spot == 1, back, jnp.where(spot == 2, far_ahead, ahead))
            ),
        )
        put(
            sorted_ref,
            at + tile_rows // 2,
            jnp.where(
                spot == 0, back, jnp.where(spot == 1, far_back, jnp.where(spot == 2, ahead, second))
            ),
        )


def start_copies(pairs, sems):
    copies = [
        pltpu.make_async_copy(source, target, sems.at[index])
        for index, (source, target) in enumerate(pairs)
    ]
    for copy in copies:
        copy.start()
    return copies


def split(values, sizes):
    ends = [sum(sizes[: index + 1]) for index in range(len(sizes))]
    return [values[end - size : end] for end, size in zip(ends, sizes)]


def joined(parts):
    return flat(jnp.concatenate([part[...] for part in parts], axis=0))


def left_blocks(tile_rows, cols):
    width = tile_rows // 2
    return [
        (at // tile_rows, at % tile_rows // width, slice(at, at + width))
        for at in range(0, cols, width)
    ]


def flat(value):
    return value.reshape(-1, value.shape[-1])


def near_square_kernel(n_col, n_row, *refs):
    lefts, pieces = refs[: n_col - 1], refs[n_col - 1 : n_col - 1 + n_row]
    sum_ref, other_ref, met_ref, give_ref, left, sems = refs[n_col - 1 + n_row :]
    row, col, layer = (lax.axis_index(axis) for axis in ("row", "col", "layer"))
    cols = sum_ref.shape[1]
    per_col = n_row // n_col
    pairs = [
        (piece.at[:, :, lanes], left.at[(col ^ shift) * per_col + block, which])
        for shift, piece in enumerate(lefts)
        for block, which, lanes in left_blocks(cols // per_col, cols)
    ]
    inner = len(pairs)
    here = give_ref.shape[1]
    pairs += [
        (piece.at[pl.ds((1 - layer) * here, here)], give_ref.at[shift])
        for shift, piece in enumerate(lefts)
    ]
    copies = start_copies(pairs, sems)
    last = col ^ (n_col - 1)
    for block in range(per_col):
        left[last * per_col + block] = jnp.zeros(left.shape[1:], left.dtype)
    for shift in range(n_row):

        @pl.when(lax.div(row ^ shift, per_col) == last)
        def _(shift=shift):
            met_ref[lax.rem(row ^ shift, per_col)] = flat(pieces[shift][...])

    for copy in copies[:inner]:
        copy.wait()
    total = jnp.zeros(sum_ref.shape, jnp.float32)
    for shift in range(n_row):
        total = total + jnp.dot(
            flat(left[row ^ shift, layer]),
            flat(pieces[shift][...]),
            preferred_element_type=jnp.float32,
        )
        other_ref[shift] = flat(left[row ^ shift, 1 - layer])
    sum_ref[...] = total
    for copy in copies[inner:]:
        copy.wait()


def far_square_kernel(n_col, n_row, *refs):
    sum_ref, other_ref, met_ref = refs[:3]
    mates, left_ref = refs[3 : 3 + n_row], refs[3 + n_row]
    low_ref, give_ref, sem = refs[6 + n_row :]
    row, col, layer = (lax.axis_index(axis) for axis in ("row", "col", "layer"))
    here = give_ref.shape[0]
    copy = pltpu.make_async_copy(
        left_ref.at[pl.ds((1 - layer) * here, here)], give_ref, sem
    )
    copy.start()
    per_col = met_ref.shape[0]
    width = other_ref.shape[2]

    def columns(block, which):
        start = pl.multiple_of((block * 2 + which) * width, width)
        return flat(left_ref[:, :, pl.ds(start, width)])

    total = sum_ref[...]
    for block in range(per_col):
        total = total + jnp.dot(
            columns(block, layer), met_ref[block], preferred_element_type=jnp.float32
        )
    for shift, mate in enumerate(mates):
        met = row ^ shift
        left = jnp.where(
            lax.div(met, per_col) == col ^ (n_col - 1),
            columns(lax.rem(met, per_col), 1 - layer),
            other_ref[shift],
        )
        total = total + jnp.dot(left, flat(mate[...]), preferred_element_type=jnp.float32)
    low_ref[...] = total.astype(jnp.bfloat16).reshape(low_ref.shape)
    copy.wait()


def near_cube_kernel(n_col, sizes, *refs):
    lefts, given, pattern_ref = refs[:n_col], refs[n_col : n_col + 2], refs[n_col + 2]
    n_row, count = len(sizes), n_col + 3 + sum(sizes)
    pieces, mates = split(refs[n_col + 3 : count], sizes), refs[count : count + n_row - 1]
    sum_ref, mask_ref, other_ref, left, own, sems = refs[count + n_row - 1 :]
    row, col, layer = (lax.axis_index(axis) for axis in ("row", "col", "layer"))
    rows, cols = sum_ref.shape
    per_col = n_row // n_col
    here = given[1].shape[0]
    given = [given[0].at[shift] for shift in range(n_col - 1)] + [given[1]]
    mine = pl.ds(layer * here, here)
    pairs = []
    for block, which, lanes in left_blocks(cols // per_col, cols):
        for shift, piece in enumerate(lefts):
            at = (col ^ shift) * per_col + block
            pairs.append((piece.at[mine, :, lanes], left.at[at, which, :, layer]))
            pairs.append(
                (given[shift].at[:, :, lanes], left.at[at, which, :, 1 - layer])
            )
    copies = start_copies(pairs, sems)
    own[:, layer] = pieces[0][0][mine]
    own[:, 1 - layer] = mates[0][mine]
    pattern = pattern_ref[...].astype(jnp.float32).astype(jnp.bfloat16)
    block_rows, block_cols = pattern.shape
    across = lax.broadcasted_iota(jnp.int32, (block_cols, cols), 1)
    which = lax.broadcasted_iota(jnp.int32, (block_cols, cols), 0)
    wide = (lax.div(across, BLK) == which).astype(jnp.float32).astype(jnp.bfloat16)
    down = lax.broadcasted_iota(jnp.int32, (rows, block_rows), 0) + layer * rows
    which = lax.broadcasted_iota(jnp.int32, (rows, block_rows), 1)
    tall = (lax.div(down, BLK) == which).astype(jnp.float32).astype(jnp.bfloat16)
    tall = jnp.dot(tall, pattern, preferred_element_type=jnp.float32).astype(jnp.bfloat16)
    mask = jnp.dot(tall, wide, preferred_element_type=jnp.float32)
    mask_ref[...] = mask.astype(jnp.bfloat16)
    total = 1.5 * flat(own[...]).astype(jnp.float32)
    for copy in copies:
        copy.wait()
    for shift in range(n_row):
        total = total - jnp.dot(
            flat(left[row ^ shift, layer]),
            joined(pieces[shift]),
            preferred_element_type=jnp.float32,
        )
    for shift, mate in enumerate(mates):
        total = total - jnp.dot(
            flat(left[row ^ shift, 1 - layer]),
            flat(mate[...]),
            preferred_element_type=jnp.float32,
        )
    other_ref[...] = flat(left[row ^ (n_row - 1), 1 - layer])
    sum_ref[...] = total


def far_cube_kernel(sum_ref, mask_ref, left_ref, *refs):
    mates, out_ref = refs[:-2], refs[-1]
    total = sum_ref[...] - jnp.dot(
        left_ref[...], joined(mates), preferred_element_type=jnp.float32
    )
    out_ref[...] = mask_ref[...].astype(jnp.float32) * (2.0 * total)


def xor_pairs(axis, shift):
    return [(i, i ^ shift) for i in range(lax.axis_size(axis))]


def gather(piece, axis):
    return [piece] + [
        lax.ppermute(piece, axis, xor_pairs(axis, shift))
        for shift in range(1, lax.axis_size(axis))
    ]


def exchange(first, second, capacity):
    def relay(parcels, out_axis, in_axis, weight):
        arrived = [parcels[0]] + [
            lax.ppermute(parcel, out_axis, xor_pairs(out_axis, shift))
            for shift, parcel in enumerate(parcels)
            if shift
        ]
        steps = lax.axis_size(in_axis)
        shape = (len(arrived) * capacity, parcels[0].shape[1])
        mixed = pl.pallas_call(
            functools.partial(mix_kernel, len(arrived), capacity),
            out_shape=[jax.ShapeDtypeStruct(shape, jnp.bfloat16)] * (steps - 1),
            in_specs=[whole_ref()] * len(arrived),
            out_specs=[whole_ref()] * (steps - 1),
            compiler_params=params(4 * steps * shape[0] * shape[1]),
            cost_estimate=cost(weight, 4 * steps * shape[0] * shape[1]),
            name="mix",
        )(*arrived[::-1])
        return arrived + [
            lax.ppermute(parcel, in_axis, xor_pairs(in_axis, shift))
            for shift, parcel in enumerate(mixed, 1)
        ]

    first = relay(first, "row", "col", EARLY)
    second = relay(second, "col", "row", LATE)
    return first, [*second, token(second, EXTRA)]


def after(value, *earlier):
    return lax.optimization_barrier((value, earlier))[0]


def token(values, weight):
    return pl.pallas_call(
        token_kernel,
        out_shape=jax.ShapeDtypeStruct((8, LANES), jnp.float32),
        in_specs=[any_ref()] * len(values),
        out_specs=whole_ref(),
        compiler_params=params(0),
        cost_estimate=cost(weight, 0),
        name="token",
    )(*values)


def gather_line(piece):
    count = lax.axis_size("col")
    pieces = {0: piece}
    step = count // 2
    while step:
        pieces |= {
            shift + step: lax.ppermute(held, "col", xor_pairs("col", step))
            for shift, held in pieces.items()
        }
        step //= 2
    return [pieces[shift] for shift in range(count)]


def gather_square(piece):
    if lax.axis_size("row") != 4:
        return [[held] for held in gather(piece, "row")]
    one, two = (lax.ppermute(piece, "row", xor_pairs("row", shift)) for shift in (1, 2))
    middle = piece.shape[0] // 2
    far = [
        lax.ppermute(two[:middle], "row", xor_pairs("row", 1)),
        lax.ppermute(one[middle:], "row", xor_pairs("row", 2)),
    ]
    return [[piece], [one], [two], far]


def swap(piece):
    return lax.ppermute(piece, "layer", xor_pairs("layer", 1))


def on_device(tasks, task_owner, task_slot, p_pattern, c_pattern, occupations):
    n_row, n_col, layers = (lax.axis_size(axis) for axis in ("row", "col", "layer"))
    owners = n_row * n_col
    count = tasks.shape[0]
    capacity = max(2, 2 * count // owners)
    places = owners * capacity
    block_rows, block_cols = p_pattern.shape
    part_rows = BLK // layers
    part = part_rows * BLK
    rows, cols = block_rows * part_rows, block_cols * BLK
    width = part + LANES
    layer = lax.axis_index("layer")

    paired = capacity % 16 == 0
    if paired:
        parcels = [(n_col * capacity, part // 2 + LANES)] * n_row
        parcels += [(n_row * capacity, part - part // 2)] * n_col
    else:
        parcels = [(places, width)]
    sent = pl.pallas_call(
        functools.partial(pack_kernel, owners, capacity, p_pattern.shape, paired),
        out_shape=[jax.ShapeDtypeStruct(shape, jnp.bfloat16) for shape in parcels],
        in_specs=[any_ref()] * 3,
        out_specs=[whole_ref()] * len(parcels),
        scratch_shapes=[
            pltpu.VMEM((count, part), jnp.bfloat16),
            pltpu.VMEM((1, count), jnp.int32),
            pltpu.VMEM((1, count), jnp.int32),
            pltpu.SemaphoreType.DMA((3,)),
        ],
        compiler_params=pltpu.CompilerParams(vmem_limit_bytes=PACK_VMEM),
        cost_estimate=cost(2 * places * count * width, 2 * (places + count) * width),
        name="pack",
    )(tasks, task_owner.reshape(1, count), task_slot.reshape(1, count))
    if paired:
        got = list(exchange(sent[:n_row], sent[n_row:], capacity))
    else:
        got = [
            [
                lax.all_to_all(
                    sent[0].reshape(owners, capacity, width),
                    ("row", "col"),
                    split_axis=0,
                    concat_axis=0,
                    tiled=True,
                ).reshape(places, width)
            ]
        ] * 2

    slots_here = block_rows * block_cols
    half_shape = jax.ShapeDtypeStruct((block_rows, part_rows // 2, cols), jnp.bfloat16)
    piece_shape = jax.ShapeDtypeStruct((block_rows, part_rows, cols), jnp.bfloat16)
    marks_shape = jax.ShapeDtypeStruct((slots_here, places), jnp.bfloat16)

    def build(half, marks, *blocks):
        return pl.pallas_call(
            functools.partial(build_kernel, half, paired),
            out_shape=[piece_shape] * 2 if half else [marks_shape, half_shape, half_shape],
            in_specs=[whole_ref()] * (2 + len(blocks)),
            out_specs=[whole_ref()] * (2 if half else 3),
            scratch_shapes=[
                pltpu.VMEM((cols // LANES, (rows + part_rows) // 2, LANES), jnp.float32)
            ],
            compiler_params=params(2 * places * width + 8 * rows * cols),
            cost_estimate=cost(places * slots_here * part, places * width),
            name="build",
        )(occupations.reshape(1, block_rows * BLK), marks, *blocks)

    marks, *first_half = build(0, p_pattern, *got[0][::-1])
    density, ordered = build(1, marks, *got[1][::-1], *first_half)

    lefts = gather_line(ordered)
    mate = swap(density)
    pieces = gather(after(density, mate), "row")
    pieces[0] = density
    ahead = (lefts[1], lefts[n_col // 2])
    mates = [mate] + [swap(after(piece, *ahead)) for piece in pieces[1:]]
    flops = 2 * rows * cols * n_col * cols
    half_width = block_rows * BLK // layers
    panel_bytes = 2 * n_row * layers * rows * half_width
    sum_shape = jax.ShapeDtypeStruct((rows, cols), jnp.float32)
    other_shape = jax.ShapeDtypeStruct((n_row, rows, half_width), jnp.bfloat16)
    met_shape = jax.ShapeDtypeStruct((n_row // n_col, rows, cols), jnp.bfloat16)
    here = block_rows // layers
    give_shape = (here, part_rows, cols)
    partial, other, met, give = pl.pallas_call(
        functools.partial(near_square_kernel, n_col, n_row),
        out_shape=[
            sum_shape,
            other_shape,
            met_shape,
            jax.ShapeDtypeStruct((n_col - 1, *give_shape), jnp.bfloat16),
        ],
        in_specs=[any_ref()] * (n_col - 1) + [whole_ref()] * n_row,
        out_specs=[whole_ref()] * 3 + [any_ref()],
        scratch_shapes=[
            pltpu.VMEM((n_row, layers, block_rows, part_rows, half_width), jnp.bfloat16),
            pltpu.SemaphoreType.DMA((n_row * layers + n_col,)),
        ],
        compiler_params=params(2 * panel_bytes + 16 * rows * cols),
        cost_estimate=cost(0, 0),
        name="near_square",
    )(*lefts[:-1], *pieces)
    received = swap(give)
    square, give = pl.pallas_call(
        functools.partial(far_square_kernel, n_col, n_row),
        out_shape=[piece_shape, jax.ShapeDtypeStruct(give_shape, jnp.bfloat16)],
        in_specs=[whole_ref()] * (4 + n_row) + [any_ref()] * 2,
        out_specs=[whole_ref(), any_ref()],
        scratch_shapes=[pltpu.SemaphoreType.DMA],
        compiler_params=params(panel_bytes + 16 * rows * cols),
        cost_estimate=cost(0, 0),
        name="far_square",
    )(partial, other, met, *mates, lefts[-1], received, token(lefts[-1:], HEAVY))

    pieces = gather_square(square)
    mates = [[swap(part) for part in parts] for parts in pieces]
    if len(pieces[-1]) > 1:
        mates[0] = [swap(after(square, pieces[1][0], pieces[2][0]))]
        mates[1:3] = [[swap(after(pieces[shift][0], pieces[3 - shift][0]))] for shift in (1, 2)]
    received = [received, swap(after(give, pieces[1][0], pieces[2][0]))]
    sizes = [len(parts) for parts in pieces]
    pieces, mates = ([part for parts in held for part in parts] for held in (pieces, mates))
    partial, mask, other = pl.pallas_call(
        functools.partial(near_cube_kernel, n_col, sizes),
        out_shape=[
            sum_shape,
            jax.ShapeDtypeStruct((rows, cols), jnp.bfloat16),
            jax.ShapeDtypeStruct((rows, half_width), jnp.bfloat16),
        ],
        in_specs=[any_ref()] * (n_col + 2) + [whole_ref()] * (n_row + len(pieces)),
        out_specs=[whole_ref()] * 3,
        scratch_shapes=[
            pltpu.VMEM((n_row, layers, here, layers, part_rows, half_width), jnp.bfloat16),
            pltpu.VMEM((here, layers, part_rows, cols), jnp.bfloat16),
            pltpu.SemaphoreType.DMA((2 * n_row * layers,)),
        ],
        compiler_params=params(2 * panel_bytes + 16 * rows * cols),
        cost_estimate=cost(0, 0),
        name="near_cube",
    )(*lefts, *received, c_pattern, *pieces, *mates[: n_row - 1])
    return pl.pallas_call(
        far_cube_kernel,
        out_shape=sum_shape,
        in_specs=[whole_ref()] * (3 + sizes[-1]) + [any_ref()],
        out_specs=whole_ref(),
        compiler_params=params(16 * rows * cols),
        cost_estimate=cost(flops // 2, 4 * 1024 * 1024),
        name="far_cube",
    )(partial, mask, other, *mates[n_row - 1 :], token(pieces[n_row - 1 :], HEAVY))


def solution(mesh):
    return jax.shard_map(
        on_device,
        mesh=mesh,
        in_specs=(
            P(("row", "col"), None),
            P(("row", "col"), None),
            P(("row", "col")),
            P("row", "col"),
            P("row", "col"),
            P("row"),
        ),
        out_specs=P(("row", "layer"), "col"),
        check_vma=False,
    )
```
